32 devices in a mesh: dp: 8 (over z, y), mp: 4 (over x, core).
Axes of the slice: x: 2, y: 2, z: 4, core: 2. Of those that a mesh axis runs over, the one named last changes fastest.
Arguments:
- residual: bfloat16 [1024, 2048], P('dp'), may hold values from -6 to 6
- lengths: int32 [8, 3], P('dp'), may hold values from 1 to 96, 128 in all within a row
- pair_order: int32 [16], replicated, may hold values from 0 to 15, each once
- token_ids: int32 [1024], P('dp'), may hold values from 0 to 25599
- desirable: int32 [24], P('dp'), may hold values 0 or 1
- ref_match: float32 [1024], P('dp'), may hold values from -14 to -10
- ref_pair: float32 [1024], P('dp'), may hold values from -14 to -10
- attn_gain: bfloat16 [2048], replicated, may hold values from 0.099609375 to 1.8984375
- attn_shift: bfloat16 [2048], replicated, may hold values from -3 to 3
- mlp_gain: bfloat16 [2048], replicated, may hold values from 0.099609375 to 1.8984375
- mlp_shift: bfloat16 [2048], replicated, may hold values from -3 to 3
- w_joined: bfloat16 [2048, 6144], P('dp', 'mp'), may hold values from -0.125 to 0.125
- b_joined: bfloat16 [6144], P('mp'), may hold values from -3 to 3
- w_dense: bfloat16 [2048, 2048], P('mp', 'dp'), may hold values from -0.5 to 0.5
- b_dense: bfloat16 [2048], replicated, may hold values from -3 to 3
- w_up: bfloat16 [2048, 8192], P('dp', 'mp'), may hold values from -0.125 to 0.125
- b_up: bfloat16 [8192], P('mp'), may hold values from -3 to 3
- w_down: bfloat16 [8192, 2048], P('mp', 'dp'), may hold values from -0.0625 to 0.0625
- b_down: bfloat16 [2048], replicated, may hold values from -3 to 3
- final_gain: bfloat16 [2048], replicated, may hold values from 0.099609375 to 1.8984375
- final_shift: bfloat16 [2048], replicated, may hold values from -3 to 3
- w_vocab: bfloat16 [2048, 25600], P('dp', 'mp'), may hold values from -0.25 to 0.25
Outputs:
- kto_loss: float32 [], replicated
- kl_estimate: float32 [], replicated
- grad_input: float32 [1024, 2048], P('dp')
- grad_attn_gain: float32 [2048], replicated
- grad_attn_shift: float32 [2048], replicated
- grad_mlp_gain: float32 [2048], replicated
- grad_mlp_shift: float32 [2048], replicated
- grad_w_joined: float32 [2048, 6144], P('dp', 'mp')
- grad_b_joined: float32 [6144], P('mp')
- grad_w_dense: float32 [2048, 2048], P('mp', 'dp')
- grad_b_dense: float32 [2048], replicated
- grad_w_up: float32 [2048, 8192], P('dp', 'mp')
- grad_b_up: float32 [8192], P('mp')
- grad_w_down: float32 [8192, 2048], P('mp', 'dp')
- grad_b_down: float32 [2048], replicated
- grad_final_gain: float32 [2048], replicated
- grad_final_shift: float32 [2048], replicated
- grad_w_vocab: float32 [2048, 25600], P('dp', 'mp')
The draws below stay inside these ranges and needn't reach their ends.
Inputs may be any that keep to these rules, and one draw needn't show every extreme that they name: `lengths`: each row sums to 128, and its largest entry is 96. `pair_order`: a permutation of the 16 blocks.
All inputs are finite; a program needn't handle non-finite values. No bound on the sum of `desirable` on one device may be relied on, other than what follows from the above.
Results may differ from the reference program's by a relative error of at most 0.014.
Values may be sent and summed in bfloat16 or wider, within the bound.
A program may use at most 320 MiB of HBM per device.

```python
import math
import jax
import jax.numpy as jnp
import numpy as np
from jax import lax

D = 2048
HEADS = 16
HD = 128
ROT = 32
FF = 8192
VOCAB = 25600
TOK_DEV = 128
SEQ_DEV = 3
LONGEST = 96
PIECE = 64
TOKENS = 1024
SEQS = 24
N_DP = 8


def set_ends(entries, rng, least, largest):
    extent = entries.shape
    place = [jax.random.randint(jax.random.fold_in(rng, axis), (), 0, extent[axis]) for axis in range(len(extent))]
    entries = entries.at[tuple(place)].set(least)
    longest = extent.index(max(extent))
    place[longest] = (place[longest] + 1) % extent[longest]
    return entries.at[tuple(place)].set(largest)


def levels(rng, dims, cuts, least, largest):
    loudness = 1.0
    for dim, parts in cuts:
        draws = jax.random.uniform(jax.random.fold_in(jax.random.fold_in(rng, 6), dim), (parts,), jnp.float32, least / len(cuts), largest / len(cuts))
        loudness = loudness * jnp.repeat(jnp.exp(draws), dims[dim] // parts).reshape((-1,) + (1,) * (len(dims) - 1 - dim))
    return loudness


def rank_bounds(number_of, slope):
    portions = [(1 << 20) // math.isqrt(standing ** slope) + 1 for standing in range(1, number_of + 1)]
    deviation = 1 + sum(portions) // (1 << 30)
    return np.cumsum(np.array([max(1, weight // deviation) for weight in portions]))


def ranked(stream_key, extent, number_of, skew):
    table = rank_bounds(number_of, skew)
    lot = jax.random.randint(jax.random.fold_in(stream_key, 1), extent, 0, int(table[number_of - 1]))
    rank = jnp.searchsorted(jnp.asarray(table, jnp.int32), lot, side="right")
    return jax.random.permutation(jax.random.fold_in(stream_key, 2), number_of)[rank].astype(jnp.int32)


def length_profile(count, total, reach, slope):
    portions = [(1 << 20) // math.isqrt(grade ** slope) + 1 for grade in range(2, count + 1)]
    spare, given = total - reach - (count - 1), [1] * (count - 1)
    while spare > 0:
        free = [i for i in range(count - 1) if given[i] < reach]
        whole, remaining = sum([portions[i] for i in free]), spare
        for i in free:
            more = min(reach - given[i], max(1, remaining * portions[i] // whole), spare)
            given[i] = given[i] + more
            spare = spare - more
    return np.array([reach] + given)


def uneven_parts(own_key, amount, total, most, lean):
    if amount == 2:
        one = jax.random.randint(own_key, (), max(1, total - most), min(most, total - 1) + 1)
        return jnp.stack([one, total - one])
    tallies = jnp.asarray(length_profile(amount, total, most, lean), jnp.int32)
    twos = (amount - 1) // 2
    source_of, receiver = tallies[1:1 + 2 * twos:2], tallies[2:2 + 2 * twos:2]
    margin = jnp.minimum(source_of - 1, most - receiver)
    shifted = jax.random.randint(jax.random.fold_in(own_key, 1), (twos,), 0, 1 << 20) % (margin + 1)
    tallies = tallies.at[1:1 + 2 * twos:2].set(source_of - shifted).at[2:2 + 2 * twos:2].set(receiver + shifted)
    return tallies[jax.random.permutation(jax.random.fold_in(own_key, 2), amount)]


def scatter_about(rng, extent, deviation, limit, cuts=(), kind=jnp.bfloat16):
    array = deviation * jax.random.normal(rng, extent, jnp.float32)
    if cuts:
        array = array * levels(rng, extent, cuts, -0.22, 0.18)
    return jnp.clip(array, -limit, limit).astype(kind)


def setup_inputs(seed: int = 0) -> dict:
    key_of = jax.random.split(jax.random.key(seed), 23)
    residual = scatter_about(key_of[0], (TOKENS, D), 1.0, 6.0, ((0, 8),))
    lengths = jax.vmap(lambda own: uneven_parts(own, SEQ_DEV, TOK_DEV, LONGEST, 1))(jax.random.split(key_of[1], N_DP)).reshape((N_DP, SEQ_DEV)).astype(jnp.int32)
    pair_order = jax.random.permutation(key_of[2], 2 * N_DP).astype(jnp.int32)
    token_ids = set_ends(ranked(key_of[3], (TOKENS,), VOCAB, 2), jax.random.fold_in(key_of[3], 3), 0, VOCAB - 1).astype(jnp.int32)
    desirable = set_ends((jax.random.randint(key_of[4], (SEQS,), 0, 4) < 3).astype(jnp.int32), jax.random.fold_in(key_of[4], 1), 0, 1)
    ref_match = jnp.clip(-14.0 + 4.0 * jax.random.uniform(key_of[5], (TOKENS,), jnp.float32) ** levels(key_of[5], (TOKENS,), ((0, 8),), -0.2, 0.2), -14.0, -10.0)
    ref_pair = jnp.clip(-14.0 + 4.0 * jax.random.uniform(key_of[6], (TOKENS,), jnp.float32) ** levels(key_of[6], (TOKENS,), ((0, 8),), -0.2, 0.2), -14.0, -10.0)
    attn_gain = jnp.clip(1.0 + 0.18 * jax.random.normal(key_of[7], (D,), jnp.float32), 0.099609375, 1.8984375).astype(jnp.bfloat16)
    attn_shift = scatter_about(key_of[8], (D,), 0.5, 3.0)
    mlp_gain = jnp.clip(1.0 + 0.18 * jax.random.normal(key_of[9], (D,), jnp.float32), 0.099609375, 1.8984375).astype(jnp.bfloat16)
    mlp_shift = scatter_about(key_of[10], (D,), 0.5, 3.0)
    w_joined = scatter_about(key_of[11], (D, 3 * D), D ** -0.5, 0.125, ((0, 8), (1, 4)))
    b_joined = scatter_about(key_of[12], (3 * D,), 0.5, 3.0, ((0, 4),))
    w_dense = scatter_about(key_of[13], (D, D), (D // 16) ** -0.5, 0.5, ((0, 4), (1, 8)))
    b_dense = scatter_about(key_of[14], (D,), 0.5, 3.0)
    w_up = scatter_about(key_of[15], (D, FF), D ** -0.5, 0.125, ((0, 8), (1, 4)))
    b_up = scatter_about(key_of[16], (FF,), 0.5, 3.0, ((0, 4),))
    w_down = scatter_about(key_of[17], (FF, D), FF ** -0.5, 0.0625, ((0, 4), (1, 8)))
    b_down = scatter_about(key_of[18], (D,), 0.5, 3.0)
    final_gain = jnp.clip(1.0 + 0.18 * jax.random.normal(key_of[19], (D,), jnp.float32), 0.099609375, 1.8984375).astype(jnp.bfloat16)
    final_shift = scatter_about(key_of[20], (D,), 0.5, 3.0)
    w_vocab = scatter_about(key_of[21], (D, VOCAB), (D // 4) ** -0.5, 0.25, ((0, 8), (1, 4)))
    return {"residual": residual, "lengths": lengths, "pair_order": pair_order, "token_ids": token_ids, "desirable": desirable, "ref_match": ref_match, "ref_pair": ref_pair, "attn_gain": attn_gain, "attn_shift": attn_shift, "mlp_gain": mlp_gain, "mlp_shift": mlp_shift, "w_joined": w_joined, "b_joined": b_joined, "w_dense": w_dense, "b_dense": b_dense, "w_up": w_up, "b_up": b_up, "w_down": w_down, "b_down": b_down, "final_gain": final_gain, "final_shift": final_shift, "w_vocab": w_vocab}


kto_beta = 4.0
norm_eps = 1e-05
masked_score = -1e+30

@jax.custom_vjp
def low(v):
    return lax.optimization_barrier(v.astype(jnp.bfloat16)).astype(jnp.float32)

@jax.custom_vjp
def low_back(v):
    return v

def low_keep(v):
    return (low(v), None)

def low_pass(kept, grad):
    return (grad,)

def back_keep(v):
    return (v, None)

def back_low(kept, grad):
    return (low(grad),)
low.defvjp(low_keep, low_pass)
low_back.defvjp(back_keep, back_low)

def layer_norm(values, norm_gain, norm_shift):
    centred = values - lax.optimization_barrier(jnp.mean(values, axis=-1, keepdims=True))
    spread = lax.optimization_barrier(jnp.mean(centred * centred, axis=-1, keepdims=True))
    return centred * lax.rsqrt(spread + norm_eps) * norm_gain + norm_shift

def rotate(values, position):
    half_rot = ROT // 2
    inverse = jnp.exp(jnp.arange(half_rot, dtype=jnp.float32) * (-2.0 * math.log(10000.0) / ROT))
    angles = position.astype(jnp.float32)[:, None] * inverse[None, :]
    cosine_table = jnp.cos(angles)[:, None, :]
    sine_table = jnp.sin(angles)[:, None, :]
    first_half = values[..., :half_rot]
    second_half = values[..., half_rot:ROT]
    return jnp.concatenate([first_half * cosine_table - second_half * sine_table, second_half * cosine_table + first_half * sine_table, values[..., ROT:]], axis=-1)

def device_means(params, rows_float, targets, scored, segment, position, ref_rows, length_both):
    attn_gain, attn_shift, mlp_gain, mlp_shift, w_joined, b_joined, w_dense, b_dense, w_up, b_up, w_down, b_down, final_gain, final_shift, w_vocab = params
    highest_prec = lax.Precision.HIGHEST
    count_rows = rows_float.shape[0]
    attn_in = low(layer_norm(rows_float, attn_gain, attn_shift))
    mlp_in = low(layer_norm(rows_float, mlp_gain, mlp_shift))
    joined_cols = low_back(jnp.dot(attn_in, w_joined, precision=highest_prec) + b_joined)
    joined_cols = joined_cols.reshape(count_rows, HEADS, 3, HD)
    query_val = low(rotate(joined_cols[:, :, 0], position))
    keys_val = low(rotate(joined_cols[:, :, 1], position))
    values_val = low(joined_cols[:, :, 2])
    scores = low_back(jnp.einsum('rhd,chd->hrc', query_val, keys_val, precision=highest_prec) / math.sqrt(HD))
    row_index = jnp.arange(count_rows, dtype=jnp.int32)
    allowed = (segment[:, None] == segment[None, :]) & (row_index[None, :] <= row_index[:, None])
    scores = jnp.where(allowed[None], scores, masked_score)
    highest = lax.optimization_barrier(jnp.max(scores, axis=-1, keepdims=True))
    scaled_exp = jnp.exp(scores - highest)
    probs = low(scaled_exp / lax.optimization_barrier(jnp.sum(scaled_exp, axis=-1, keepdims=True)))
    mixed = jnp.einsum('hrc,chd->rhd', probs, values_val, precision=highest_prec).reshape(count_rows, D)
    mixed = low(low_back(mixed))
    hidden = low_back(jnp.dot(mlp_in, w_up, precision=highest_prec) + b_up)
    active = low(jax.nn.gelu(hidden, approximate=False))
    branch = low_back(jnp.dot(mixed, w_dense, precision=highest_prec) + jnp.dot(active, w_down, precision=highest_prec))
    resid_sum = rows_float + branch + b_dense + b_down
    final_in = low(layer_norm(resid_sum, final_gain, final_shift))
    logits = low_back(jnp.dot(final_in, w_vocab, precision=highest_prec))
    logit_top = lax.optimization_barrier(jnp.max(logits, axis=-1, keepdims=True))
    log_total = logit_top[:, 0] + jnp.log(lax.optimization_barrier(jnp.sum(jnp.exp(logits - logit_top), axis=-1)))
    picked = jnp.take_along_axis(logits, targets[:, None].astype(jnp.int32), axis=1)[:, 0]
    token_terms = (picked - log_total - ref_rows) * scored
    seq_match = segment[:, None] == jnp.arange(2 * SEQ_DEV, dtype=jnp.int32)[None, :]
    seq_sums = lax.optimization_barrier(jnp.sum(jnp.where(seq_match, token_terms[:, None], 0.0), axis=0))
    return seq_sums / length_both

def reference(residual, lengths, pair_order, token_ids, desirable, ref_match, ref_pair, attn_gain, attn_shift, mlp_gain, mlp_shift, w_joined, b_joined, w_dense, b_dense, w_up, b_up, w_down, b_down, final_gain, final_shift, w_vocab):
    params = tuple((value.astype(jnp.float32) for value in (attn_gain, attn_shift, mlp_gain, mlp_shift, w_joined, b_joined, w_dense, b_dense, w_up, b_up, w_down, b_down, final_gain, final_shift, w_vocab)))
    inputs = residual.astype(jnp.float32)
    block_count = 2 * N_DP
    block_slots = jnp.arange(block_count, dtype=jnp.int32)
    source_block = lax.optimization_barrier(jnp.sum(jnp.where(pair_order.astype(jnp.int32)[None, :] == block_slots[:, None], block_slots[None, :], 0), axis=1)).astype(jnp.int32)
    paired_ids = token_ids.reshape(block_count, PIECE)[source_block].reshape(N_DP, TOK_DEV)
    ids_all = jnp.concatenate([token_ids.reshape(N_DP, TOK_DEV), paired_ids], axis=1)
    seq_ends = jnp.cumsum(lengths, axis=1).astype(jnp.int32)
    seq_starts = (seq_ends - lengths).astype(jnp.int32)
    places = jnp.arange(TOK_DEV, dtype=jnp.int32)
    segment = lax.optimization_barrier(jnp.sum((places[None, :, None] >= seq_ends[:, None, :]).astype(jnp.int32), axis=2))
    own_start = jnp.take_along_axis(seq_starts, segment, axis=1)
    position_half = places[None, :] - own_start
    segment_all = jnp.concatenate([segment, segment + SEQ_DEV], axis=1)
    position = jnp.concatenate([position_half, position_half], axis=1)
    targets = jnp.concatenate([ids_all[:, 1:], jnp.zeros((N_DP, 1), jnp.int32)], axis=1)
    scored = jnp.concatenate([segment_all[:, 1:] == segment_all[:, :-1], jnp.zeros((N_DP, 1), jnp.bool_)], axis=1).astype(jnp.float32)
    ref_rows = jnp.concatenate([ref_match.reshape(N_DP, TOK_DEV), ref_pair.reshape(N_DP, TOK_DEV)], axis=1)
    length_float = lengths.astype(jnp.float32)
    length_both = jnp.concatenate([length_float, length_float], axis=1)
    signs = 2.0 * desirable.astype(jnp.float32) - 1.0

    def objective(param_set, input_rows):
        blocks = input_rows.reshape(block_count, PIECE, D)
        paired = blocks[source_block].reshape(N_DP, TOK_DEV, D)
        rows_all = jnp.concatenate([input_rows.reshape(N_DP, TOK_DEV, D), paired], axis=1)

        def one_index(operands):
            return device_means(param_set, *operands)
        seq_means = lax.map(jax.checkpoint(one_index), (rows_all, targets, scored, segment_all, position, ref_rows, length_both))
        kl_value = jnp.sum(seq_means[:, SEQ_DEV:]) / SEQS
        own_means = seq_means[:, :SEQ_DEV].reshape(SEQS)
        sigmoid_val = jax.nn.sigmoid(kto_beta * signs * (own_means - kl_value))
        return (jnp.sum(1.0 - sigmoid_val), kl_value)
    (kto_loss, kl_estimate), pullback = jax.vjp(objective, params, inputs)
    param_grads, grad_input = pullback((jnp.ones_like(kto_loss), jnp.zeros_like(kl_estimate)))
    return (kto_loss, kl_estimate, grad_input, param_grads[0], param_grads[1], param_grads[2], param_grads[3], param_grads[4], param_grads[5], param_grads[6], param_grads[7], param_grads[8], param_grads[9], param_grads[10], param_grads[11], param_grads[12], param_grads[13], param_grads[14])
```

```python
import functools
import math

import jax
import jax.numpy as jnp
from jax import lax
from jax.experimental import pallas as pl
from jax.experimental.pallas import tpu as pltpu
from jax.sharding import PartitionSpec as P

HD = 128
ROT = 32


kto_beta = 4.0
norm_eps = 1e-05
masked_score = -1e30


def joined(value, axis, join):
    pieces = jax.tree.map(lambda part: lax.all_gather(part, axis), value)
    head = jax.tree.map(lambda part: part[0], pieces)
    tail = jax.tree.map(lambda part: part[1:], pieces)
    subtotal, _ = lax.scan(lambda subtotal, piece: (join(subtotal, piece), None), head, tail)
    return subtotal


def layer_norm(values, norm_gain, norm_shift):
    centred = values - jnp.mean(values, axis=-1, keepdims=True)
    spread = jnp.mean(centred * centred, axis=-1, keepdims=True)
    return centred * lax.rsqrt(spread + norm_eps) * norm_gain + norm_shift


def rotate(values, position):
    half_rot = ROT // 2
    inverse = jnp.exp(jnp.arange(half_rot, dtype=jnp.float32) * (-2.0 * math.log(10000.0) / ROT))
    angles = position.astype(jnp.float32)[:, None] * inverse[None, :]
    cosine_table = jnp.cos(angles)[:, None, :]
    sine_table = jnp.sin(angles)[:, None, :]
    first_half = values[..., :half_rot]
    second_half = values[..., half_rot:ROT]
    return jnp.concatenate(
        [
            first_half * cosine_table - second_half * sine_table,
            second_half * cosine_table + first_half * sine_table,
            values[..., ROT:],
        ],
        axis=-1,
    )


def gelu_exact(values):
    return jax.nn.gelu(values, approximate=False)


def attention_scores(query_low, keys_low, allowed):
    raw_scores = jnp.einsum(
        "rhd,chd->hrc", query_low, keys_low, preferred_element_type=jnp.float32
    ) / math.sqrt(HD)
    return jnp.where(allowed[None], raw_scores, masked_score)


def combine_vocab(first, second):
    high_first, total_first, pick_first = first
    high_second, total_second, pick_second = second
    highest = jnp.maximum(high_first, high_second)
    merged_total = total_first * jnp.exp(high_first - highest) + total_second * jnp.exp(
        high_second - highest
    )
    return (highest, merged_total, pick_first + pick_second)


def gather_weights(weights_low):
    w_joined, w_up, w_vocab, w_dense, w_down = weights_low
    joined_all, up_all, vocab_all = (
        lax.all_gather(w_joined, "dp", axis=0, tiled=True),
        lax.all_gather(w_up, "dp", axis=0, tiled=True),
        lax.all_gather(w_vocab, "dp", axis=0, tiled=True),
    )
    dense_all, down_all = (
        lax.all_gather(w_dense, "dp", axis=1, tiled=True),
        lax.all_gather(w_down, "dp", axis=1, tiled=True),
    )
    return (joined_all, up_all, vocab_all, dense_all, down_all)


def forward_pass(gathered, smalls, rows_low, allowed, position, targets):
    joined_all, up_all, vocab_all, dense_all, down_all = gathered
    (
        attn_gain,
        attn_shift,
        mlp_gain,
        mlp_shift,
        b_joined,
        b_dense,
        b_up,
        b_down,
        final_gain,
        final_shift,
    ) = smalls
    rows_float = rows_low.astype(jnp.float32)
    count_rows = rows_float.shape[0]
    attn_low = layer_norm(rows_float, attn_gain, attn_shift).astype(jnp.bfloat16)
    mlp_low = layer_norm(rows_float, mlp_gain, mlp_shift).astype(jnp.bfloat16)
    joined_cols = jnp.dot(attn_low, joined_all, preferred_element_type=jnp.float32) + b_joined
    joined_cols = joined_cols.reshape(count_rows, -1, 3, HD)
    query_low = rotate(joined_cols[:, :, 0], position).astype(jnp.bfloat16)
    keys_low = rotate(joined_cols[:, :, 1], position).astype(jnp.bfloat16)
    values_low = joined_cols[:, :, 2].astype(jnp.bfloat16)
    scores = attention_scores(query_low, keys_low, allowed)
    highest = jnp.max(scores, axis=-1, keepdims=True)
    scaled_exp = jnp.exp(scores - highest)
    totals = jnp.sum(scaled_exp, axis=-1, keepdims=True)
    probs_low = (scaled_exp / totals).astype(jnp.bfloat16)
    score_lse = highest + jnp.log(totals)
    mixed_low = (
        jnp.einsum("hrc,chd->rhd", probs_low, values_low, preferred_element_type=jnp.float32)
        .reshape(count_rows, -1)
        .astype(jnp.bfloat16)
    )
    hidden = jnp.dot(mlp_low, up_all, preferred_element_type=jnp.float32) + b_up
    active_low = gelu_exact(hidden).astype(jnp.bfloat16)
    branch_part = jnp.dot(mixed_low, dense_all, preferred_element_type=jnp.float32) + jnp.dot(
        active_low, down_all, preferred_element_type=jnp.float32
    )
    branch = lax.psum(branch_part, "mp")
    resid_sum = rows_float + branch + b_dense + b_down
    final_low = layer_norm(resid_sum, final_gain, final_shift).astype(jnp.bfloat16)
    logits = jnp.dot(final_low, vocab_all, preferred_element_type=jnp.float32)
    local_high = jnp.max(logits, axis=-1)
    local_total = jnp.sum(jnp.exp(logits - local_high[:, None]), axis=-1)
    column = targets - lax.axis_index("mp") * logits.shape[1]
    target_hit = lax.broadcasted_iota(jnp.int32, logits.shape, 1) == column[:, None]
    local_pick = jnp.sum(jnp.where(target_hit, logits, 0.0), axis=-1)
    high_all, total_all, picked = joined((local_high, local_total, local_pick), "mp", combine_vocab)
    vocab_lse = high_all + jnp.log(total_all)
    return (
        attn_low,
        mlp_low,
        joined_cols,
        query_low,
        keys_low,
        values_low,
        score_lse,
        mixed_low,
        hidden,
        active_low,
        resid_sum,
        final_low,
        logits,
        vocab_lse,
        target_hit,
        picked - vocab_lse,
    )


def shards(
    residual,
    lengths,
    pair_order,
    token_ids,
    desirable,
    ref_match,
    ref_pair,
    attn_gain,
    attn_shift,
    mlp_gain,
    mlp_shift,
    w_joined,
    b_joined,
    w_dense,
    b_dense,
    w_up,
    b_up,
    w_down,
    b_down,
    final_gain,
    final_shift,
    w_vocab,
):
    dp_count = lax.axis_size("dp")
    tokens_here = residual.shape[0]
    piece_rows = tokens_here // 2
    width = residual.shape[1]
    seq_here = lengths.shape[1]
    block_count = 2 * dp_count
    my_index = lax.axis_index("dp")
    block_slots = jnp.arange(block_count, dtype=jnp.int32)
    my_blocks = 2 * my_index + jnp.arange(2, dtype=jnp.int32)
    my_targets = jnp.sum(
        jnp.where(block_slots[None, :] == my_blocks[:, None], pair_order[None, :], 0), axis=1
    )
    send_hot = my_targets[:, None] == block_slots[None, :]
    own_blocks = residual.reshape(2, piece_rows, width)
    own_ids = token_ids.reshape(2, piece_rows)
    sent_rows = jnp.einsum(
        "ht,hpd->tpd", send_hot.astype(jnp.bfloat16), own_blocks, preferred_element_type=jnp.float32
    ).astype(jnp.bfloat16)
    sent_ids = jnp.sum(jnp.where(send_hot[:, :, None], own_ids[:, None, :], 0), axis=0)
    got_rows, got_ids = (
        lax.all_to_all(
            sent_rows.reshape(dp_count, 2, piece_rows, width),
            "dp",
            split_axis=0,
            concat_axis=0,
            tiled=True,
        ),
        lax.all_to_all(
            sent_ids.reshape(dp_count, 2, piece_rows), "dp", split_axis=0, concat_axis=0, tiled=True
        ),
    )
    paired_rows = jnp.sum(got_rows.astype(jnp.float32), axis=0).astype(jnp.bfloat16)
    paired_ids = jnp.sum(got_ids, axis=0)
    rows_low = jnp.concatenate([residual, paired_rows.reshape(tokens_here, width)], axis=0)
    ids_all = jnp.concatenate([token_ids, paired_ids.reshape(tokens_here)], axis=0)
    seq_lengths = lengths[0]
    seq_slots = jnp.arange(seq_here, dtype=jnp.int32)
    seq_ends = jnp.sum(
        jnp.where(seq_slots[None, :] <= seq_slots[:, None], seq_lengths[None, :], 0), axis=1
    )
    seq_starts = seq_ends - seq_lengths
    places = jnp.arange(tokens_here, dtype=jnp.int32)
    segment = jnp.sum((places[:, None] >= seq_ends[None, :]).astype(jnp.int32), axis=1)
    own_start = jnp.sum(
        jnp.where(segment[:, None] == seq_slots[None, :], seq_starts[None, :], 0), axis=1
    )
    position_half = places - own_start
    segment_all = jnp.concatenate([segment, segment + seq_here])
    position = jnp.concatenate([position_half, position_half])
    count_rows = 2 * tokens_here
    row_index = jnp.arange(count_rows, dtype=jnp.int32)
    allowed = (segment_all[:, None] == segment_all[None, :]) & (
        row_index[None, :] <= row_index[:, None]
    )
    targets = jnp.concatenate([ids_all[1:], jnp.zeros((1,), jnp.int32)])
    scored = jnp.concatenate(
        [segment_all[1:] == segment_all[:-1], jnp.zeros((1,), jnp.bool_)]
    ).astype(jnp.float32)
    ref_rows = jnp.concatenate([ref_match, ref_pair])
    length_float = seq_lengths.astype(jnp.float32)
    length_both = jnp.concatenate([length_float, length_float])
    seq_match = segment_all[:, None] == jnp.arange(2 * seq_here, dtype=jnp.int32)[None, :]
    smalls = tuple(
        (
            value.astype(jnp.float32)
            for value in (
                attn_gain,
                attn_shift,
                mlp_gain,
                mlp_shift,
                b_joined,
                b_dense,
                b_up,
                b_down,
                final_gain,
                final_shift,
            )
        )
    )
    weights_low = (w_joined, w_up, w_vocab, w_dense, w_down)
    gathered = gather_weights(weights_low)
    first_pass = forward_pass(gathered, smalls, rows_low, allowed, position, targets)
    token_terms = (first_pass[15] - ref_rows) * scored
    seq_means = jnp.sum(jnp.where(seq_match, token_terms[:, None], 0.0), axis=0) / length_both
    kl_total = lax.psum(jnp.sum(seq_means[seq_here:]), "dp")
    seq_total = seq_here * dp_count
    kl_estimate = kl_total / seq_total
    signs = 2.0 * desirable.astype(jnp.float32) - 1.0
    sigmoid_val = jax.nn.sigmoid(kto_beta * signs * (seq_means[:seq_here] - kl_estimate))
    slope = -kto_beta * signs * sigmoid_val * (1.0 - sigmoid_val)
    kto_loss, slope_total = lax.psum((jnp.sum(1.0 - sigmoid_val), jnp.sum(slope)), "dp")
    seq_coef = (
        jnp.concatenate([slope, jnp.broadcast_to(-slope_total / seq_total, (seq_here,))])
        / length_both
    )
    token_coef = jnp.sum(jnp.where(seq_match, seq_coef[None, :], 0.0), axis=1) * scored
    matrices = gather_weights(weights_low)
    current = forward_pass(matrices, smalls, rows_low, allowed, position, targets)
    joined_all, up_all, vocab_all, dense_all, down_all = matrices
    (
        attn_low,
        mlp_low,
        joined_cols,
        query_low,
        keys_low,
        values_low,
        score_lse,
        mixed_low,
        hidden,
        active_low,
        resid_sum,
        final_low,
        logits,
        vocab_lse,
        target_hit,
        log_probs,
    ) = current
    softmax_local = jnp.exp(logits - vocab_lse[:, None])
    dlogits = (token_coef[:, None] * (jnp.where(target_hit, 1.0, 0.0) - softmax_local)).astype(
        jnp.bfloat16
    )
    grad_vocab = jnp.einsum("rd,rv->dv", final_low, dlogits, preferred_element_type=jnp.float32)
    dfinal_part = jnp.einsum("rv,dv->rd", dlogits, vocab_all, preferred_element_type=jnp.float32)
    dfinal = lax.psum(dfinal_part, "mp")
    _, final_pull = jax.vjp(layer_norm, resid_sum, smalls[8], smalls[9])
    dresid, grad_final_gain, grad_final_shift = final_pull(dfinal)
    grad_b_out = jnp.sum(dresid, axis=0)
    dbranch = dresid.astype(jnp.bfloat16)
    grad_dense = jnp.einsum("rk,rd->kd", mixed_low, dbranch, preferred_element_type=jnp.float32)
    grad_down = jnp.einsum("rf,rd->fd", active_low, dbranch, preferred_element_type=jnp.float32)
    dmixed = jnp.einsum("rd,kd->rk", dbranch, dense_all, preferred_element_type=jnp.float32).astype(
        jnp.bfloat16
    )
    dactive = jnp.einsum("rd,fd->rf", dbranch, down_all, preferred_element_type=jnp.float32)
    _, gelu_pull = jax.vjp(gelu_exact, hidden)
    dhidden = gelu_pull(dactive)[0].astype(jnp.bfloat16)
    grad_up = jnp.einsum("rd,rf->df", mlp_low, dhidden, preferred_element_type=jnp.float32)
    grad_b_up = jnp.sum(dhidden.astype(jnp.float32), axis=0)
    dmlp_part = jnp.einsum("rf,df->rd", dhidden, up_all, preferred_element_type=jnp.float32)
    dmixed_heads = dmixed.reshape(count_rows, -1, HD)
    scores = attention_scores(query_low, keys_low, allowed)
    probs_float = jnp.where(allowed[None], jnp.exp(scores - score_lse), 0.0)
    dvalues = jnp.einsum(
        "hrc,rhd->chd",
        probs_float.astype(jnp.bfloat16),
        dmixed_heads,
        preferred_element_type=jnp.float32,
    )
    dprobs = jnp.einsum(
        "rhd,chd->hrc", dmixed_heads, values_low, preferred_element_type=jnp.float32
    )
    inner_sum = jnp.sum(probs_float * dprobs, axis=-1, keepdims=True)
    dscores = (probs_float * (dprobs - inner_sum)).astype(jnp.bfloat16)
    dquery = jnp.einsum(
        "hrc,chd->rhd", dscores, keys_low, preferred_element_type=jnp.float32
    ) / math.sqrt(HD)
    dkeys = jnp.einsum(
        "hrc,rhd->chd", dscores, query_low, preferred_element_type=jnp.float32
    ) / math.sqrt(HD)
    _, rotate_pull = jax.vjp(lambda value: rotate(value, position), joined_cols[:, :, 0])
    dfused = jnp.stack([rotate_pull(dquery)[0], rotate_pull(dkeys)[0], dvalues], axis=2)
    dfused = dfused.reshape(count_rows, -1).astype(jnp.bfloat16)
    grad_joined = jnp.einsum("rd,re->de", attn_low, dfused, preferred_element_type=jnp.float32)
    grad_b_joined = jnp.sum(dfused.astype(jnp.float32), axis=0)
    dattn_part = jnp.einsum("re,de->rd", dfused, joined_all, preferred_element_type=jnp.float32)
    dattn, dmlp = lax.psum((dattn_part, dmlp_part), "mp")
    rows_float = rows_low.astype(jnp.float32)
    _, attn_pull = jax.vjp(layer_norm, rows_float, smalls[0], smalls[1])
    drows_attn, grad_attn_gain, grad_attn_shift = attn_pull(dattn)
    _, mlp_pull = jax.vjp(layer_norm, rows_float, smalls[2], smalls[3])
    drows_mlp, grad_mlp_gain, grad_mlp_shift = mlp_pull(dmlp)
    drows = dresid + drows_attn + drows_mlp
    my_slots = 2 * my_index + jnp.arange(2, dtype=jnp.int32)
    anchor = jnp.sum(
        jnp.where(pair_order[None, :] == my_slots[:, None], block_slots[None, :], 0), axis=1
    )
    back_hot = (anchor[:, None] == block_slots[None, :]).astype(jnp.float32)
    back_blocks = drows[tokens_here:].reshape(2, piece_rows, width)
    back_sent = jnp.einsum("st,spd->tpd", back_hot, back_blocks, precision=lax.Precision.HIGHEST)
    returned = lax.all_to_all(
        back_sent.reshape(dp_count, 2, piece_rows, width),
        "dp",
        split_axis=0,
        concat_axis=0,
        tiled=True,
    )
    grad_input = drows[:tokens_here] + jnp.sum(returned, axis=0).reshape(tokens_here, width)
    gw_joined, gw_up, gw_vocab = (
        lax.psum_scatter(grad_joined, "dp", scatter_dimension=0, tiled=True),
        lax.psum_scatter(grad_up, "dp", scatter_dimension=0, tiled=True),
        lax.psum_scatter(grad_vocab, "dp", scatter_dimension=0, tiled=True),
    )
    gw_dense, gw_down = (
        lax.psum_scatter(grad_dense, "dp", scatter_dimension=1, tiled=True),
        lax.psum_scatter(grad_down, "dp", scatter_dimension=1, tiled=True),
    )
    (
        sg_attn_gain,
        sg_attn_shift,
        sg_mlp_gain,
        sg_mlp_shift,
        sg_b_joined,
        sg_b_up,
        sg_b_out,
        sg_final_gain,
        sg_final_shift,
    ) = lax.psum(
        (
            grad_attn_gain,
            grad_attn_shift,
            grad_mlp_gain,
            grad_mlp_shift,
            grad_b_joined,
            grad_b_up,
            grad_b_out,
            grad_final_gain,
            grad_final_shift,
        ),
        "dp",
    )
    return (
        kto_loss,
        kl_estimate,
        grad_input,
        sg_attn_gain,
        sg_attn_shift,
        sg_mlp_gain,
        sg_mlp_shift,
        gw_joined,
        sg_b_joined,
        gw_dense,
        sg_b_out,
        gw_up,
        sg_b_up,
        gw_down,
        sg_b_out,
        sg_final_gain,
        sg_final_shift,
        gw_vocab,
    )


DP = ("z", "y")
CHIPS = ("z", "y", "x")
ALL = ("z", "y", "x", "c")
SWAP = ((0, 1), (1, 0))
F32, BF16 = jnp.float32, jnp.bfloat16


def dot(a, b, contract):
    return lax.dot_general(a, b, ((contract[:1], contract[1:]), ((), ())), preferred_element_type=F32)


def swap(value):
    return lax.ppermute(value, "c", SWAP)


def normed(values):
    centred = values - jnp.mean(values, axis=-1, keepdims=True)
    inverse = lax.rsqrt(jnp.mean(centred * centred, axis=-1, keepdims=True) + norm_eps)
    return centred * inverse, inverse


def norm_back(t, hat, inverse):
    return inverse * (
        t - jnp.mean(t, axis=-1, keepdims=True) - hat * jnp.mean(t * hat, axis=-1, keepdims=True)
    )


def turn(values, cosine, sine):
    half_rot = ROT // 2
    first, second = values[:, :half_rot], values[:, half_rot:ROT]
    return jnp.concatenate(
        [first * cosine - second * sine, second * cosine + first * sine, values[:, ROT:]], axis=1
    )


def copy_block(order_ref, from_ref, to_ref):
    to_ref[...] = from_ref[...]


def take_blocks(values, order, piece):
    count, width = values.shape[0] // piece, values.shape[1]
    return pl.pallas_call(
        copy_block,
        out_shape=jax.ShapeDtypeStruct(values.shape, values.dtype),
        grid_spec=pltpu.PrefetchScalarGridSpec(
            num_scalar_prefetch=1,
            grid=(count,),
            in_specs=[pl.BlockSpec((piece, width), lambda i, order: (order[i], 0))],
            out_specs=pl.BlockSpec((piece, width), lambda i, order: (i, 0)),
        ),
    )(order, values)


def exchange(value):
    return lax.all_to_all(value, DP, split_axis=0, concat_axis=0, tiled=True)


def here():
    return tuple(lax.axis_index(a) for a in ALL)


def send(source, target, out_sem, in_sem, device):
    copy = pltpu.make_async_remote_copy(
        src_ref=source,
        dst_ref=target,
        send_sem=out_sem,
        recv_sem=in_sem,
        device_id=device,
        device_id_type=pl.DeviceIdType.MESH,
    )
    copy.start()
    return copy


def arrived(target, out_sem, in_sem, device):
    pltpu.make_async_remote_copy(
        src_ref=target,
        dst_ref=target,
        send_sem=out_sem,
        recv_sem=in_sem,
        device_id=device,
        device_id_type=pl.DeviceIdType.MESH,
    ).wait_recv()


def greet(devices):
    barrier = pltpu.get_barrier_semaphore()
    for device in devices:
        pl.semaphore_signal(barrier, inc=1, device_id=device, device_id_type=pl.DeviceIdType.MESH)
    pl.semaphore_wait(barrier, len(devices))


def neighbours(nz):
    iz, iy, ix, ic = here()
    return [(lax.rem(iz + k, nz), iy, ix, ic) for k in range(1, nz)] + [
        (iz, 1 - iy, ix, ic),
        (iz, iy, 1 - ix, ic),
    ]


def other_core():
    iz, iy, ix, ic = here()
    return (iz, iy, ix, 1 - ic)


class Reduce:
    @staticmethod
    def scratch(nz, half, width):
        dma = pltpu.SemaphoreType.DMA
        return [
            pltpu.VMEM((2, nz, 2, half, width), BF16),
            pltpu.VMEM((2, nz, half, width), BF16),
            pltpu.VMEM((2, nz, half, width), BF16),
            pltpu.VMEM((2, nz, half, width), BF16),
            pltpu.VMEM((2, nz, half, width), BF16),
            dma((2, nz, 2)),
            dma((2, nz, 2)),
            dma((2, nz)),
            dma((2, nz)),
            dma((2, nz)),
            dma((2, nz)),
        ]

    def __init__(self, nz, half, part, refs):
        self.nz, self.half, self.part = nz, half, part
        (
            self.in1,
            self.out2,
            self.in2,
            self.out3,
            self.in3,
            self.s1,
            self.r1,
            self.s2,
            self.r2,
            self.s3,
            self.r3,
        ) = refs
        self.copies = []

    def along(self, h):
        iz, iy, ix, ic = here()
        across_x, across_y = (iz, iy, 1 - ix, ic), (iz, 1 - iy, ix, ic)
        return (across_x, across_y) if h == 0 else (across_y, across_x)

    def block(self, h, z, first_mine, second):
        _, iy, ix, _ = here()
        rows = pl.ds(h * self.half, self.half)
        if h == 0:
            return self.part.at[z, second, ix if first_mine else 1 - ix, rows]
        return self.part.at[z, iy if first_mine else 1 - iy, second, rows]

    def mine(self, h):
        _, iy, ix, _ = here()
        return iy if h == 0 else ix

    def plane(self, k):
        return lax.rem(here()[0] + k, self.nz)

    def start(self, h, far):
        first, _ = self.along(h)
        second = 1 - self.mine(h) if far else self.mine(h)
        for k in list(range(1, self.nz)) + [0]:
            z = self.plane(k)
            self.copies.append(
                send(
                    self.block(h, z, False, second),
                    self.in1.at[h, z, second],
                    self.s1.at[h, z, second],
                    self.r1.at[h, z, second],
                    first,
                )
            )

    def second(self, h):
        first, across = self.along(h)
        far = 1 - self.mine(h)
        for k in list(range(1, self.nz)) + [0]:
            z = self.plane(k)
            arrived(self.in1.at[h, z, far], self.s1.at[h, z, far], self.r1.at[h, z, far], first)
            self.out2[h, z] = (
                self.block(h, z, True, far)[...].astype(F32) + self.in1[h, z, far].astype(F32)
            ).astype(BF16)
            self.copies.append(
                send(self.out2.at[h, z], self.in2.at[h, z], self.s2.at[h, z], self.r2.at[h, z], across)
            )

    def third(self, h):
        iz, iy, ix, ic = here()
        first, across = self.along(h)
        near = self.mine(h)
        for k in list(range(1, self.nz)) + [0]:
            z = self.plane(k)
            arrived(self.in1.at[h, z, near], self.s1.at[h, z, near], self.r1.at[h, z, near], first)
            arrived(self.in2.at[h, z], self.s2.at[h, z], self.r2.at[h, z], across)
            total = (
                self.block(h, z, True, near)[...].astype(F32)
                + self.in1[h, z, near].astype(F32)
                + self.in2[h, z].astype(F32)
            )
            if k == 0:
                return total
            self.out3[h, k] = total.astype(BF16)
            self.copies.append(
                send(
                    self.out3.at[h, k],
                    self.in3.at[h, k],
                    self.s3.at[h, k],
                    self.r3.at[h, k],
                    (z, iy, ix, ic),
                )
            )

    def finish(self, h, total):
        _, iy, ix, ic = here()
        for k in range(1, self.nz):
            z = self.plane(self.nz - k)
            arrived(self.in3.at[h, k], self.s3.at[h, k], self.r3.at[h, k], (z, iy, ix, ic))
            total = total + self.in3[h, k].astype(F32)
        return total


class Gather:
    @staticmethod
    def scratch(nz):
        dma = pltpu.SemaphoreType.DMA
        return [dma((2, nz)), dma((2, nz)), dma((2, nz, 2)), dma((2, nz, 2, 2)), dma((2,))]

    def __init__(self, nz, half, out, refs, forward=None):
        self.nz, self.half, self.out = nz, half, out
        self.sz, self.sp, self.sq, self.r, self.local = refs
        self.copies, self.locals, self.forward = [], [], forward

    def axes(self, h):
        iz, iy, ix, ic = here()
        across_x, across_y = (iz, iy, 1 - ix, ic), (iz, 1 - iy, ix, ic)
        return (across_y, across_x) if h == 0 else (across_x, across_y)

    def block(self, h, z, y, x):
        return self.out.at[z, y, x, pl.ds(h * self.half, self.half)]

    def on(self, h, source, z, y, x, which):
        iz, iy, ix, ic = here()
        p, q = self.axes(h)
        there, got = self.block(h, z, y, x), self.r.at[h, z, y, x]
        if "z" in which:
            for k in range(1, self.nz):
                far = (lax.rem(iz + k, self.nz), iy, ix, ic)
                self.copies.append(send(source, there, self.sz.at[h, k], got, far))
        if "p" in which:
            self.copies.append(send(source, there, self.sp.at[h, z], got, p))
        if "q" in which:
            side = x if h == 1 else y
            self.copies.append(send(source, there, self.sq.at[h, z, side], got, q))
        if self.forward is not None:
            self.forward(h, source, z, y, x)

    def start(self, h, source):
        iz, iy, ix, _ = here()
        copy = pltpu.make_async_copy(source, self.block(h, iz, iy, ix), self.local.at[h])
        copy.start()
        self.locals.append(copy)
        self.on(h, source, iz, iy, ix, "zpq")

    def got(self, h, z, y, x):
        arrived(self.block(h, z, y, x), self.sz.at[h, 0], self.r.at[h, z, y, x], self.axes(h)[0])

    def first(self, h, k):
        iz, iy, ix, _ = here()
        z = lax.rem(iz + k, self.nz)
        self.got(h, z, iy, ix)
        self.on(h, self.block(h, z, iy, ix), z, iy, ix, "pq")

    def second(self, h, k):
        iz, iy, ix, _ = here()
        z = lax.rem(iz + k, self.nz)
        y, x = (1 - iy, ix) if h == 0 else (iy, 1 - ix)
        self.got(h, z, y, x)
        self.on(h, self.block(h, z, y, x), z, y, x, "q")

    def third(self, h, k):
        iz, iy, ix, _ = here()
        z = lax.rem(iz + k, self.nz)
        for side in (0, 1):
            if h == 0:
                y, x = (iy if side == 0 else 1 - iy), 1 - ix
            else:
                y, x = 1 - iy, (ix if side == 0 else 1 - ix)
            self.got(h, z, y, x)
            if self.forward is not None:
                self.forward(h, self.block(h, z, y, x), z, y, x)

    def rest(self):
        turns = [1, self.nz - 1] + [k for k in range(2, self.nz - 1)]
        for h in (0, 1):
            self.second(h, 0)
        for k in turns:
            for h in (0, 1):
                self.first(h, k)
        for k in turns:
            for h in (0, 1):
                self.second(h, k)
        for k in [0] + turns:
            for h in (0, 1):
                self.third(h, k)

    def end(self):
        for copy in self.locals:
            copy.wait()
        for copy in self.copies:
            copy.wait_send()


def run_reduce(reduce):
    for far in (True, False):
        for h in (0, 1):
            reduce.start(h, far)
    for h in (0, 1):
        reduce.second(h)


def forward_kernel(nz, half, part, rows, bias, gain, shift, out, resid, fin, *refs):
    reduce = Reduce(nz, half, part, refs[:11])
    gather = Gather(nz, half, out, refs[11:])
    greet(neighbours(nz))
    run_reduce(reduce)
    kept = [reduce.third(h) for h in (0, 1)]
    for h in (0, 1):
        at = pl.ds(h * half, half)
        total = rows[at].astype(F32) + reduce.finish(h, kept[h]) + bias[...]
        resid[at] = total
        hat, _ = normed(total)
        fin[h] = (hat * gain[...] + shift[...]).astype(BF16)
        gather.start(h, fin.at[h])
    gather.rest()
    gather.end()
    for copy in reduce.copies:
        copy.wait_send()


def backward_kernel(nz, half, part, resid, gain, out, vectors, fin, *refs):
    reduce = Reduce(nz, half, part, refs[:11])
    gather = Gather(nz, half, out, refs[11:])
    greet(neighbours(nz))
    run_reduce(reduce)
    kept = [reduce.third(h) for h in (0, 1)]
    sums = []
    for h in (0, 1):
        total = reduce.finish(h, kept[h])
        hat, inverse = normed(resid[pl.ds(h * half, half)])
        dresid = norm_back(total * gain[...], hat, inverse)
        fin[h] = dresid.astype(BF16)
        gather.start(h, fin.at[h])
        sums.append([jnp.sum(v, axis=0, keepdims=True) for v in (total * hat, total, dresid)])
    for i in range(3):
        vectors[pl.ds(i, 1)] = sums[0][i] + sums[1][i]
    gather.rest()
    gather.end()
    for copy in reduce.copies:
        copy.wait_send()


def vmem():
    return pl.BlockSpec(memory_space=pltpu.VMEM)


def anywhere():
    return pl.BlockSpec(memory_space=pl.ANY)


def comm(which, limit=48):
    return pltpu.CompilerParams(collective_id=which, has_side_effects=True, vmem_limit_bytes=limit << 20)


def reduce_norm_gather(nz, part, rows, bias, gain, shift):
    share, width = rows.shape
    half = share // 2
    out, resid = pl.pallas_call(
        functools.partial(forward_kernel, nz, half),
        out_shape=[
            jax.ShapeDtypeStruct((nz, 2, 2, share, width), BF16),
            jax.ShapeDtypeStruct((share, width), F32),
        ],
        in_specs=[vmem()] * 5,
        out_specs=[anywhere(), vmem()],
        scratch_shapes=[pltpu.VMEM((2, half, width), BF16)]
        + Reduce.scratch(nz, half, width)
        + Gather.scratch(nz),
        compiler_params=comm(2),
    )(part.reshape(nz, 2, 2, share, width), rows, bias, gain, shift)
    return out.reshape(4 * nz * share, width), resid


def reduce_back_gather(nz, part, resid, gain):
    share, width = resid.shape
    half = share // 2
    out, vectors = pl.pallas_call(
        functools.partial(backward_kernel, nz, half),
        out_shape=[
            jax.ShapeDtypeStruct((nz, 2, 2, share, width), BF16),
            jax.ShapeDtypeStruct((3, width), F32),
        ],
        in_specs=[vmem()] * 3,
        out_specs=[anywhere(), vmem()],
        scratch_shapes=[pltpu.VMEM((2, half, width), BF16)]
        + Reduce.scratch(nz, half, width)
        + Gather.scratch(nz),
        compiler_params=comm(3),
    )(part.reshape(nz, 2, 2, share, width), resid, gain)
    return out.reshape(4 * nz * share, width), vectors


def merge(a, b):
    top = jnp.maximum(a[0], b[0])
    return (top, a[1] * jnp.exp(a[0] - top) + b[1] * jnp.exp(b[0] - top), a[2] + b[2])


def objective_kernel(
    nz, seqs, seq_total, stats, hot, scored, refs, lens, wanted, coef, lse_out, scalars, held, got, ss, rs
):
    iz, iy, ix, ic = here()
    peers = neighbours(nz) + [other_core()]
    greet(peers)
    current = tuple(stats[i] for i in range(3))
    copies = []
    for step, (mine, device) in enumerate(((ix, (iz, iy, 1 - ix, ic)), (iy, (iz, 1 - iy, ix, ic)))):
        for i in range(3):
            held[step, i] = current[i]
        copies.append(send(held.at[step], got.at[step], ss.at[step], rs.at[step], device))
        arrived(got.at[step], ss.at[step], rs.at[step], device)
        theirs = tuple(got[step, i] for i in range(3))
        low = tuple(jnp.where(mine == 0, a, b) for a, b in zip(current, theirs))
        high = tuple(jnp.where(mine == 0, b, a) for a, b in zip(current, theirs))
        current = merge(low, high)
    for i in range(3):
        held[2, i] = current[i]
    for k in range(1, nz):
        z = lax.rem(iz + k, nz)
        copies.append(send(held.at[2], got.at[2 + iz], ss.at[2 + k], rs.at[2 + iz], (z, iy, ix, ic)))
    for i in range(3):
        got[2 + iz, i] = current[i]
    for k in range(1, nz):
        z = lax.rem(iz + k, nz)
        arrived(got.at[2 + z], ss.at[2], rs.at[2 + z], (z, iy, ix, ic))
    current = tuple(got[2, i] for i in range(3))
    for z in range(1, nz):
        current = merge(current, tuple(got[2 + z, i] for i in range(3)))
    lse = current[0] + jnp.log(current[1])
    logp = current[2] - lse
    lse_out[...] = lse
    held[3, 0] = logp
    last = 2 + nz
    copies.append(send(held.at[3, 0], got.at[last, 0], ss.at[last], rs.at[last], other_core()))
    arrived(got.at[last, 0], ss.at[last], rs.at[last], other_core())
    theirs = got[last, 0]
    own = jnp.where(ic == 0, logp, theirs)
    pair = jnp.where(ic == 0, theirs, logp)

    def means(values, ref):
        terms = (values - ref) * scored[...]
        return [
            jnp.sum(terms * hot[s], axis=1, keepdims=True) / lens[:, s : s + 1] for s in range(seqs)
        ]

    own_means, pair_means = means(own, refs[0]), means(pair, refs[1])
    kl = jnp.sum(sum(pair_means), axis=0, keepdims=True) / seq_total
    loss = jnp.zeros((1, 1), F32)
    slopes = []
    for s in range(seqs):
        sign = 2.0 * wanted[:, s : s + 1] - 1.0
        sigmoid = jax.nn.sigmoid(kto_beta * sign * (own_means[s] - kl))
        slopes.append(-kto_beta * sign * sigmoid * (1.0 - sigmoid))
        loss = loss + jnp.sum(1.0 - sigmoid, axis=0, keepdims=True)
    shared = -jnp.sum(sum(slopes), axis=0, keepdims=True) / seq_total
    total = jnp.zeros_like(logp)
    for s in range(seqs):
        value = jnp.where(ic == 0, slopes[s], shared) / lens[:, s : s + 1]
        total = total + hot[s] * value
    coef[...] = total * scored[...]
    scalars[0] = jnp.broadcast_to(loss, scalars.shape[1:])
    scalars[1] = jnp.broadcast_to(kl, scalars.shape[1:])
    for copy in copies:
        copy.wait_send()


def objective(nz, seq_total, stats, hot, scored, refs, lens, wanted):
    shape = scored.shape
    dma = pltpu.SemaphoreType.DMA
    return pl.pallas_call(
        functools.partial(objective_kernel, nz, hot.shape[0], seq_total),
        out_shape=[
            jax.ShapeDtypeStruct(shape, F32),
            jax.ShapeDtypeStruct(shape, F32),
            jax.ShapeDtypeStruct((2, 8, 128), F32),
        ],
        in_specs=[vmem()] * 6,
        out_specs=[vmem()] * 3,
        scratch_shapes=[
            pltpu.VMEM((4, 3) + shape, F32),
            pltpu.VMEM((3 + nz, 3) + shape, F32),
            dma((3 + nz,)),
            dma((3 + nz,)),
        ],
        compiler_params=comm(4),
    )(stats, hot, scored, refs, lens, wanted)


def diagonal(nz):
    iz, iy, ix, ic = here()
    return [(lax.rem(iz + k, nz), 1 - iy, ix, 1 - ic) for k in range(nz)]


def to_head(nz, k, pairs, local_sem, out_sem, in_sem):
    iz, iy, ix, ic = here()
    z = lax.rem(iz + k, nz)
    device = (z, ic, ix, iy)

    def remote():
        for i, (source, target) in enumerate(pairs):
            send(source, target, out_sem.at[i, z], in_sem.at[i, iz], device)

    if k:
        remote()
        return
    pl.when(iy != ic)(remote)

    @pl.when(iy == ic)
    def _():
        for i, (source, target) in enumerate(pairs):
            copy = pltpu.make_async_copy(source, target, local_sem.at[i])
            copy.start()
            copy.wait()


def from_head(nz, k, targets, out_sem, in_sem):
    iz, iy, ix, ic = here()
    z = lax.rem(iz + k, nz)

    def wait():
        for i, target in enumerate(targets):
            arrived(target, out_sem.at[i, z], in_sem.at[i, z], (z, ic, ix, iy))

    if k:
        wait()
    else:
        pl.when(iy != ic)(wait)


def sent_head(nz, k, sources, out_sem, in_sem):
    iz, iy, ix, ic = here()
    z = lax.rem(iz + k, nz)

    def wait():
        for i, source in enumerate(sources):
            pltpu.make_async_remote_copy(
                src_ref=source,
                dst_ref=source,
                send_sem=out_sem.at[i, z],
                recv_sem=in_sem.at[i, z],
                device_id=(z, ic, ix, iy),
                device_id_type=pl.DeviceIdType.MESH,
            ).wait_send()

    if k:
        wait()
    else:
        pl.when(iy != ic)(wait)


def lanes(index, size):
    return pl.ds(pl.multiple_of(index * size, size), size)


def front_kernel(
    nz,
    half,
    residual,
    info,
    bias,
    joined_in,
    dense_in,
    natural,
    info_out,
    bias_out,
    joined_out,
    dense_out,
    fs,
    fr,
    js,
    jr,
    jl,
    cs,
    cr,
    ms,
    mr,
    zs,
    zr,
    ps,
    *refs,
):
    iz, iy, ix, ic = here()
    core = other_core()
    greet(neighbours(nz) + [core] + diagonal(nz))
    depth = joined_in.shape[0]
    cols = joined_out.shape[1]
    heads = dense_out.shape[0]
    copies = []

    def rows_of(h, z, y, x, c):
        return natural.at[z, y, x, c, pl.ds(h * half, half)]

    def forward(h, source, z, y, x):
        copies.append(send(source, rows_of(h, z, y, x, ic), fs.at[h, z, y, x], fr.at[h, z, y, x], core))

    class Rows(Gather):
        def block(self, h, z, y, x):
            return rows_of(h, z, y, x, ic)

    gather = Rows(nz, half, natural, refs, forward)
    first = pl.multiple_of((ix * 2 + ic) * 2 * half, 2 * half)
    for h in (0, 1):
        gather.start(h, residual.at[pl.ds(first + h * half, half)])

    copies.append(send(bias, bias_out, ms.at[0], mr.at[0], core))
    info_out[iz, iy] = info[...]
    across_y = (iz, 1 - iy, ix, ic)
    for k in range(1, nz):
        far = (lax.rem(iz + k, nz), iy, ix, ic)
        copies.append(send(info, info_out.at[iz, iy], zs.at[k], zr.at[iz, iy], far))
    copies.append(send(info, info_out.at[iz, iy], ps.at[iz], zr.at[iz, iy], across_y))

    mine = iz * 2 + iy
    for k in list(range(1, nz)) + [0]:
        z = lax.rem(iz + k, nz)
        to_head(
            nz,
            k,
            [
                (joined_in.at[:, lanes(z, cols)], joined_out.at[lanes(mine, depth)]),
                (dense_in.at[lanes(z, heads)], dense_out.at[:, lanes(mine, depth)]),
            ],
            jl,
            js,
            jr,
        )

    for k in range(1, nz):
        z = lax.rem(iz + k, nz)
        arrived(info_out.at[z, iy], zs.at[k], zr.at[z, iy], across_y)
        copies.append(send(info_out.at[z, iy], info_out.at[z, iy], ps.at[z], zr.at[z, iy], across_y))

    gather.rest()

    def head_parts(z, side):
        d = z * 2 + side
        return joined_out.at[lanes(d, depth)], dense_out.at[:, lanes(d, depth)]

    for k in [0] + list(range(1, nz)):
        z = lax.rem(iz + k, nz)
        parts = head_parts(z, ic)
        from_head(nz, k, parts, js, jr)
        for i, part in enumerate(parts):
            copies.append(send(part, part, cs.at[i, z], cr.at[i, z], core))
    for k in range(nz):
        z = lax.rem(iz + k, nz)
        arrived(info_out.at[z, 1 - iy], ps.at[z], zr.at[z, 1 - iy], across_y)
    for z in range(nz):
        for y in (0, 1):
            for x in (0, 1):
                for h in (0, 1):
                    arrived(rows_of(h, z, y, x, 1 - ic), fs.at[h, z, y, x], fr.at[h, z, y, x], core)
    for z in range(nz):
        for i, part in enumerate(head_parts(z, 1 - ic)):
            arrived(part, cs.at[i, z], cr.at[i, z], core)
    arrived(bias_out, ms.at[0], mr.at[0], core)
    gather.end()
    for k in range(nz):
        z = lax.rem(iz + k, nz)
        sent_head(nz, k, [joined_in.at[:, lanes(z, cols)], dense_in.at[lanes(z, heads)]], js, jr)
    for copy in copies:
        copy.wait_send()


def front(nz, residual, info, bias, joined_in, dense_in):
    held, width = residual.shape
    half = held // 8
    depth, cols = joined_in.shape[0], joined_in.shape[1] // nz
    heads = dense_in.shape[0] // nz
    dma = pltpu.SemaphoreType.DMA
    outs = pl.pallas_call(
        functools.partial(front_kernel, nz, half),
        out_shape=[
            jax.ShapeDtypeStruct((nz, 2, 2, 2, 2 * half, width), BF16),
            jax.ShapeDtypeStruct((nz, 2) + info.shape, F32),
            jax.ShapeDtypeStruct(bias.shape, F32),
            jax.ShapeDtypeStruct((2 * nz * depth, cols), BF16),
            jax.ShapeDtypeStruct((heads, 2 * nz * depth), BF16),
        ],
        in_specs=[anywhere(), vmem(), vmem(), anywhere(), anywhere()],
        out_specs=[anywhere(), vmem(), vmem(), anywhere(), anywhere()],
        scratch_shapes=[
            dma((2, nz, 2, 2)),
            dma((2, nz, 2, 2)),
            dma((2, nz)),
            dma((2, nz)),
            dma((2,)),
            dma((2, nz)),
            dma((2, nz)),
            dma((1,)),
            dma((1,)),
            dma((nz,)),
            dma((nz, 2)),
            dma((nz,)),
        ]
        + Gather.scratch(nz),
        compiler_params=comm(1, 16),
    )(residual, info, bias, joined_in, dense_in)
    natural = outs[0].reshape(8 * nz * 2 * half, width)
    return natural, outs[1].reshape((2 * nz,) + info.shape), outs[2], outs[3], outs[4]


def end_kernel(
    nz,
    half,
    part,
    mine_rows,
    other_rows,
    rows,
    vectors,
    keep,
    give,
    joined_in,
    dense_in,
    rows_out,
    vectors_out,
    bias_out,
    joined_out,
    dense_out,
    merged,
    came,
    rows_in,
    vector_in,
    vector_sum,
    give_in,
    joined_came,
    joined_sum,
    dense_came,
    dense_sum,
    ms,
    mr,
    vs,
    vr,
    bs,
    br,
    bp,
    js,
    jr,
    jl,
    cs,
    cr,
    os,
    orr,
    *refs,
):
    iz, iy, ix, ic = here()
    core = other_core()
    across_x, across_y = (iz, iy, 1 - ix, ic), (iz, 1 - iy, ix, ic)
    greet(neighbours(nz) + [core] + diagonal(nz))
    reduce = Reduce(nz, half, merged, refs)
    copies = []
    depth = joined_in.shape[0] // (2 * nz)
    cols = joined_in.shape[1]
    heads = dense_in.shape[0]
    groups = [(1 - iy, 1 - ix), (iy, 1 - ix), (1 - iy, ix), (iy, ix)]

    for y, x in groups:
        for k in list(range(1, nz)) + [0]:
            z = lax.rem(iz + k, nz)
            copies.append(
                send(part.at[z, y, x, 1 - ic], came.at[z, y, x], ms.at[z, y, x], mr.at[z, y, x], core)
            )
    copies.append(send(vectors, vector_in.at[0], vs.at[0], vr.at[0], core))
    copies.append(send(give, give_in, bs.at[0], br.at[nz, 0], core))
    copies.append(send(other_rows, rows_in, os.at[0], orr.at[0], core))
    for k in range(nz):
        z = lax.rem(iz + k, nz)
        theirs = z * 2 + 1 - ic
        copies.append(
            send(joined_in.at[lanes(theirs, depth)], joined_came.at[z], cs.at[0, z], cr.at[0, z], core)
        )
        copies.append(
            send(dense_in.at[:, lanes(theirs, depth)], dense_came.at[z], cs.at[1, z], cr.at[1, z], core)
        )

    def merge_group(y, x):
        for k in list(range(1, nz)) + [0]:
            z = lax.rem(iz + k, nz)
            arrived(came.at[z, y, x], ms.at[z, y, x], mr.at[z, y, x], core)
            merged[z, y, x] = (part[z, y, x, ic].astype(F32) + came[z, y, x].astype(F32)).astype(BF16)

    merge_group(*groups[0])
    reduce.start(0, True)
    merge_group(*groups[1])
    reduce.start(0, False)
    merge_group(*groups[2])
    reduce.start(1, True)
    reduce.start(1, False)
    merge_group(*groups[3])

    arrived(vector_in.at[0], vs.at[0], vr.at[0], core)
    vector_sum[0] = vectors[...] + vector_in[0]
    copies.append(send(vector_sum.at[0], vector_in.at[1], vs.at[1], vr.at[1], across_x))
    arrived(give_in, bs.at[0], br.at[nz, 0], core)
    bias_out[iz, iy] = keep[...] + give_in[...]
    for k in range(1, nz):
        far = (lax.rem(iz + k, nz), iy, ix, ic)
        copies.append(send(bias_out.at[iz, iy], bias_out.at[iz, iy], bs.at[k], br.at[iz, iy], far))
    copies.append(send(bias_out.at[iz, iy], bias_out.at[iz, iy], bp.at[iz], br.at[iz, iy], across_y))

    for k in list(range(1, nz)) + [0]:
        z = lax.rem(iz + k, nz)
        ours = z * 2 + ic
        arrived(joined_came.at[z], cs.at[0, z], cr.at[0, z], core)
        joined_sum[z] = (joined_in[lanes(ours, depth)].astype(F32) + joined_came[z].astype(F32)).astype(BF16)
        arrived(dense_came.at[z], cs.at[1, z], cr.at[1, z], core)
        dense_sum[z] = (dense_in[:, lanes(ours, depth)].astype(F32) + dense_came[z].astype(F32)).astype(BF16)
        to_head(
            nz,
            k,
            [
                (joined_sum.at[z], joined_out.at[:, lanes(iz, cols)]),
                (dense_sum.at[z], dense_out.at[lanes(iz, heads)]),
            ],
            jl,
            js,
            jr,
        )

    for h in (0, 1):
        reduce.second(h)
    arrived(vector_in.at[1], vs.at[1], vr.at[1], across_x)
    vector_sum[1] = vector_sum[0] + vector_in[1]
    copies.append(send(vector_sum.at[1], vector_in.at[2], vs.at[2], vr.at[2], across_y))
    for k in range(1, nz):
        z = lax.rem(iz + k, nz)
        arrived(bias_out.at[z, iy], bs.at[k], br.at[z, iy], across_y)
        copies.append(send(bias_out.at[z, iy], bias_out.at[z, iy], bp.at[z], br.at[z, iy], across_y))
    kept = [reduce.third(h) for h in (0, 1)]
    arrived(vector_in.at[2], vs.at[2], vr.at[2], across_y)
    vector_sum[2] = vector_sum[1] + vector_in[2]
    for k in range(1, nz):
        far = (lax.rem(iz + k, nz), iy, ix, ic)
        copies.append(send(vector_sum.at[2], vector_in.at[3 + iz], vs.at[2 + k], vr.at[3 + iz], far))
    vector_in[3 + iz] = vector_sum[2]
    arrived(rows_in, os.at[0], orr.at[0], core)
    for h in (0, 1):
        at = pl.ds(h * half, half)
        hat, inverse = normed(rows[at].astype(F32))
        back = norm_back(reduce.finish(h, kept[h]), hat, inverse)
        block = rows_out.at[ix, ic, at]
        rows_out[ix, ic, at] = (
            mine_rows[at].astype(F32) + rows_in[at].astype(F32) + back
        ).astype(BF16)
        copies.append(send(block, block, os.at[1 + h], orr.at[1 + h], across_x))
        copies.append(send(block, block, os.at[3 + h], orr.at[3 + h], core))
    for h in (0, 1):
        block = rows_out.at[1 - ix, ic, pl.ds(h * half, half)]
        arrived(block, os.at[1 + h], orr.at[1 + h], across_x)
        copies.append(send(block, block, os.at[5 + h], orr.at[5 + h], core))
    for k in range(1, nz):
        z = lax.rem(iz + k, nz)
        arrived(vector_in.at[3 + z], vs.at[2 + k], vr.at[3 + z], (z, iy, ix, ic))
    total = vector_in[3]
    for z in range(1, nz):
        total = total + vector_in[3 + z]
    vectors_out[...] = total
    for k in range(nz):
        z = lax.rem(iz + k, nz)
        arrived(bias_out.at[z, 1 - iy], bp.at[z], br.at[z, 1 - iy], across_y)
        from_head(
            nz, k, [joined_out.at[:, lanes(z, cols)], dense_out.at[lanes(z, heads)]], js, jr
        )
        sent_head(nz, k, [joined_sum.at[z], dense_sum.at[z]], js, jr)
    for h in (0, 1):
        at = pl.ds(h * half, half)
        arrived(rows_out.at[ix, 1 - ic, at], os.at[3 + h], orr.at[3 + h], core)
        arrived(rows_out.at[1 - ix, 1 - ic, at], os.at[5 + h], orr.at[5 + h], core)
    for copy in copies + reduce.copies:
        copy.wait_send()


def end(nz, part, mine_rows, other_rows, rows, vectors, keep, give, joined_in, dense_in):
    share, width = rows.shape
    half = share // 2
    depth, cols, heads = joined_in.shape[0] // (2 * nz), joined_in.shape[1], dense_in.shape[0]
    dma = pltpu.SemaphoreType.DMA
    return pl.pallas_call(
        functools.partial(end_kernel, nz, half),
        out_shape=[
            jax.ShapeDtypeStruct((2, 2, share, width), BF16),
            jax.ShapeDtypeStruct(vectors.shape, F32),
            jax.ShapeDtypeStruct((nz, 2) + keep.shape, F32),
            jax.ShapeDtypeStruct((depth, nz * cols), BF16),
            jax.ShapeDtypeStruct((nz * heads, depth), BF16),
        ],
        in_specs=[vmem()] * 9,
        out_specs=[vmem(), vmem(), vmem(), vmem(), vmem()],
        scratch_shapes=[
            pltpu.VMEM((nz, 2, 2, share, width), BF16),
            pltpu.VMEM((nz, 2, 2, share, width), BF16),
            pltpu.VMEM((share, width), BF16),
            pltpu.VMEM((3 + nz,) + vectors.shape, F32),
            pltpu.VMEM((3,) + vectors.shape, F32),
            pltpu.VMEM(keep.shape, F32),
            pltpu.VMEM((nz, depth, cols), BF16),
            pltpu.VMEM((nz, depth, cols), BF16),
            pltpu.VMEM((nz, heads, depth), BF16),
            pltpu.VMEM((nz, heads, depth), BF16),
            dma((nz, 2, 2)),
            dma((nz, 2, 2)),
            dma((2 + nz,)),
            dma((3 + nz,)),
            dma((nz,)),
            dma((nz + 1, 2)),
            dma((nz,)),
            dma((2, nz)),
            dma((2, nz)),
            dma((2,)),
            dma((2, nz)),
            dma((2, nz)),
            dma((7,)),
            dma((7,)),
        ]
        + Reduce.scratch(nz, half, width),
        compiler_params=comm(5),
    )(part, mine_rows, other_rows, rows, vectors, keep, give, joined_in, dense_in)


def fast_shards(
    residual,
    lengths,
    pair_order,
    token_ids,
    desirable,
    ref_match,
    ref_pair,
    attn_gain,
    attn_shift,
    mlp_gain,
    mlp_shift,
    w_joined,
    b_joined,
    w_dense,
    b_dense,
    w_up,
    b_up,
    w_down,
    b_down,
    final_gain,
    final_shift,
    w_vocab,
):
    nz, ny, nx = lax.axis_size("z"), lax.axis_size("y"), lax.axis_size("x")
    n = nz * ny
    chips = n * nx
    iz, iy, ix, ic = (lax.axis_index(a) for a in ALL)
    dp = iz * ny + iy
    held, width = residual.shape
    total = n * held
    blocks = 2 * n
    piece = held // 2
    seqs = lengths.shape[1]
    depth = width // n
    vcols = w_vocab.shape[1] // n
    ffs = w_up.shape[1] // n
    hcols = 3 * HD
    mine = ix * 2 + ic

    info = jnp.stack(
        [
            token_ids.astype(F32),
            ref_match,
            ref_pair,
            jnp.concatenate(
                [lengths[0].astype(F32), desirable.astype(F32), jnp.zeros((held - 2 * seqs,), F32)]
            ),
        ]
    )
    bias_own = jnp.concatenate([b_joined, b_up]).astype(F32)
    natural, info, bias_other, wj, wd = front(nz, residual, info, bias_own.reshape(-1, HD), w_joined, w_dense)
    bias_other = bias_other.reshape(-1)

    send_up = w_up.reshape(depth, n, ffs).transpose(1, 0, 2)
    send_down = w_down.reshape(n, ffs, depth)
    send_vocab = w_vocab.reshape(depth, n, vcols).transpose(1, 0, 2)
    up_own = exchange(send_up).reshape(width, ffs)
    down_own = exchange(send_down).transpose(1, 0, 2).reshape(ffs, width)
    vocab_own = exchange(send_vocab).reshape(width, vcols)
    up_other, down_other, vocab_other = swap(up_own), swap(down_own), swap(vocab_own)
    wup = jnp.concatenate([up_own, up_other], axis=1)
    wout = jnp.concatenate([wd, down_own, down_other], axis=0)
    bias_first = jnp.where(ic == 0, bias_own, bias_other)
    bias_second = jnp.where(ic == 0, bias_other, bias_own)
    bj_all = jnp.where(iy == 0, bias_first, bias_second)[: nz * hcols].reshape(nz, hcols)
    bj = lax.dynamic_index_in_dim(bj_all, iz, 0, keepdims=False)
    bu_all = jnp.stack([bias_own[nz * hcols :], bias_other[nz * hcols :]]).reshape(2, n, ffs)
    bu = lax.dynamic_index_in_dim(bu_all, dp, 1, keepdims=False).reshape(2 * ffs)

    ids = info[:, 0].astype(jnp.int32)
    refs = jnp.stack([info[:, 1], info[:, 2]])
    lens = info[:, 3, :seqs].astype(jnp.int32)
    wanted = info[:, 3, seqs : 2 * seqs]
    slots = jnp.arange(blocks, dtype=jnp.int32)
    anchor = jnp.sum(
        jnp.where(pair_order[None, :] == slots[:, None], slots[None, :], 0), axis=1
    )
    order = jnp.where(ic == 0, slots, anchor)
    back = jnp.where(ic == 0, slots, pair_order)
    rows_low = take_blocks(natural, order, piece)
    anchor_hot = (anchor[:, None] == slots[None, :])[:, :, None]
    pair_ids = jnp.sum(jnp.where(anchor_hot, ids.reshape(1, blocks, piece), 0), axis=1).reshape(n, held)
    all_ids = jnp.stack([ids, pair_ids])

    ends = jnp.stack([jnp.sum(lens[:, : s + 1], axis=1) for s in range(seqs)], axis=1)
    starts = ends - lens
    places = jnp.arange(held, dtype=jnp.int32)
    segment = jnp.sum((places[None, :, None] >= ends[:, None, :]).astype(jnp.int32), axis=2)
    hot = (segment[:, :, None] == jnp.arange(seqs, dtype=jnp.int32)).astype(F32)
    position = places[None, :] - jnp.sum(hot * starts[:, None, :].astype(F32), axis=2).astype(jnp.int32)
    allowed = (segment[:, :, None] == segment[:, None, :]) & (places[None, :, None] >= places[None, None, :])
    scored = jnp.concatenate(
        [segment[:, 1:] == segment[:, :-1], jnp.zeros((n, 1), jnp.bool_)], axis=1
    ).astype(F32)
    targets = jnp.concatenate([all_ids[:, :, 1:], jnp.zeros((2, n, 1), jnp.int32)], axis=2)

    rows_float = rows_low.astype(F32)
    hat, inverse = normed(rows_float)
    ga, sa, gm, sm, gf, sf = (
        v.astype(F32) for v in (attn_gain, attn_shift, mlp_gain, mlp_shift, final_gain, final_shift)
    )
    attn_low = (hat * ga + sa).astype(BF16)
    mlp_low = (hat * gm + sm).astype(BF16)
    frequency = jnp.exp(jnp.arange(ROT // 2, dtype=F32) * (-2.0 * math.log(10000.0) / ROT))
    angles = position.reshape(total)[:, None].astype(F32) * frequency[None, :]
    cosine, sine = jnp.cos(angles), jnp.sin(angles)
    fused = dot(attn_low, wj, (1, 0)) + bj
    query = turn(fused[:, :HD], cosine, sine).astype(BF16)
    keys = turn(fused[:, HD : 2 * HD], cosine, sine).astype(BF16)
    values = fused[:, 2 * HD :].astype(BF16)
    q3, k3, v3 = (a.reshape(n, held, HD) for a in (query, keys, values))
    scores = jnp.einsum("grd,gcd->grc", q3, k3, preferred_element_type=F32) / math.sqrt(HD)
    scores = jnp.where(allowed, scores, masked_score)
    highest = jnp.max(scores, axis=-1, keepdims=True)
    weights = jnp.exp(scores - highest)
    probs = weights / jnp.sum(weights, axis=-1, keepdims=True)
    probs_low = probs.astype(BF16)
    mixed = (
        jnp.einsum("grc,gcd->grd", probs_low, v3, preferred_element_type=F32)
        .astype(BF16)
        .reshape(total, HD)
    )
    hidden = dot(mlp_low, wup, (1, 0)) + bu
    bell = 0.5 * (1.0 + lax.erf(hidden * math.sqrt(0.5)))
    active = (hidden * bell).astype(BF16)
    outs_low = jnp.concatenate([mixed, active], axis=1)
    branch_part = dot(outs_low, wout, (1, 0)).astype(BF16)
    share = total // chips
    chip = dp * nx + ix
    rows_here = lax.dynamic_slice_in_dim(rows_low, chip * share, share, 0)
    bias_out = (b_dense.astype(F32) + b_down.astype(F32))[None]
    final, resid = reduce_norm_gather(nz, branch_part, rows_here, bias_out, gf[None], sf[None])

    my_targets = jnp.where(ic == 0, targets[0], targets[1]).reshape(total)
    logits = [dot(final, w, (1, 0)) for w in (vocab_own, vocab_other)]
    hits = [
        lax.broadcasted_iota(jnp.int32, (total, vcols), 1)
        == (my_targets - ((ix * 2 + core) * n + dp) * vcols)[:, None]
        for core in (ic, 1 - ic)
    ]
    tops = [jnp.max(part, axis=1) for part in logits]
    top = jnp.maximum(tops[0], tops[1])
    sums = sum(jnp.sum(jnp.exp(part - top[:, None]), axis=1) for part in logits)
    picks = sum(jnp.sum(jnp.where(h, part, 0.0), axis=1) for h, part in zip(hits, logits))
    stats = jnp.stack([top, sums, picks]).reshape(3, n, held)
    coef, my_lse, scalars = objective(
        nz, n * seqs, stats, hot.transpose(2, 0, 1), scored, refs, lens.astype(F32), wanted
    )
    coef, my_lse = coef.reshape(total), my_lse.reshape(total)
    kto_loss, kl_estimate = scalars[0, 0, 0], scalars[1, 0, 0]

    dlogits = [
        (coef[:, None] * (jnp.where(h, 1.0, 0.0) - jnp.exp(part - my_lse[:, None]))).astype(BF16)
        for h, part in zip(hits, logits)
    ]
    gv_own = dot(final, dlogits[0], (0, 0))
    gv_other = dot(final, dlogits[1], (0, 0)).astype(BF16)
    dfinal_part = (dot(dlogits[0], vocab_own, (1, 1)) + dot(dlogits[1], vocab_other, (1, 1))).astype(BF16)
    dbranch, final_vectors = reduce_back_gather(nz, dfinal_part, resid, gf[None])
    gv = (gv_own + swap(gv_other).astype(F32)).astype(BF16)
    grad_vocab = (
        exchange(gv.reshape(n, depth, vcols)).transpose(1, 0, 2).reshape(depth, n * vcols).astype(F32)
    )

    gout = dot(outs_low, dbranch, (0, 0))
    douts = dot(dbranch, wout, (1, 1))
    dmixed = douts[:, :HD].astype(BF16).reshape(n, held, HD)
    slope_of = bell + hidden * jnp.exp(-0.5 * hidden * hidden) * (1.0 / math.sqrt(2.0 * math.pi))
    dhidden = (douts[:, HD:] * slope_of).astype(BF16)
    dvalues = jnp.einsum("grc,grd->gcd", probs_low, dmixed, preferred_element_type=F32)
    dprobs = jnp.einsum("grd,gcd->grc", dmixed, v3, preferred_element_type=F32)
    dscores = (probs * (dprobs - jnp.sum(probs * dprobs, axis=-1, keepdims=True))).astype(BF16)
    dquery = jnp.einsum("grc,gcd->grd", dscores, k3, preferred_element_type=F32) / math.sqrt(HD)
    dkeys = jnp.einsum("grc,grd->gcd", dscores, q3, preferred_element_type=F32) / math.sqrt(HD)
    dfused = jnp.concatenate(
        [
            turn(dquery.reshape(total, HD), cosine, -sine),
            turn(dkeys.reshape(total, HD), cosine, -sine),
            dvalues.reshape(total, HD),
        ],
        axis=1,
    ).astype(BF16)
    gj = dot(attn_low, dfused, (0, 0)).astype(BF16)
    gu = dot(mlp_low, dhidden, (0, 0))
    dattn = dot(dfused, wj, (1, 1))
    dmlp = dot(dhidden, wup, (1, 1))
    g_attn_gain = jnp.sum(dattn * hat, axis=0)
    g_attn_shift = jnp.sum(dattn, axis=0)
    g_mlp_gain = jnp.sum(dmlp * hat, axis=0)
    g_mlp_shift = jnp.sum(dmlp, axis=0)
    t_part = (dattn * ga + dmlp * gm).astype(BF16)
    t_part = take_blocks(t_part, back, piece)

    gout_low = gout.astype(BF16)
    gu_low = gu.astype(BF16)
    gdown = gout[HD : HD + ffs] + swap(gout_low[HD + ffs :]).astype(F32)
    gup = gu[:, :ffs] + swap(gu_low[:, ffs:]).astype(F32)
    grad_down = exchange(
        gdown.astype(BF16).reshape(ffs, n, depth).transpose(1, 0, 2)
    ).reshape(n * ffs, depth).astype(F32)
    grad_up = (
        exchange(gup.astype(BF16).reshape(n, depth, ffs)).transpose(1, 0, 2).reshape(depth, n * ffs).astype(F32)
    )

    share2 = total // (2 * chips)

    def natural_rows(core):
        first = dp * held + (ix * 2 + core) * share2
        place = jnp.sum(jnp.where(slots == first // piece, back, 0)) * piece + first % piece
        return lax.dynamic_slice_in_dim(dbranch, place, share2, 0)

    gbj = jnp.sum(dfused.astype(F32), axis=0)
    gbu = jnp.sum(dhidden.astype(F32), axis=0)
    spare = jnp.zeros((8 * HD - hcols - ffs,), F32)
    keep = jnp.concatenate([gbj, gbu[:ffs], spare]).reshape(8, HD)
    give = jnp.concatenate([gbj, gbu[ffs:], spare]).reshape(8, HD)
    vectors = jnp.concatenate(
        [
            jnp.stack([g_attn_gain, g_attn_shift, g_mlp_gain, g_mlp_shift]),
            final_vectors,
            jnp.zeros((1, width), F32),
        ]
    )
    rows_out, vectors, biases, grad_joined, grad_dense = end(
        nz,
        t_part.reshape(nz, 2, 2, 2, share2, width),
        natural_rows(ic),
        natural_rows(1 - ic),
        lax.dynamic_slice_in_dim(residual, mine * share2, share2, 0),
        vectors,
        keep,
        give,
        gj,
        gout_low[:HD],
    )
    grad_input = rows_out.reshape(held, width).astype(F32)
    grad_joined, grad_dense = grad_joined.astype(F32), grad_dense.astype(F32)
    g_attn_gain, g_attn_shift, g_mlp_gain, g_mlp_shift, g_final_gain, g_final_shift, g_out = vectors[:7]
    biases = biases.reshape(nz, 2, 8 * HD)
    gb_joined = jnp.where(ic == 0, biases[:, 0, :hcols], biases[:, 1, :hcols]).reshape(nz * hcols)
    gb_up = biases[:, :, hcols : hcols + ffs].reshape(n * ffs)
    return (
        kto_loss,
        kl_estimate,
        grad_input,
        g_attn_gain,
        g_attn_shift,
        g_mlp_gain,
        g_mlp_shift,
        grad_joined,
        gb_joined,
        grad_dense,
        g_out,
        grad_up,
        gb_up,
        grad_down,
        g_out,
        g_final_gain,
        g_final_shift,
        grad_vocab,
    )


def placed(dp, mp):
    ins = (
        P(dp, None),
        P(dp, None),
        P(),
        P(dp),
        P(dp),
        P(dp),
        P(dp),
        P(),
        P(),
        P(),
        P(),
        P(dp, mp),
        P(mp),
        P(mp, dp),
        P(),
        P(dp, mp),
        P(mp),
        P(mp, dp),
        P(),
        P(),
        P(),
        P(dp, mp),
    )
    outs = (
        P(),
        P(),
        P(dp, None),
        P(),
        P(),
        P(),
        P(),
        P(dp, mp),
        P(mp),
        P(mp, dp),
        P(),
        P(dp, mp),
        P(mp),
        P(mp, dp),
        P(),
        P(),
        P(),
        P(dp, mp),
    )
    return ins, outs


def solution(mesh):
    n_dp, n_mp = mesh.shape["dp"], mesh.shape["mp"]
    if n_dp == 8 and n_mp == 4:
        fine = jax.sharding.Mesh(mesh.devices.reshape(n_dp // 2, 2, n_mp // 2, 2), ALL)
        ins, outs = placed(DP, ("x", "c"))
        return jax.shard_map(fast_shards, mesh=fine, in_specs=ins, out_specs=outs, check_vma=False)
    ins, outs = placed("dp", "mp")
    return jax.shard_map(shards, mesh=mesh, in_specs=ins, out_specs=outs, check_vma=False)
```

```python
import functools
import math

import jax
import jax.numpy as jnp
from jax import lax
from jax.experimental import pallas as pl
from jax.experimental.pallas import tpu as pltpu
from jax.sharding import PartitionSpec as P

HD = 128
ROT = 32


kto_beta = 4.0
norm_eps = 1e-05
masked_score = -1e30


def joined(value, axis, join):
    pieces = jax.tree.map(lambda part: lax.all_gather(part, axis), value)
    head = jax.tree.map(lambda part: part[0], pieces)
    tail = jax.tree.map(lambda part: part[1:], pieces)
    subtotal, _ = lax.scan(lambda subtotal, piece: (join(subtotal, piece), None), head, tail)
    return subtotal


def layer_norm(values, norm_gain, norm_shift):
    centred = values - jnp.mean(values, axis=-1, keepdims=True)
    spread = jnp.mean(centred * centred, axis=-1, keepdims=True)
    return centred * lax.rsqrt(spread + norm_eps) * norm_gain + norm_shift


def rotate(values, position):
    half_rot = ROT // 2
    inverse = jnp.exp(jnp.arange(half_rot, dtype=jnp.float32) * (-2.0 * math.log(10000.0) / ROT))
    angles = position.astype(jnp.float32)[:, None] * inverse[None, :]
    cosine_table = jnp.cos(angles)[:, None, :]
    sine_table = jnp.sin(angles)[:, None, :]
    first_half = values[..., :half_rot]
    second_half = values[..., half_rot:ROT]
    return jnp.concatenate(
        [
            first_half * cosine_table - second_half * sine_table,
            second_half * cosine_table + first_half * sine_table,
            values[..., ROT:],
        ],
        axis=-1,
    )


def gelu_exact(values):
    return jax.nn.gelu(values, approximate=False)


def attention_scores(query_low, keys_low, allowed):
    raw_scores = jnp.einsum(
        "rhd,chd->hrc", query_low, keys_low, preferred_element_type=jnp.float32
    ) / math.sqrt(HD)
    return jnp.where(allowed[None], raw_scores, masked_score)


def combine_vocab(first, second):
    high_first, total_first, pick_first = first
    high_second, total_second, pick_second = second
    highest = jnp.maximum(high_first, high_second)
    merged_total = total_first * jnp.exp(high_first - highest) + total_second * jnp.exp(
        high_second - highest
    )
    return (highest, merged_total, pick_first + pick_second)


def gather_weights(weights_low):
    w_joined, w_up, w_vocab, w_dense, w_down = weights_low
    joined_all, up_all, vocab_all = (
        lax.all_gather(w_joined, "dp", axis=0, tiled=True),
        lax.all_gather(w_up, "dp", axis=0, tiled=True),
        lax.all_gather(w_vocab, "dp", axis=0, tiled=True),
    )
    dense_all, down_all = (
        lax.all_gather(w_dense, "dp", axis=1, tiled=True),
        lax.all_gather(w_down, "dp", axis=1, tiled=True),
    )
    return (joined_all, up_all, vocab_all, dense_all, down_all)


def forward_pass(gathered, smalls, rows_low, allowed, position, targets):
    joined_all, up_all, vocab_all, dense_all, down_all = gathered
    (
        attn_gain,
        attn_shift,
        mlp_gain,
        mlp_shift,
        b_joined,
        b_dense,
        b_up,
        b_down,
        final_gain,
        final_shift,
    ) = smalls
    rows_float = rows_low.astype(jnp.float32)
    count_rows = rows_float.shape[0]
    attn_low = layer_norm(rows_float, attn_gain, attn_shift).astype(jnp.bfloat16)
    mlp_low = layer_norm(rows_float, mlp_gain, mlp_shift).astype(jnp.bfloat16)
    joined_cols = jnp.dot(attn_low, joined_all, preferred_element_type=jnp.float32) + b_joined
    joined_cols = joined_cols.reshape(count_rows, -1, 3, HD)
    query_low = rotate(joined_cols[:, :, 0], position).astype(jnp.bfloat16)
    keys_low = rotate(joined_cols[:, :, 1], position).astype(jnp.bfloat16)
    values_low = joined_cols[:, :, 2].astype(jnp.bfloat16)
    scores = attention_scores(query_low, keys_low, allowed)
    highest = jnp.max(scores, axis=-1, keepdims=True)
    scaled_exp = jnp.exp(scores - highest)
    totals = jnp.sum(scaled_exp, axis=-1, keepdims=True)
    probs_low = (scaled_exp / totals).astype(jnp.bfloat16)
    score_lse = highest + jnp.log(totals)
    mixed_low = (
        jnp.einsum("hrc,chd->rhd", probs_low, values_low, preferred_element_type=jnp.float32)
        .reshape(count_rows, -1)
        .astype(jnp.bfloat16)
    )
    hidden = jnp.dot(mlp_low, up_all, preferred_element_type=jnp.float32) + b_up
    active_low = gelu_exact(hidden).astype(jnp.bfloat16)
    branch_part = jnp.dot(mixed_low, dense_all, preferred_element_type=jnp.float32) + jnp.dot(
        active_low, down_all, preferred_element_type=jnp.float32
    )
    branch = lax.psum(branch_part, "mp")
    resid_sum = rows_float + branch + b_dense + b_down
    final_low = layer_norm(resid_sum, final_gain, final_shift).astype(jnp.bfloat16)
    logits = jnp.dot(final_low, vocab_all, preferred_element_type=jnp.float32)
    local_high = jnp.max(logits, axis=-1)
    local_total = jnp.sum(jnp.exp(logits - local_high[:, None]), axis=-1)
    column = targets - lax.axis_index("mp") * logits.shape[1]
    target_hit = lax.broadcasted_iota(jnp.int32, logits.shape, 1) == column[:, None]
    local_pick = jnp.sum(jnp.where(target_hit, logits, 0.0), axis=-1)
    high_all, total_all, picked = joined((local_high, local_total, local_pick), "mp", combine_vocab)
    vocab_lse = high_all + jnp.log(total_all)
    return (
        attn_low,
        mlp_low,
        joined_cols,
        query_low,
        keys_low,
        values_low,
        score_lse,
        mixed_low,
        hidden,
        active_low,
        resid_sum,
        final_low,
        logits,
        vocab_lse,
        target_hit,
        picked - vocab_lse,
    )


def shards(
    residual,
    lengths,
    pair_order,
    token_ids,
    desirable,
    ref_match,
    ref_pair,
    attn_gain,
    attn_shift,
    mlp_gain,
    mlp_shift,
    w_joined,
    b_joined,
    w_dense,
    b_dense,
    w_up,
    b_up,
    w_down,
    b_down,
    final_gain,
    final_shift,
    w_vocab,
):
    dp_count = lax.axis_size("dp")
    tokens_here = residual.shape[0]
    piece_rows = tokens_here // 2
    width = residual.shape[1]
    seq_here = lengths.shape[1]
    block_count = 2 * dp_count
    my_index = lax.axis_index("dp")
    block_slots = jnp.arange(block_count, dtype=jnp.int32)
    my_blocks = 2 * my_index + jnp.arange(2, dtype=jnp.int32)
    my_targets = jnp.sum(
        jnp.where(block_slots[None, :] == my_blocks[:, None], pair_order[None, :], 0), axis=1
    )
    send_hot = my_targets[:, None] == block_slots[None, :]
    own_blocks = residual.reshape(2, piece_rows, width)
    own_ids = token_ids.reshape(2, piece_rows)
    sent_rows = jnp.einsum(
        "ht,hpd->tpd", send_hot.astype(jnp.bfloat16), own_blocks, preferred_element_type=jnp.float32
    ).astype(jnp.bfloat16)
    sent_ids = jnp.sum(jnp.where(send_hot[:, :, None], own_ids[:, None, :], 0), axis=0)
    got_rows, got_ids = (
        lax.all_to_all(
            sent_rows.reshape(dp_count, 2, piece_rows, width),
            "dp",
            split_axis=0,
            concat_axis=0,
            tiled=True,
        ),
        lax.all_to_all(
            sent_ids.reshape(dp_count, 2, piece_rows), "dp", split_axis=0, concat_axis=0, tiled=True
        ),
    )
    paired_rows = jnp.sum(got_rows.astype(jnp.float32), axis=0).astype(jnp.bfloat16)
    paired_ids = jnp.sum(got_ids, axis=0)
    rows_low = jnp.concatenate([residual, paired_rows.reshape(tokens_here, width)], axis=0)
    ids_all = jnp.concatenate([token_ids, paired_ids.reshape(tokens_here)], axis=0)
    seq_lengths = lengths[0]
    seq_slots = jnp.arange(seq_here, dtype=jnp.int32)
    seq_ends = jnp.sum(
        jnp.where(seq_slots[None, :] <= seq_slots[:, None], seq_lengths[None, :], 0), axis=1
    )
    seq_starts = seq_ends - seq_lengths
    places = jnp.arange(tokens_here, dtype=jnp.int32)
    segment = jnp.sum((places[:, None] >= seq_ends[None, :]).astype(jnp.int32), axis=1)
    own_start = jnp.sum(
        jnp.where(segment[:, None] == seq_slots[None, :], seq_starts[None, :], 0), axis=1
    )
    position_half = places - own_start
    segment_all = jnp.concatenate([segment, segment + seq_here])
    position = jnp.concatenate([position_half, position_half])
    count_rows = 2 * tokens_here
    row_index = jnp.arange(count_rows, dtype=jnp.int32)
    allowed = (segment_all[:, None] == segment_all[None, :]) & (
        row_index[None, :] <= row_index[:, None]
    )
    targets = jnp.concatenate([ids_all[1:], jnp.zeros((1,), jnp.int32)])
    scored = jnp.concatenate(
        [segment_all[1:] == segment_all[:-1], jnp.zeros((1,), jnp.bool_)]
    ).astype(jnp.float32)
    ref_rows = jnp.concatenate([ref_match, ref_pair])
    length_float = seq_lengths.astype(jnp.float32)
    length_both = jnp.concatenate([length_float, length_float])
    seq_match = segment_all[:, None] == jnp.arange(2 * seq_here, dtype=jnp.int32)[None, :]
    smalls = tuple(
        (
            value.astype(jnp.float32)
            for value in (
                attn_gain,
                attn_shift,
                mlp_gain,
                mlp_shift,
                b_joined,
                b_dense,
                b_up,
                b_down,
                final_gain,
                final_shift,
            )
        )
    )
    weights_low = (w_joined, w_up, w_vocab, w_dense, w_down)
    gathered = gather_weights(weights_low)
    first_pass = forward_pass(gathered, smalls, rows_low, allowed, position, targets)
    token_terms = (first_pass[15] - ref_rows) * scored
    seq_means = jnp.sum(jnp.where(seq_match, token_terms[:, None], 0.0), axis=0) / length_both
    kl_total = lax.psum(jnp.sum(seq_means[seq_here:]), "dp")
    seq_total = seq_here * dp_count
    kl_estimate = kl_total / seq_total
    signs = 2.0 * desirable.astype(jnp.float32) - 1.0
    sigmoid_val = jax.nn.sigmoid(kto_beta * signs * (seq_means[:seq_here] - kl_estimate))
    slope = -kto_beta * signs * sigmoid_val * (1.0 - sigmoid_val)
    kto_loss, slope_total = lax.psum((jnp.sum(1.0 - sigmoid_val), jnp.sum(slope)), "dp")
    seq_coef = (
        jnp.concatenate([slope, jnp.broadcast_to(-slope_total / seq_total, (seq_here,))])
        / length_both
    )
    token_coef = jnp.sum(jnp.where(seq_match, seq_coef[None, :], 0.0), axis=1) * scored
    matrices = gather_weights(weights_low)
    current = forward_pass(matrices, smalls, rows_low, allowed, position, targets)
    joined_all, up_all, vocab_all, dense_all, down_all = matrices
    (
        attn_low,
        mlp_low,
        joined_cols,
        query_low,
        keys_low,
        values_low,
        score_lse,
        mixed_low,
        hidden,
        active_low,
        resid_sum,
        final_low,
        logits,
        vocab_lse,
        target_hit,
        log_probs,
    ) = current
    softmax_local = jnp.exp(logits - vocab_lse[:, None])
    dlogits = (token_coef[:, None] * (jnp.where(target_hit, 1.0, 0.0) - softmax_local)).astype(
        jnp.bfloat16
    )
    grad_vocab = jnp.einsum("rd,rv->dv", final_low, dlogits, preferred_element_type=jnp.float32)
    dfinal_part = jnp.einsum("rv,dv->rd", dlogits, vocab_all, preferred_element_type=jnp.float32)
    dfinal = lax.psum(dfinal_part, "mp")
    _, final_pull = jax.vjp(layer_norm, resid_sum, smalls[8], smalls[9])
    dresid, grad_final_gain, grad_final_shift = final_pull(dfinal)
    grad_b_out = jnp.sum(dresid, axis=0)
    dbranch = dresid.astype(jnp.bfloat16)
    grad_dense = jnp.einsum("rk,rd->kd", mixed_low, dbranch, preferred_element_type=jnp.float32)
    grad_down = jnp.einsum("rf,rd->fd", active_low, dbranch, preferred_element_type=jnp.float32)
    dmixed = jnp.einsum("rd,kd->rk", dbranch, dense_all, preferred_element_type=jnp.float32).astype(
        jnp.bfloat16
    )
    dactive = jnp.einsum("rd,fd->rf", dbranch, down_all, preferred_element_type=jnp.float32)
    _, gelu_pull = jax.vjp(gelu_exact, hidden)
    dhidden = gelu_pull(dactive)[0].astype(jnp.bfloat16)
    grad_up = jnp.einsum("rd,rf->df", mlp_low, dhidden, preferred_element_type=jnp.float32)
    grad_b_up = jnp.sum(dhidden.astype(jnp.float32), axis=0)
    dmlp_part = jnp.einsum("rf,df->rd", dhidden, up_all, preferred_element_type=jnp.float32)
    dmixed_heads = dmixed.reshape(count_rows, -1, HD)
    scores = attention_scores(query_low, keys_low, allowed)
    probs_float = jnp.where(allowed[None], jnp.exp(scores - score_lse), 0.0)
    dvalues = jnp.einsum(
        "hrc,rhd->chd",
        probs_float.astype(jnp.bfloat16),
        dmixed_heads,
        preferred_element_type=jnp.float32,
    )
    dprobs = jnp.einsum(
        "rhd,chd->hrc", dmixed_heads, values_low, preferred_element_type=jnp.float32
    )
    inner_sum = jnp.sum(probs_float * dprobs, axis=-1, keepdims=True)
    dscores = (probs_float * (dprobs - inner_sum)).astype(jnp.bfloat16)
    dquery = jnp.einsum(
        "hrc,chd->rhd", dscores, keys_low, preferred_element_type=jnp.float32
    ) / math.sqrt(HD)
    dkeys = jnp.einsum(
        "hrc,rhd->chd", dscores, query_low, preferred_element_type=jnp.float32
    ) / math.sqrt(HD)
    _, rotate_pull = jax.vjp(lambda value: rotate(value, position), joined_cols[:, :, 0])
    dfused = jnp.stack([rotate_pull(dquery)[0], rotate_pull(dkeys)[0], dvalues], axis=2)
    dfused = dfused.reshape(count_rows, -1).astype(jnp.bfloat16)
    grad_joined = jnp.einsum("rd,re->de", attn_low, dfused, preferred_element_type=jnp.float32)
    grad_b_joined = jnp.sum(dfused.astype(jnp.float32), axis=0)
    dattn_part = jnp.einsum("re,de->rd", dfused, joined_all, preferred_element_type=jnp.float32)
    dattn, dmlp = lax.psum((dattn_part, dmlp_part), "mp")
    rows_float = rows_low.astype(jnp.float32)
    _, attn_pull = jax.vjp(layer_norm, rows_float, smalls[0], smalls[1])
    drows_attn, grad_attn_gain, grad_attn_shift = attn_pull(dattn)
    _, mlp_pull = jax.vjp(layer_norm, rows_float, smalls[2], smalls[3])
    drows_mlp, grad_mlp_gain, grad_mlp_shift = mlp_pull(dmlp)
    drows = dresid + drows_attn + drows_mlp
    my_slots = 2 * my_index + jnp.arange(2, dtype=jnp.int32)
    anchor = jnp.sum(
        jnp.where(pair_order[None, :] == my_slots[:, None], block_slots[None, :], 0), axis=1
    )
    back_hot = (anchor[:, None] == block_slots[None, :]).astype(jnp.float32)
    back_blocks = drows[tokens_here:].reshape(2, piece_rows, width)
    back_sent = jnp.einsum("st,spd->tpd", back_hot, back_blocks, precision=lax.Precision.HIGHEST)
    returned = lax.all_to_all(
        back_sent.reshape(dp_count, 2, piece_rows, width),
        "dp",
        split_axis=0,
        concat_axis=0,
        tiled=True,
    )
    grad_input = drows[:tokens_here] + jnp.sum(returned, axis=0).reshape(tokens_here, width)
    gw_joined, gw_up, gw_vocab = (
        lax.psum_scatter(grad_joined, "dp", scatter_dimension=0, tiled=True),
        lax.psum_scatter(grad_up, "dp", scatter_dimension=0, tiled=True),
        lax.psum_scatter(grad_vocab, "dp", scatter_dimension=0, tiled=True),
    )
    gw_dense, gw_down = (
        lax.psum_scatter(grad_dense, "dp", scatter_dimension=1, tiled=True),
        lax.psum_scatter(grad_down, "dp", scatter_dimension=1, tiled=True),
    )
    (
        sg_attn_gain,
        sg_attn_shift,
        sg_mlp_gain,
        sg_mlp_shift,
        sg_b_joined,
        sg_b_up,
        sg_b_out,
        sg_final_gain,
        sg_final_shift,
    ) = lax.psum(
        (
            grad_attn_gain,
            grad_attn_shift,
            grad_mlp_gain,
            grad_mlp_shift,
            grad_b_joined,
            grad_b_up,
            grad_b_out,
            grad_final_gain,
            grad_final_shift,
        ),
        "dp",
    )
    return (
        kto_loss,
        kl_estimate,
        grad_input,
        sg_attn_gain,
        sg_attn_shift,
        sg_mlp_gain,
        sg_mlp_shift,
        gw_joined,
        sg_b_joined,
        gw_dense,
        sg_b_out,
        gw_up,
        sg_b_up,
        gw_down,
        sg_b_out,
        sg_final_gain,
        sg_final_shift,
        gw_vocab,
    )


DP = ("z", "y")
CHIPS = ("z", "y", "x")
ALL = ("z", "y", "x", "c")
SWAP = ((0, 1), (1, 0))
F32, BF16 = jnp.float32, jnp.bfloat16
BY_X = (0, 2)
END_BY_X = (0,)


def dot(a, b, contract):
    return lax.dot_general(a, b, ((contract[:1], contract[1:]), ((), ())), preferred_element_type=F32)


def swap(value):
    return lax.ppermute(value, "c", SWAP)


def normed(values):
    centred = values - jnp.mean(values, axis=-1, keepdims=True)
    inverse = lax.rsqrt(jnp.mean(centred * centred, axis=-1, keepdims=True) + norm_eps)
    return centred * inverse, inverse


def norm_back(t, hat, inverse):
    return inverse * (
        t - jnp.mean(t, axis=-1, keepdims=True) - hat * jnp.mean(t * hat, axis=-1, keepdims=True)
    )


def exchange(value):
    return lax.all_to_all(value, DP, split_axis=0, concat_axis=0, tiled=True)


def here():
    return tuple(lax.axis_index(a) for a in ALL)


def send(source, target, out_sem, in_sem, device):
    copy = pltpu.make_async_remote_copy(
        src_ref=source,
        dst_ref=target,
        send_sem=out_sem,
        recv_sem=in_sem,
        device_id=device,
        device_id_type=pl.DeviceIdType.MESH,
    )
    copy.start()
    return copy


def arrived(target, out_sem, in_sem, device):
    pltpu.make_async_remote_copy(
        src_ref=target,
        dst_ref=target,
        send_sem=out_sem,
        recv_sem=in_sem,
        device_id=device,
        device_id_type=pl.DeviceIdType.MESH,
    ).wait_recv()


def left(source, out_sem, in_sem, device):
    pltpu.make_async_remote_copy(
        src_ref=source,
        dst_ref=source,
        send_sem=out_sem,
        recv_sem=in_sem,
        device_id=device,
        device_id_type=pl.DeviceIdType.MESH,
    ).wait_send()


def greet(devices):
    barrier = pltpu.get_barrier_semaphore()
    for device in devices:
        pl.semaphore_signal(barrier, inc=1, device_id=device, device_id_type=pl.DeviceIdType.MESH)
    pl.semaphore_wait(barrier, len(devices))


def neighbours(nz):
    iz, iy, ix, ic = here()
    return [(lax.rem(iz + k, nz), iy, ix, ic) for k in range(1, nz)] + [
        (iz, 1 - iy, ix, ic),
        (iz, iy, 1 - ix, ic),
    ]


def other_core():
    iz, iy, ix, ic = here()
    return (iz, iy, ix, 1 - ic)


class Reduce:
    @staticmethod
    def scratch(parts, nz, half, width):
        dma = pltpu.SemaphoreType.DMA
        return [
            pltpu.VMEM((parts, nz, 2, half, width), BF16),
            pltpu.VMEM((parts, nz, half, width), BF16),
            pltpu.VMEM((parts, nz, half, width), BF16),
            pltpu.VMEM((parts, nz, half, width), BF16),
            pltpu.VMEM((parts, nz, half, width), BF16),
            pltpu.VMEM((parts, nz, half, width), BF16),
            dma((parts, nz, 2)),
            dma((parts, nz, 2)),
            dma((parts, nz)),
            dma((parts, nz)),
            dma((parts, nz)),
            dma((parts, nz)),
            dma((parts, nz)),
        ]

    def __init__(self, nz, half, part, refs, by_x=(0,)):
        self.by_x = by_x
        self.nz, self.half, self.part = nz, half, part
        (
            self.in1,
            self.out2,
            self.in2,
            self.out3,
            self.below,
            self.above,
            self.s1,
            self.r1,
            self.s2,
            self.r2,
            self.s3,
            self.rb,
            self.ra,
        ) = refs
        self.copies = []

    def along(self, h):
        iz, iy, ix, ic = here()
        across_x, across_y = (iz, iy, 1 - ix, ic), (iz, 1 - iy, ix, ic)
        return (across_x, across_y) if h in self.by_x else (across_y, across_x)

    def block(self, h, z, first_mine, second):
        _, iy, ix, _ = here()
        rows = pl.ds(h * self.half, self.half)
        if h in self.by_x:
            return self.part.at[z, second, ix if first_mine else 1 - ix, rows]
        return self.part.at[z, iy if first_mine else 1 - iy, second, rows]

    def mine(self, h):
        _, iy, ix, _ = here()
        return iy if h in self.by_x else ix

    def plane(self, k):
        return lax.rem(here()[0] + k, self.nz)

    def start(self, h, far):
        first, _ = self.along(h)
        second = 1 - self.mine(h) if far else self.mine(h)
        for k in list(range(1, self.nz)) + [0]:
            z = self.plane(k)
            self.copies.append(
                send(
                    self.block(h, z, False, second),
                    self.in1.at[h, z, second],
                    self.s1.at[h, z, second],
                    self.r1.at[h, z, second],
                    first,
                )
            )

    def second(self, h):
        first, across = self.along(h)
        far = 1 - self.mine(h)
        for k in list(range(1, self.nz)) + [0]:
            z = self.plane(k)
            arrived(self.in1.at[h, z, far], self.s1.at[h, z, far], self.r1.at[h, z, far], first)
            self.out2[h, z] = (
                self.block(h, z, True, far)[...].astype(F32) + self.in1[h, z, far].astype(F32)
            ).astype(BF16)
            self.copies.append(
                send(self.out2.at[h, z], self.in2.at[h, z], self.s2.at[h, z], self.r2.at[h, z], across)
            )

    def third(self, h):
        first, across = self.along(h)
        near = self.mine(h)
        for k in list(range(1, self.nz)) + [0]:
            z = self.plane(k)
            arrived(self.in1.at[h, z, near], self.s1.at[h, z, near], self.r1.at[h, z, near], first)
            arrived(self.in2.at[h, z], self.s2.at[h, z], self.r2.at[h, z], across)
            total = (
                self.block(h, z, True, near)[...].astype(F32)
                + self.in1[h, z, near].astype(F32)
                + self.in2[h, z].astype(F32)
            )
            if k == 0:
                return total
            self.out3[h, z] = total.astype(BF16)

    def hops(self, m):
        up = [(z, m + 1, self.below, self.rb, m > 0) for z in range(self.nz - 1, m, -1)]
        down = [(z, m - 1, self.above, self.ra, m < self.nz - 1) for z in range(m)]
        return up + down

    def chain(self, h):
        iz, iy, ix, ic = here()
        for m in range(self.nz):

            @pl.when(iz == m)
            def _():
                for z, to, buffer, sems, waits in self.hops(m):
                    device = (to, iy, ix, ic)
                    if waits:
                        arrived(buffer.at[h, z], self.s3.at[h, z], sems.at[h, z], device)
                        self.out3[h, z] = (
                            self.out3[h, z].astype(F32) + buffer[h, z].astype(F32)
                        ).astype(BF16)
                    send(self.out3.at[h, z], buffer.at[h, z], self.s3.at[h, z], sems.at[h, z], device)
                if m == 0:
                    self.below[h, m] = jnp.zeros(self.below.shape[2:], BF16)
                if m == self.nz - 1:
                    self.above[h, m] = jnp.zeros(self.above.shape[2:], BF16)

    def finish(self, h, total):
        iz, iy, ix, ic = here()
        for at_end, buffer, sems in (
            (iz == 0, self.below, self.rb),
            (iz == self.nz - 1, self.above, self.ra),
        ):

            @pl.when(jnp.logical_not(at_end))
            def _():
                arrived(buffer.at[h, iz], self.s3.at[h, iz], sems.at[h, iz], (1 - iz, iy, ix, ic))

        return total + self.below[h, iz].astype(F32) + self.above[h, iz].astype(F32)

    def end(self, parts):
        iz, iy, ix, ic = here()
        for copy in self.copies:
            copy.wait_send()
        for h in parts:
            for k in range(1, self.nz):
                z = self.plane(k)
                left(self.out3.at[h, z], self.s3.at[h, z], self.rb.at[h, z], (z, iy, ix, ic))


class Gather:
    @staticmethod
    def scratch(parts, nz):
        dma = pltpu.SemaphoreType.DMA
        return [dma((parts, nz + 1)), dma((parts, nz)), dma((parts, nz, 2)), dma((parts, nz, 2, 2)), dma((parts,))]

    def __init__(self, nz, half, out, refs, forward=None, by_x=(0,)):
        self.by_x = by_x
        self.nz, self.half, self.out = nz, half, out
        self.sz, self.sp, self.sq, self.r, self.local = refs
        self.copies, self.locals, self.forward = [], [], forward

    def axes(self, h):
        iz, iy, ix, ic = here()
        across_x, across_y = (iz, iy, 1 - ix, ic), (iz, 1 - iy, ix, ic)
        return (across_y, across_x) if h in self.by_x else (across_x, across_y)

    def block(self, h, z, y, x):
        return self.out.at[z, y, x, pl.ds(h * self.half, self.half)]

    def on(self, h, source, z, y, x, which):
        p, q = self.axes(h)
        there, got = self.block(h, z, y, x), self.r.at[h, z, y, x]
        if "p" in which:
            send(source, there, self.sp.at[h, z], got, p)
        if "q" in which:
            send(source, there, self.sq.at[h, z, x if h not in self.by_x else y], got, q)
        if self.forward is not None:
            self.forward(h, source, z, y, x)

    def along_z(self, h, source, z, step, sem):
        iz, iy, ix, ic = here()
        there = iz + step

        @pl.when((there >= 0) & (there < self.nz))
        def _():
            send(source, self.block(h, z, iy, ix), self.sz.at[h, sem], self.r.at[h, z, iy, ix], (there, iy, ix, ic))

    def start(self, h, source):
        iz, iy, ix, _ = here()
        copy = pltpu.make_async_copy(source, self.block(h, iz, iy, ix), self.local.at[h])
        copy.start()
        self.locals.append(copy)
        self.along_z(h, source, iz, 1, iz)
        self.along_z(h, source, iz, -1, self.nz)
        self.on(h, source, iz, iy, ix, "pq")

    def got(self, h, z, y, x):
        arrived(self.block(h, z, y, x), self.sz.at[h, 0], self.r.at[h, z, y, x], self.axes(h)[0])

    def first(self, h, distance, step):
        iz, iy, ix, _ = here()
        z = iz - distance * step

        @pl.when((z >= 0) & (z < self.nz))
        def _():
            self.got(h, z, iy, ix)
            block = self.block(h, z, iy, ix)
            self.along_z(h, block, z, step, z)
            self.on(h, block, z, iy, ix, "pq")

    def second(self, h, k):
        iz, iy, ix, _ = here()
        z = lax.rem(iz + k, self.nz)
        y, x = (1 - iy, ix) if h in self.by_x else (iy, 1 - ix)
        self.got(h, z, y, x)
        self.on(h, self.block(h, z, y, x), z, y, x, "q")

    def third(self, h, k):
        iz, iy, ix, _ = here()
        z = lax.rem(iz + k, self.nz)
        for side in (0, 1):
            if h in self.by_x:
                y, x = (iy if side == 0 else 1 - iy), 1 - ix
            else:
                y, x = 1 - iy, (ix if side == 0 else 1 - ix)
            self.got(h, z, y, x)
            if self.forward is not None:
                self.forward(h, self.block(h, z, y, x), z, y, x)

    def turns(self):
        return [1, self.nz - 1] + [k for k in range(2, self.nz - 1)]

    def firsts(self, parts):
        for h in parts:
            self.second(h, 0)
        for distance in range(1, self.nz):
            for step in (1, -1):
                for h in parts:
                    self.first(h, distance, step)

    def seconds(self, parts):
        for k in self.turns():
            for h in parts:
                self.second(h, k)

    def thirds(self, parts):
        for k in [0] + self.turns():
            for h in parts:
                self.third(h, k)

    def rest(self):
        self.firsts((0, 1))
        self.seconds((0, 1))
        self.thirds((0, 1))

    def end(self, parts):
        iz, iy, ix, ic = here()
        for copy in self.locals:
            copy.wait()
        for h in parts:
            p, q = self.axes(h)
            for k in range(self.nz):
                z = lax.rem(iz + k, self.nz)
                block, got = self.block(h, z, iy, ix), self.r.at[h, z, iy, ix]
                left(block, self.sp.at[h, z], got, p)
                for side in (0, 1):
                    left(block, self.sq.at[h, z, side], got, q)
                up = (z <= iz) & (iz < self.nz - 1)
                down = (z > iz) & (iz > 0)

                @pl.when(up | down)
                def _():
                    left(block, self.sz.at[h, z], got, p)

            @pl.when(iz > 0)
            def _():
                left(self.block(h, iz, iy, ix), self.sz.at[h, self.nz], self.r.at[h, iz, iy, ix], p)


def reduce_gather(nz, half, part, out, refs, finished):
    reduce = Reduce(nz, half, part, refs[:13], BY_X)
    gather = Gather(nz, half, out, refs[13:], None, BY_X)
    greet(neighbours(nz))
    early, late = (0, 1), (2, 3)

    def begin(parts):
        for far in (True, False):
            for h in parts:
                reduce.start(h, far)

    def finish(parts, kept):
        for h in parts:
            gather.start(h, finished(h, reduce.finish(h, kept[h])))

    begin(early)
    for h in early:
        reduce.second(h)
    begin(late)
    kept = {h: reduce.third(h) for h in early}
    for h in early:
        reduce.chain(h)
    for h in late:
        reduce.second(h)
    finish(early, kept)
    kept = {h: reduce.third(h) for h in late}
    for h in late:
        reduce.chain(h)
    gather.firsts(early)
    finish(late, kept)
    gather.seconds(early)
    gather.firsts(late)
    gather.thirds(early)
    gather.seconds(late)
    gather.thirds(late)
    gather.end(early + late)
    reduce.end(early + late)


def forward_kernel(nz, half, part, rows, bias, gain, shift, out, resid, fin, *refs):
    def finished(h, total):
        at = pl.ds(h * half, half)
        total = rows[at].astype(F32) + total + bias[...]
        resid[at] = total
        hat, _ = normed(total)
        fin[h] = (hat * gain[...] + shift[...]).astype(BF16)
        return fin.at[h]

    reduce_gather(nz, half, part, out, refs, finished)


def backward_kernel(nz, half, part, resid, gain, out, vectors, fin, *refs):
    sums = []

    def finished(h, total):
        hat, inverse = normed(resid[pl.ds(h * half, half)])
        dresid = norm_back(total * gain[...], hat, inverse)
        fin[h] = dresid.astype(BF16)
        sums.append([jnp.sum(v, axis=0, keepdims=True) for v in (total * hat, total, dresid)])
        return fin.at[h]

    reduce_gather(nz, half, part, out, refs, finished)
    for i in range(3):
        vectors[pl.ds(i, 1)] = sum(part_sums[i] for part_sums in sums)


def vmem():
    return pl.BlockSpec(memory_space=pltpu.VMEM)


def anywhere():
    return pl.BlockSpec(memory_space=pl.ANY)


def busy(us):
    return pl.CostEstimate(flops=0, bytes_accessed=us * 3_000_000, transcendentals=0)


def comm(which, limit=48):
    return pltpu.CompilerParams(collective_id=which, has_side_effects=True, vmem_limit_bytes=limit << 20)


def reduce_norm_gather(nz, part, rows, bias, gain, shift):
    share, width = rows.shape
    half = share // 4
    out, resid = pl.pallas_call(
        functools.partial(forward_kernel, nz, half),
        out_shape=[
            jax.ShapeDtypeStruct((nz, 2, 2, share, width), BF16),
            jax.ShapeDtypeStruct((share, width), F32),
        ],
        in_specs=[vmem()] * 5,
        out_specs=[anywhere(), vmem()],
        scratch_shapes=[pltpu.VMEM((4, half, width), BF16)]
        + Reduce.scratch(4, nz, half, width)
        + Gather.scratch(4, nz),
        cost_estimate=busy(90),
        compiler_params=comm(2),
    )(part.reshape(nz, 2, 2, share, width), rows, bias, gain, shift)
    return out.reshape(4 * nz * share, width), resid


def reduce_back_gather(nz, part, resid, gain):
    share, width = resid.shape
    half = share // 4
    out, vectors = pl.pallas_call(
        functools.partial(backward_kernel, nz, half),
        out_shape=[
            jax.ShapeDtypeStruct((nz, 2, 2, share, width), BF16),
            jax.ShapeDtypeStruct((3, width), F32),
        ],
        in_specs=[vmem()] * 3,
        out_specs=[anywhere(), vmem()],
        scratch_shapes=[pltpu.VMEM((4, half, width), BF16)]
        + Reduce.scratch(4, nz, half, width)
        + Gather.scratch(4, nz),
        cost_estimate=busy(90),
        compiler_params=comm(3),
    )(part.reshape(nz, 2, 2, share, width), resid, gain)
    return out.reshape(4 * nz * share, width), vectors


def merge(a, b):
    top = jnp.maximum(a[0], b[0])
    return (top, a[1] * jnp.exp(a[0] - top) + b[1] * jnp.exp(b[0] - top), a[2] + b[2])


def objective_kernel(
    nz, seqs, seq_total, stats, hot, scored, refs, lens, wanted, coef, lse_out, scalars, held, near, far, s1, r1, s2, r2
):
    iz, iy, ix, ic = here()
    plane = [(iz, iy, 1 - ix, ic), (iz, 1 - iy, ix, ic), (iz, 1 - iy, 1 - ix, ic)]
    line = [(lax.rem(iz + k, nz), iy, ix, c) for c in (ic, 1 - ic) for k in range(nz)][1:]
    greet(plane + line)
    copies = []
    for i, device in enumerate(plane):
        copies.append(send(stats, near.at[iy, ix], s1.at[i], r1.at[iy, ix], device))
    near[iy, ix] = stats[...]
    for _, y, x, _ in plane:
        arrived(near.at[y, x], s1.at[0], r1.at[y, x], plane[0])
    sides = [tuple(near[y, x, i] for i in range(3)) for y in (0, 1) for x in (0, 1)]
    current = merge(merge(sides[0], sides[1]), merge(sides[2], sides[3]))
    for i in range(3):
        held[i] = current[i]
        far[iz, ic, i] = current[i]
    for i, device in enumerate(line):
        copies.append(send(held, far.at[iz, ic], s2.at[i], r2.at[iz, ic], device))
    for z, _, _, c in line:
        arrived(far.at[z, c], s2.at[0], r2.at[z, c], line[0])

    def whole(c):
        total = tuple(far[0, c, i] for i in range(3))
        for z in range(1, nz):
            total = merge(total, tuple(far[z, c, i] for i in range(3)))
        lse = total[0] + jnp.log(total[1])
        return lse, total[2] - lse

    (own_lse, own), (pair_lse, pair) = whole(0), whole(1)
    lse_out[...] = jnp.where(ic == 0, own_lse, pair_lse)

    def means(values, ref):
        terms = (values - ref) * scored[...]
        return [
            jnp.sum(terms * hot[s], axis=1, keepdims=True) / lens[:, s : s + 1] for s in range(seqs)
        ]

    own_means, pair_means = means(own, refs[0]), means(pair, refs[1])
    kl = jnp.sum(sum(pair_means), axis=0, keepdims=True) / seq_total
    loss = jnp.zeros((1, 1), F32)
    slopes = []
    for s in range(seqs):
        sign = 2.0 * wanted[:, s : s + 1] - 1.0
        sigmoid = jax.nn.sigmoid(kto_beta * sign * (own_means[s] - kl))
        slopes.append(-kto_beta * sign * sigmoid * (1.0 - sigmoid))
        loss = loss + jnp.sum(1.0 - sigmoid, axis=0, keepdims=True)
    shared = -jnp.sum(sum(slopes), axis=0, keepdims=True) / seq_total
    total = jnp.zeros_like(own)
    for s in range(seqs):
        value = jnp.where(ic == 0, slopes[s], shared) / lens[:, s : s + 1]
        total = total + hot[s] * value
    coef[...] = total * scored[...]
    scalars[0] = jnp.broadcast_to(loss, scalars.shape[1:])
    scalars[1] = jnp.broadcast_to(kl, scalars.shape[1:])
    for copy in copies:
        copy.wait_send()


def objective(nz, seq_total, stats, hot, scored, refs, lens, wanted):
    shape = scored.shape
    dma = pltpu.SemaphoreType.DMA
    return pl.pallas_call(
        functools.partial(objective_kernel, nz, hot.shape[0], seq_total),
        out_shape=[
            jax.ShapeDtypeStruct(shape, F32),
            jax.ShapeDtypeStruct(shape, F32),
            jax.ShapeDtypeStruct((2, 8, 128), F32),
        ],
        in_specs=[vmem()] * 6,
        out_specs=[vmem()] * 3,
        scratch_shapes=[
            pltpu.VMEM((3,) + shape, F32),
            pltpu.VMEM((2, 2, 3) + shape, F32),
            pltpu.VMEM((nz, 2, 3) + shape, F32),
            dma((3,)),
            dma((2, 2)),
            dma((2 * nz - 1,)),
            dma((nz, 2)),
        ],
        cost_estimate=busy(15),
        compiler_params=comm(4),
    )(stats, hot, scored, refs, lens, wanted)


def diagonal(nz):
    iz, iy, ix, ic = here()
    return [(lax.rem(iz + k, nz), 1 - iy, ix, 1 - ic) for k in range(nz)]


def to_head(nz, k, pairs, local_sem, out_sem, in_sem):
    iz, iy, ix, ic = here()
    z = lax.rem(iz + k, nz)
    device = (z, ic, ix, iy)

    def remote():
        for i, (source, target) in enumerate(pairs):
            send(source, target, out_sem.at[i, z], in_sem.at[i, iz], device)

    if k:
        remote()
        return
    pl.when(iy != ic)(remote)

    @pl.when(iy == ic)
    def _():
        for i, (source, target) in enumerate(pairs):
            copy = pltpu.make_async_copy(source, target, local_sem.at[i])
            copy.start()
            copy.wait()


def from_head(nz, k, targets, out_sem, in_sem):
    iz, iy, ix, ic = here()
    z = lax.rem(iz + k, nz)

    def wait():
        for i, target in enumerate(targets):
            arrived(target, out_sem.at[i, z], in_sem.at[i, z], (z, ic, ix, iy))

    if k:
        wait()
    else:
        pl.when(iy != ic)(wait)


def sent_head(nz, k, sources, out_sem, in_sem):
    iz, iy, ix, ic = here()
    z = lax.rem(iz + k, nz)

    def wait():
        for i, source in enumerate(sources):
            pltpu.make_async_remote_copy(
                src_ref=source,
                dst_ref=source,
                send_sem=out_sem.at[i, z],
                recv_sem=in_sem.at[i, z],
                device_id=(z, ic, ix, iy),
                device_id_type=pl.DeviceIdType.MESH,
            ).wait_send()

    if k:
        wait()
    else:
        pl.when(iy != ic)(wait)


def lanes(index, size):
    return pl.ds(pl.multiple_of(index * size, size), size)


def front_kernel(
    nz,
    half,
    residual,
    info,
    bias,
    joined_in,
    dense_in,
    down_in,
    natural,
    info_out,
    bias_out,
    joined_out,
    out_all,
    fs,
    fr,
    js,
    jr,
    jl,
    cs,
    cr,
    ms,
    mr,
    zs,
    zr,
    ps,
    ds,
    dr,
    dl,
    es,
    er,
    *refs,
):
    iz, iy, ix, ic = here()
    core = other_core()
    across = [(lax.rem(iz + k, nz), 1 - iy, ix, ic) for k in range(nz)]
    greet(neighbours(nz) + [core] + diagonal(nz) + across[1:])
    depth = joined_in.shape[0]
    cols = joined_out.shape[1]
    heads = dense_in.shape[0] // nz
    units = down_in.shape[0] // (2 * nz)
    dense_out = out_all.at[pl.ds(0, heads)]
    down_out, down_other = (out_all.at[pl.ds(heads + i * units, units)] for i in (0, 1))
    copies = []

    def rows_of(h, z, y, x, c):
        return natural.at[z, y, x, c, pl.ds(h * half, half)]

    def forward(h, source, z, y, x):
        send(source, rows_of(h, z, y, x, ic), fs.at[h, z, y, x], fr.at[h, z, y, x], core)

    class Rows(Gather):
        def block(self, h, z, y, x):
            return rows_of(h, z, y, x, ic)

    gather = Rows(nz, half, natural, refs, forward)
    first = pl.multiple_of((ix * 2 + ic) * 2 * half, 2 * half)
    for h in (0, 1):
        gather.start(h, residual.at[pl.ds(first + h * half, half)])

    copies.append(send(bias, bias_out, ms.at[0], mr.at[0], core))
    info_out[iz, iy] = info[...]
    across_y = (iz, 1 - iy, ix, ic)
    for k in range(1, nz):
        far = (lax.rem(iz + k, nz), iy, ix, ic)
        copies.append(send(info, info_out.at[iz, iy], zs.at[k], zr.at[iz, iy], far))
    copies.append(send(info, info_out.at[iz, iy], ps.at[iz], zr.at[iz, iy], across_y))

    mine = iz * 2 + iy
    for k in list(range(1, nz)) + [0]:
        z = lax.rem(iz + k, nz)
        to_head(
            nz,
            k,
            [
                (joined_in.at[:, lanes(z, cols)], joined_out.at[lanes(mine, depth)]),
                (dense_in.at[lanes(z, heads)], dense_out.at[:, lanes(mine, depth)]),
            ],
            jl,
            js,
            jr,
        )

    for k in range(1, nz):
        z = lax.rem(iz + k, nz)
        arrived(info_out.at[z, iy], zs.at[k], zr.at[z, iy], across_y)
        copies.append(send(info_out.at[z, iy], info_out.at[z, iy], ps.at[z], zr.at[z, iy], across_y))

    gather.firsts((0, 1))

    line = [(lax.rem(iz + k, nz), iy, ix, ic) for k in range(1, nz)]
    local = pltpu.make_async_copy(down_in.at[lanes(mine, units)], down_out.at[:, lanes(mine, depth)], dl.at[0])
    local.start()
    for device in line + across:
        d = device[0] * 2 + device[1]
        copies.append(
            send(down_in.at[lanes(d, units)], down_out.at[:, lanes(mine, depth)], ds.at[d], dr.at[mine], device)
        )
    gather.seconds((0, 1))
    gather.thirds((0, 1))

    def head_parts(z, side):
        d = z * 2 + side
        return joined_out.at[lanes(d, depth)], dense_out.at[:, lanes(d, depth)]

    for k in [0] + list(range(1, nz)):
        z = lax.rem(iz + k, nz)
        parts = head_parts(z, ic)
        from_head(nz, k, parts, js, jr)
        for i, part in enumerate(parts):
            copies.append(send(part, part, cs.at[i, z], cr.at[i, z], core))
    local.wait()
    for device in [(iz, iy, ix, ic)] + line + across:
        d = device[0] * 2 + device[1]
        block = down_out.at[:, lanes(d, depth)]
        if device[0] is not iz or device[1] is not iy:
            arrived(block, ds.at[d], dr.at[d], device)
        copies.append(send(block, down_other.at[:, lanes(d, depth)], es.at[d], er.at[d], core))
    for d in range(2 * nz):
        arrived(down_other.at[:, lanes(d, depth)], es.at[d], er.at[d], core)
    for k in range(nz):
        z = lax.rem(iz + k, nz)
        arrived(info_out.at[z, 1 - iy], ps.at[z], zr.at[z, 1 - iy], across_y)
    for z in range(nz):
        for y in (0, 1):
            for x in (0, 1):
                for h in (0, 1):
                    arrived(rows_of(h, z, y, x, 1 - ic), fs.at[h, z, y, x], fr.at[h, z, y, x], core)
                    left(rows_of(h, z, y, x, ic), fs.at[h, z, y, x], fr.at[h, z, y, x], core)
    for z in range(nz):
        for i, part in enumerate(head_parts(z, 1 - ic)):
            arrived(part, cs.at[i, z], cr.at[i, z], core)
    arrived(bias_out, ms.at[0], mr.at[0], core)
    gather.end((0, 1))
    for k in range(nz):
        z = lax.rem(iz + k, nz)
        sent_head(nz, k, [joined_in.at[:, lanes(z, cols)], dense_in.at[lanes(z, heads)]], js, jr)
    for copy in copies:
        copy.wait_send()


def front(nz, residual, info, bias, joined_in, dense_in, down_in):
    held, width = residual.shape
    half = held // 8
    depth, cols = joined_in.shape[0], joined_in.shape[1] // nz
    heads = dense_in.shape[0] // nz
    units = down_in.shape[0] // (2 * nz)
    dma = pltpu.SemaphoreType.DMA
    outs = pl.pallas_call(
        functools.partial(front_kernel, nz, half),
        out_shape=[
            jax.ShapeDtypeStruct((nz, 2, 2, 2, 2 * half, width), BF16),
            jax.ShapeDtypeStruct((nz, 2) + info.shape, F32),
            jax.ShapeDtypeStruct(bias.shape, F32),
            jax.ShapeDtypeStruct((2 * nz * depth, cols), BF16),
            jax.ShapeDtypeStruct((heads + 2 * units, 2 * nz * depth), BF16),
        ],
        in_specs=[anywhere(), vmem(), vmem(), anywhere(), anywhere(), anywhere()],
        out_specs=[anywhere(), vmem(), vmem(), anywhere(), anywhere()],
        scratch_shapes=[
            dma((2, nz, 2, 2)),
            dma((2, nz, 2, 2)),
            dma((2, nz)),
            dma((2, nz)),
            dma((2,)),
            dma((2, nz)),
            dma((2, nz)),
            dma((1,)),
            dma((1,)),
            dma((nz,)),
            dma((nz, 2)),
            dma((nz,)),
            dma((2 * nz,)),
            dma((2 * nz,)),
            dma((1,)),
            dma((2 * nz,)),
            dma((2 * nz,)),
        ]
        + Gather.scratch(2, nz),
        cost_estimate=busy(45),
        compiler_params=comm(1, 16),
    )(residual, info, bias, joined_in, dense_in, down_in)
    natural = outs[0].reshape(8 * nz * 2 * half, width)
    return natural, outs[1].reshape((2 * nz,) + info.shape), outs[2], outs[3], outs[4]


def end_kernel(
    nz,
    half,
    part,
    mine_rows,
    other_rows,
    rows,
    vectors,
    keep,
    give,
    joined_in,
    dense_in,
    rows_out,
    vectors_out,
    bias_out,
    joined_out,
    dense_out,
    merged,
    came,
    rows_in,
    vector_in,
    vector_sum,
    give_in,
    joined_came,
    joined_sum,
    dense_came,
    dense_sum,
    ms,
    mr,
    vs,
    vr,
    bs,
    br,
    bp,
    js,
    jr,
    jl,
    cs,
    cr,
    os,
    orr,
    *refs,
):
    iz, iy, ix, ic = here()
    core = other_core()
    across_x, across_y = (iz, iy, 1 - ix, ic), (iz, 1 - iy, ix, ic)
    greet(neighbours(nz) + [core] + diagonal(nz))
    reduce = Reduce(nz, half, merged, refs, END_BY_X)
    copies = []
    depth = joined_in.shape[0] // (2 * nz)
    cols = joined_in.shape[1]
    heads = dense_in.shape[0]
    groups = [(1 - iy, 1 - ix), (iy, 1 - ix), (1 - iy, ix), (iy, ix)]

    for y, x in groups:
        for k in list(range(1, nz)) + [0]:
            z = lax.rem(iz + k, nz)
            copies.append(
                send(part.at[z, y, x, 1 - ic], came.at[z, y, x], ms.at[z, y, x], mr.at[z, y, x], core)
            )
    copies.append(send(vectors, vector_in.at[0], vs.at[0], vr.at[0], core))
    copies.append(send(give, give_in, bs.at[0], br.at[nz, 0], core))
    copies.append(send(other_rows, rows_in, os.at[0], orr.at[0], core))
    for k in range(nz):
        z = lax.rem(iz + k, nz)
        theirs = z * 2 + 1 - ic
        copies.append(
            send(joined_in.at[lanes(theirs, depth)], joined_came.at[z], cs.at[0, z], cr.at[0, z], core)
        )
        copies.append(
            send(dense_in.at[:, lanes(theirs, depth)], dense_came.at[z], cs.at[1, z], cr.at[1, z], core)
        )

    def merge_group(y, x):
        for k in list(range(1, nz)) + [0]:
            z = lax.rem(iz + k, nz)
            arrived(came.at[z, y, x], ms.at[z, y, x], mr.at[z, y, x], core)
            merged[z, y, x] = (part[z, y, x, ic].astype(F32) + came[z, y, x].astype(F32)).astype(BF16)

    merge_group(*groups[0])
    reduce.start(0, True)
    merge_group(*groups[1])
    reduce.start(0, False)
    merge_group(*groups[2])
    reduce.start(1, True)
    reduce.start(1, False)
    merge_group(*groups[3])

    arrived(vector_in.at[0], vs.at[0], vr.at[0], core)
    vector_sum[0] = vectors[...] + vector_in[0]
    copies.append(send(vector_sum.at[0], vector_in.at[1], vs.at[1], vr.at[1], across_x))
    arrived(give_in, bs.at[0], br.at[nz, 0], core)
    bias_out[iz, iy] = keep[...] + give_in[...]
    for k in range(1, nz):
        far = (lax.rem(iz + k, nz), iy, ix, ic)
        copies.append(send(bias_out.at[iz, iy], bias_out.at[iz, iy], bs.at[k], br.at[iz, iy], far))
    copies.append(send(bias_out.at[iz, iy], bias_out.at[iz, iy], bp.at[iz], br.at[iz, iy], across_y))

    for k in list(range(1, nz)) + [0]:
        z = lax.rem(iz + k, nz)
        ours = z * 2 + ic
        arrived(joined_came.at[z], cs.at[0, z], cr.at[0, z], core)
        joined_sum[z] = (joined_in[lanes(ours, depth)].astype(F32) + joined_came[z].astype(F32)).astype(BF16)
        arrived(dense_came.at[z], cs.at[1, z], cr.at[1, z], core)
        dense_sum[z] = (dense_in[:, lanes(ours, depth)].astype(F32) + dense_came[z].astype(F32)).astype(BF16)
        to_head(
            nz,
            k,
            [
                (joined_sum.at[z], joined_out.at[:, lanes(iz, cols)]),
                (dense_sum.at[z], dense_out.at[lanes(iz, heads)]),
            ],
            jl,
            js,
            jr,
        )

    for h in (0, 1):
        reduce.second(h)
    arrived(vector_in.at[1], vs.at[1], vr.at[1], across_x)
    vector_sum[1] = vector_sum[0] + vector_in[1]
    copies.append(send(vector_sum.at[1], vector_in.at[2], vs.at[2], vr.at[2], across_y))
    for k in range(1, nz):
        z = lax.rem(iz + k, nz)
        arrived(bias_out.at[z, iy], bs.at[k], br.at[z, iy], across_y)
        copies.append(send(bias_out.at[z, iy], bias_out.at[z, iy], bp.at[z], br.at[z, iy], across_y))
    kept = [reduce.third(h) for h in (0, 1)]
    for h in (0, 1):
        reduce.chain(h)
    arrived(vector_in.at[2], vs.at[2], vr.at[2], across_y)
    vector_sum[2] = vector_sum[1] + vector_in[2]
    for k in range(1, nz):
        far = (lax.rem(iz + k, nz), iy, ix, ic)
        copies.append(send(vector_sum.at[2], vector_in.at[3 + iz], vs.at[2 + k], vr.at[3 + iz], far))
    vector_in[3 + iz] = vector_sum[2]
    arrived(rows_in, os.at[0], orr.at[0], core)
    for h in (0, 1):
        at = pl.ds(h * half, half)
        hat, inverse = normed(rows[at].astype(F32))
        back = norm_back(reduce.finish(h, kept[h]), hat, inverse)
        block = rows_out.at[ix, ic, at]
        rows_out[ix, ic, at] = (
            mine_rows[at].astype(F32) + rows_in[at].astype(F32) + back
        ).astype(BF16)
        copies.append(send(block, block, os.at[1 + h], orr.at[1 + h], across_x))
        copies.append(send(block, block, os.at[3 + h], orr.at[3 + h], core))
    for h in (0, 1):
        block = rows_out.at[1 - ix, ic, pl.ds(h * half, half)]
        arrived(block, os.at[1 + h], orr.at[1 + h], across_x)
        copies.append(send(block, block, os.at[5 + h], orr.at[5 + h], core))
    for k in range(1, nz):
        z = lax.rem(iz + k, nz)
        arrived(vector_in.at[3 + z], vs.at[2 + k], vr.at[3 + z], (z, iy, ix, ic))
    total = vector_in[3]
    for z in range(1, nz):
        total = total + vector_in[3 + z]
    vectors_out[...] = total
    for k in range(nz):
        z = lax.rem(iz + k, nz)
        arrived(bias_out.at[z, 1 - iy], bp.at[z], br.at[z, 1 - iy], across_y)
        from_head(
            nz, k, [joined_out.at[:, lanes(z, cols)], dense_out.at[lanes(z, heads)]], js, jr
        )
        sent_head(nz, k, [joined_sum.at[z], dense_sum.at[z]], js, jr)
    for h in (0, 1):
        at = pl.ds(h * half, half)
        arrived(rows_out.at[ix, 1 - ic, at], os.at[3 + h], orr.at[3 + h], core)
        arrived(rows_out.at[1 - ix, 1 - ic, at], os.at[5 + h], orr.at[5 + h], core)
    reduce.end((0, 1))
    for copy in copies:
        copy.wait_send()


def end(nz, part, mine_rows, other_rows, rows, vectors, keep, give, joined_in, dense_in):
    share, width = rows.shape
    half = share // 2
    depth, cols, heads = joined_in.shape[0] // (2 * nz), joined_in.shape[1], dense_in.shape[0]
    dma = pltpu.SemaphoreType.DMA
    return pl.pallas_call(
        functools.partial(end_kernel, nz, half),
        out_shape=[
            jax.ShapeDtypeStruct((2, 2, share, width), BF16),
            jax.ShapeDtypeStruct(vectors.shape, F32),
            jax.ShapeDtypeStruct((nz, 2) + keep.shape, F32),
            jax.ShapeDtypeStruct((depth, nz * cols), BF16),
            jax.ShapeDtypeStruct((nz * heads, depth), BF16),
        ],
        in_specs=[vmem()] * 9,
        out_specs=[vmem(), vmem(), vmem(), vmem(), vmem()],
        scratch_shapes=[
            pltpu.VMEM((nz, 2, 2, share, width), BF16),
            pltpu.VMEM((nz, 2, 2, share, width), BF16),
            pltpu.VMEM((share, width), BF16),
            pltpu.VMEM((3 + nz,) + vectors.shape, F32),
            pltpu.VMEM((3,) + vectors.shape, F32),
            pltpu.VMEM(keep.shape, F32),
            pltpu.VMEM((nz, depth, cols), BF16),
            pltpu.VMEM((nz, depth, cols), BF16),
            pltpu.VMEM((nz, heads, depth), BF16),
            pltpu.VMEM((nz, heads, depth), BF16),
            dma((nz, 2, 2)),
            dma((nz, 2, 2)),
            dma((2 + nz,)),
            dma((3 + nz,)),
            dma((nz,)),
            dma((nz + 1, 2)),
            dma((nz,)),
            dma((2, nz)),
            dma((2, nz)),
            dma((2,)),
            dma((2, nz)),
            dma((2, nz)),
            dma((7,)),
            dma((7,)),
        ]
        + Reduce.scratch(2, nz, half, width),
        cost_estimate=busy(70),
        compiler_params=comm(5),
    )(part, mine_rows, other_rows, rows, vectors, keep, give, joined_in, dense_in)


def turned(values, cosine, low, high):
    half_rot = ROT // 2
    return (
        values * cosine
        + pltpu.roll(values, values.shape[1] - half_rot, 1) * low
        + pltpu.roll(values, half_rot, 1) * high
    )


def block_rows(order, ref, piece, first, count):
    return jnp.concatenate(
        [ref[pl.ds(pl.multiple_of(order[first + i] * piece, piece), piece), :] for i in range(count)], axis=0
    )


def attention_kernel(piece, order, fused, tables, allowed, qkv, probs_out, mixed):
    groups, held = allowed.shape[0], allowed.shape[1]
    per = held // piece
    for g in range(groups):
        at = pl.ds(g * held, held)
        rows = block_rows(order, fused, piece, g * per, per)
        turn_by = [tables[i, at] for i in range(3)]
        query = turned(rows[:, :HD], *turn_by).astype(BF16)
        keys = turned(rows[:, HD : 2 * HD], *turn_by).astype(BF16)
        values = rows[:, 2 * HD :].astype(BF16)
        qkv[at, :HD] = query
        qkv[at, HD : 2 * HD] = keys
        qkv[at, 2 * HD :] = values
        scores = jnp.where(allowed[g] > 0.5, dot(query, keys, (1, 1)) / math.sqrt(HD), masked_score)
        weights = jnp.exp(scores - jnp.max(scores, axis=-1, keepdims=True))
        probs = weights / jnp.sum(weights, axis=-1, keepdims=True)
        probs_out[g] = probs
        mixed[at] = dot(probs.astype(BF16), values, (1, 0)).astype(BF16)


def attention(order, fused, tables, allowed, piece):
    total = fused.shape[0]
    return pl.pallas_call(
        functools.partial(attention_kernel, piece),
        out_shape=[
            jax.ShapeDtypeStruct((total, 3 * HD), BF16),
            jax.ShapeDtypeStruct(allowed.shape, F32),
            jax.ShapeDtypeStruct((total, HD), BF16),
        ],
        in_specs=[pl.BlockSpec(memory_space=pltpu.SMEM)] + [vmem()] * 3,
        out_specs=[vmem()] * 3,
        compiler_params=pltpu.CompilerParams(vmem_limit_bytes=32 << 20),
    )(order, fused, tables, allowed)


def place_kernel(piece, order, mixed, active, out):
    per = 2
    out[:, :HD] = mixed[...]
    for g in range(mixed.shape[0] // (per * piece)):
        out[pl.ds(g * per * piece, per * piece), HD:] = block_rows(order, active, piece, g * per, per)


def place(order, mixed, active, piece):
    total = mixed.shape[0]
    return pl.pallas_call(
        functools.partial(place_kernel, piece),
        out_shape=jax.ShapeDtypeStruct((total, HD + active.shape[1]), BF16),
        in_specs=[pl.BlockSpec(memory_space=pltpu.SMEM)] + [vmem()] * 2,
        out_specs=vmem(),
        compiler_params=pltpu.CompilerParams(vmem_limit_bytes=32 << 20),
    )(order, mixed, active)


def attention_back_kernel(piece, order, douts, slope, qkv, probs_in, tables, dfused, dhidden, sums):
    groups, held = probs_in.shape[0], probs_in.shape[1]
    per = held // piece
    joined_sum = jnp.zeros((1, 3 * HD), F32)
    hidden_sum = jnp.zeros((1, slope.shape[1]), F32)
    for g in range(groups):
        at = pl.ds(g * held, held)
        query, keys, values = qkv[at, :HD], qkv[at, HD : 2 * HD], qkv[at, 2 * HD :]
        dmixed = douts[at, :HD].astype(BF16)
        probs = probs_in[g]
        dvalues = dot(probs.astype(BF16), dmixed, (0, 0))
        dprobs = dot(dmixed, values, (1, 1))
        dscores = (probs * (dprobs - jnp.sum(probs * dprobs, axis=-1, keepdims=True))).astype(BF16)
        turn_by = [tables[0, at], -tables[1, at], -tables[2, at]]
        dquery = turned(dot(dscores, keys, (1, 0)) / math.sqrt(HD), *turn_by)
        dkeys = turned(dot(dscores, query, (0, 0)) / math.sqrt(HD), *turn_by)
        whole = jnp.concatenate([dquery, dkeys, dvalues], axis=1).astype(BF16)
        joined_sum = joined_sum + jnp.sum(whole.astype(F32), axis=0, keepdims=True)
        for i in range(per):
            to = pl.ds(pl.multiple_of(order[g * per + i] * piece, piece), piece)
            dfused[to, :] = whole[i * piece : (i + 1) * piece]
            grown = (douts[pl.ds(g * held + i * piece, piece), HD:] * slope[to, :]).astype(BF16)
            dhidden[to, :] = grown
            hidden_sum = hidden_sum + jnp.sum(grown.astype(F32), axis=0, keepdims=True)
    sums[:, : 3 * HD] = joined_sum
    sums[:, 3 * HD :] = hidden_sum


def attention_back(order, douts, slope, qkv, probs, tables, piece):
    total, units = slope.shape
    return pl.pallas_call(
        functools.partial(attention_back_kernel, piece),
        out_shape=[
            jax.ShapeDtypeStruct((total, 3 * HD), BF16),
            jax.ShapeDtypeStruct((total, units), BF16),
            jax.ShapeDtypeStruct((1, 3 * HD + units), F32),
        ],
        in_specs=[pl.BlockSpec(memory_space=pltpu.SMEM)] + [vmem()] * 5,
        out_specs=[vmem()] * 3,
        compiler_params=pltpu.CompilerParams(vmem_limit_bytes=40 << 20),
    )(order, douts, slope, qkv, probs, tables)


def fast_shards(
    residual,
    lengths,
    pair_order,
    token_ids,
    desirable,
    ref_match,
    ref_pair,
    attn_gain,
    attn_shift,
    mlp_gain,
    mlp_shift,
    w_joined,
    b_joined,
    w_dense,
    b_dense,
    w_up,
    b_up,
    w_down,
    b_down,
    final_gain,
    final_shift,
    w_vocab,
):
    nz, ny, nx = lax.axis_size("z"), lax.axis_size("y"), lax.axis_size("x")
    n = nz * ny
    chips = n * nx
    iz, iy, ix, ic = (lax.axis_index(a) for a in ALL)
    dp = iz * ny + iy
    held, width = residual.shape
    total = n * held
    blocks = 2 * n
    piece = held // 2
    seqs = lengths.shape[1]
    depth = width // n
    vcols = w_vocab.shape[1] // n
    ffs = w_up.shape[1] // n
    hcols = 3 * HD
    mine = ix * 2 + ic

    info = jnp.stack(
        [
            token_ids.astype(F32),
            ref_match,
            ref_pair,
            jnp.concatenate(
                [lengths[0].astype(F32), desirable.astype(F32), jnp.zeros((held - 2 * seqs,), F32)]
            ),
        ]
    )
    bias_own = jnp.concatenate([b_joined, b_up]).astype(F32)
    natural, info, bias_other, wj, wout = front(
        nz, residual, info, bias_own.reshape(-1, HD), w_joined, w_dense, w_down
    )
    bias_other = bias_other.reshape(-1)

    send_up = w_up.reshape(depth, n, ffs).transpose(1, 0, 2)
    send_vocab = w_vocab.reshape(depth, n, vcols).transpose(1, 0, 2)
    send_up, bias_other = lax.optimization_barrier((send_up, bias_other))
    up_own = exchange(send_up)
    bias_first = jnp.where(ic == 0, bias_own, bias_other)
    bias_second = jnp.where(ic == 0, bias_other, bias_own)
    bj_all = jnp.where(iy == 0, bias_first, bias_second)[: nz * hcols].reshape(nz, hcols)
    bj = lax.dynamic_index_in_dim(bj_all, iz, 0, keepdims=False)
    bu_all = jnp.stack([bias_own[nz * hcols :], bias_other[nz * hcols :]]).reshape(2, n, ffs)
    bu = lax.dynamic_index_in_dim(bu_all, dp, 1, keepdims=False).reshape(2 * ffs)

    ids = info[:, 0].astype(jnp.int32)
    refs = jnp.stack([info[:, 1], info[:, 2]])
    lens = info[:, 3, :seqs].astype(jnp.int32)
    wanted = info[:, 3, seqs : 2 * seqs]
    slots = jnp.arange(blocks, dtype=jnp.int32)
    anchor = jnp.sum(
        jnp.where(pair_order[None, :] == slots[:, None], slots[None, :], 0), axis=1
    )
    order = jnp.where(ic == 0, slots, anchor)
    back = jnp.where(ic == 0, slots, pair_order)
    anchor_hot = (anchor[:, None] == slots[None, :])[:, :, None]
    pair_ids = jnp.sum(jnp.where(anchor_hot, ids.reshape(1, blocks, piece), 0), axis=1).reshape(n, held)
    all_ids = jnp.stack([ids, pair_ids])

    ends = jnp.stack([jnp.sum(lens[:, : s + 1], axis=1) for s in range(seqs)], axis=1)
    starts = ends - lens
    places = jnp.arange(held, dtype=jnp.int32)
    segment = jnp.sum((places[None, :, None] >= ends[:, None, :]).astype(jnp.int32), axis=2)
    hot = (segment[:, :, None] == jnp.arange(seqs, dtype=jnp.int32)).astype(F32)
    position = places[None, :] - jnp.sum(hot * starts[:, None, :].astype(F32), axis=2).astype(jnp.int32)
    allowed = (segment[:, :, None] == segment[:, None, :]) & (places[None, :, None] >= places[None, None, :])
    scored = jnp.concatenate(
        [segment[:, 1:] == segment[:, :-1], jnp.zeros((n, 1), jnp.bool_)], axis=1
    ).astype(F32)
    targets = jnp.concatenate([all_ids[:, :, 1:], jnp.zeros((2, n, 1), jnp.int32)], axis=2)

    hat, inverse = normed(natural.astype(F32))
    ga, sa, gm, sm, gf, sf = (
        v.astype(F32) for v in (attn_gain, attn_shift, mlp_gain, mlp_shift, final_gain, final_shift)
    )
    attn_low = (hat * ga + sa).astype(BF16)
    mlp_low = (hat * gm + sm).astype(BF16)
    lane = jnp.arange(HD, dtype=jnp.int32)
    frequency = jnp.exp((lane % (ROT // 2)).astype(F32) * (-2.0 * math.log(10000.0) / ROT))
    angles = position.reshape(total)[:, None].astype(F32) * frequency[None, :]
    cosine = jnp.where(lane < ROT, jnp.cos(angles), 1.0)
    sine = jnp.sin(angles)
    tables = jnp.stack(
        [
            cosine,
            jnp.where(lane < ROT // 2, -sine, 0.0),
            jnp.where((lane >= ROT // 2) & (lane < ROT), sine, 0.0),
        ]
    )
    fused = dot(attn_low, wj, (1, 0)) + bj
    qkv, probs, mixed = attention(order, fused, tables, allowed.astype(F32), piece)
    up_own, mixed, send_vocab = lax.optimization_barrier((up_own, mixed, send_vocab))
    up_other = swap(up_own)
    vocab_got = exchange(send_vocab)
    wup = jnp.concatenate([w.reshape(width, ffs) for w in (up_own, up_other)], axis=1)
    hidden = dot(mlp_low, wup, (1, 0)) + bu
    bell = 0.5 * (1.0 + lax.erf(hidden * math.sqrt(0.5)))
    active = (hidden * bell).astype(BF16)
    gelu_slope = bell + hidden * jnp.exp(-0.5 * hidden * hidden) * (1.0 / math.sqrt(2.0 * math.pi))
    outs_low = place(order, mixed, active, piece)
    branch_part = dot(outs_low, wout, (1, 0)).astype(BF16)
    share = total // chips
    chip = dp * nx + ix
    first_row = jnp.sum(jnp.where(slots == chip * share // piece, order, 0)) * piece + chip * share % piece
    rows_here = lax.dynamic_slice_in_dim(natural, first_row, share, 0)
    bias_out = (b_dense.astype(F32) + b_down.astype(F32))[None]
    final, resid = reduce_norm_gather(nz, branch_part, rows_here, bias_out, gf[None], sf[None])

    vocab_got, final = lax.optimization_barrier((vocab_got, final))
    vocab_own = vocab_got.reshape(width, vcols)
    vocab_other = swap(vocab_own)
    my_targets = jnp.where(ic == 0, targets[0], targets[1]).reshape(total)
    logits = [dot(final, w, (1, 0)) for w in (vocab_own, vocab_other)]
    hits = [
        lax.broadcasted_iota(jnp.int32, (total, vcols), 1)
        == (my_targets - ((ix * 2 + core) * n + dp) * vcols)[:, None]
        for core in (ic, 1 - ic)
    ]
    tops = [jnp.max(part, axis=1) for part in logits]
    top = jnp.maximum(tops[0], tops[1])
    sums = sum(jnp.sum(jnp.exp(part - top[:, None]), axis=1) for part in logits)
    picks = sum(jnp.sum(jnp.where(h, part, 0.0), axis=1) for h, part in zip(hits, logits))
    stats = jnp.stack([top, sums, picks]).reshape(3, n, held)
    coef, my_lse, scalars = objective(
        nz, n * seqs, stats, hot.transpose(2, 0, 1), scored, refs, lens.astype(F32), wanted
    )
    coef, my_lse = coef.reshape(total), my_lse.reshape(total)
    kto_loss, kl_estimate = scalars[0, 0, 0], scalars[1, 0, 0]

    dlogits = [
        (coef[:, None] * (jnp.where(h, 1.0, 0.0) - jnp.exp(part - my_lse[:, None]))).astype(BF16)
        for h, part in zip(hits, logits)
    ]
    gv_own = dot(final, dlogits[0], (0, 0))
    gv_other = dot(final, dlogits[1], (0, 0)).astype(BF16)
    dfinal_part = (dot(dlogits[0], vocab_own, (1, 1)) + dot(dlogits[1], vocab_other, (1, 1))).astype(BF16)
    gv = (gv_own + swap(gv_other).astype(F32)).astype(BF16)
    gv, dfinal_part = lax.optimization_barrier((gv, dfinal_part))
    early_cols = vcols * 272 // 800
    gv = gv.reshape(n, depth, vcols)
    grad_early = exchange(gv[:, :, :early_cols])
    dbranch, final_vectors = reduce_back_gather(nz, dfinal_part, resid, gf[None])
    gv_late, dbranch, grad_early = lax.optimization_barrier((gv[:, :, early_cols:], dbranch, grad_early))
    grad_late = exchange(gv_late)
    grad_vocab = jnp.concatenate([grad_early, grad_late], axis=2).transpose(1, 0, 2).reshape(depth, n * vcols)
    grad_vocab = lax.optimization_barrier(grad_vocab).astype(F32)

    gout = dot(outs_low, dbranch, (0, 0))
    douts = dot(dbranch, wout, (1, 1))
    dfused, dhidden, bias_sums = attention_back(order, douts, gelu_slope, qkv, probs, tables, piece)
    gj = dot(attn_low, dfused, (0, 0)).astype(BF16)
    gu = dot(mlp_low, dhidden, (0, 0))
    dattn = dot(dfused, wj, (1, 1))
    dmlp = dot(dhidden, wup, (1, 1))
    g_attn_gain = jnp.sum(dattn * hat, axis=0)
    g_attn_shift = jnp.sum(dattn, axis=0)
    g_mlp_gain = jnp.sum(dmlp * hat, axis=0)
    g_mlp_shift = jnp.sum(dmlp, axis=0)
    t_part = (dattn * ga + dmlp * gm).astype(BF16)

    def to_send(up, down):
        return jnp.concatenate(
            [up.reshape(n, depth, ffs), down.reshape(ffs, n, depth).transpose(1, 0, 2)], axis=1
        )

    give_grads = to_send(gu[:, ffs:].astype(BF16), gout[HD + ffs :].astype(BF16))
    layer_grads = to_send(gu[:, :ffs], gout[HD : HD + ffs]) + swap(give_grads).astype(F32)
    layer_grads = exchange(layer_grads.astype(BF16))
    grad_up = layer_grads[:, :depth].transpose(1, 0, 2).reshape(depth, n * ffs).astype(F32)
    grad_down = layer_grads[:, depth:].reshape(n * ffs, depth).astype(F32)

    share2 = total // (2 * chips)

    def natural_rows(core):
        first = dp * held + (ix * 2 + core) * share2
        place = jnp.sum(jnp.where(slots == first // piece, back, 0)) * piece + first % piece
        return lax.dynamic_slice_in_dim(dbranch, place, share2, 0)

    gbj, gbu = bias_sums[0, :hcols], bias_sums[0, hcols:]
    spare = jnp.zeros((8 * HD - hcols - ffs,), F32)
    keep = jnp.concatenate([gbj, gbu[:ffs], spare]).reshape(8, HD)
    give = jnp.concatenate([gbj, gbu[ffs:], spare]).reshape(8, HD)
    vectors = jnp.concatenate(
        [
            jnp.stack([g_attn_gain, g_attn_shift, g_mlp_gain, g_mlp_shift]),
            final_vectors,
            jnp.zeros((1, width), F32),
        ]
    )
    rows_out, vectors, biases, grad_joined, grad_dense = end(
        nz,
        t_part.reshape(nz, 2, 2, 2, share2, width),
        natural_rows(ic),
        natural_rows(1 - ic),
        lax.dynamic_slice_in_dim(residual, mine * share2, share2, 0),
        vectors,
        keep,
        give,
        gj,
        gout[:HD].astype(BF16),
    )
    grad_input = rows_out.reshape(held, width).astype(F32)
    grad_joined, grad_dense = grad_joined.astype(F32), grad_dense.astype(F32)
    g_attn_gain, g_attn_shift, g_mlp_gain, g_mlp_shift, g_final_gain, g_final_shift, g_out = vectors[:7]
    biases = biases.reshape(nz, 2, 8 * HD)
    gb_joined = jnp.where(ic == 0, biases[:, 0, :hcols], biases[:, 1, :hcols]).reshape(nz * hcols)
    gb_up = biases[:, :, hcols : hcols + ffs].reshape(n * ffs)
    return (
        kto_loss,
        kl_estimate,
        grad_input,
        g_attn_gain,
        g_attn_shift,
        g_mlp_gain,
        g_mlp_shift,
        grad_joined,
        gb_joined,
        grad_dense,
        g_out,
        grad_up,
        gb_up,
        grad_down,
        g_out,
        g_final_gain,
        g_final_shift,
        grad_vocab,
    )


def placed(dp, mp):
    ins = (
        P(dp, None),
        P(dp, None),
        P(),
        P(dp),
        P(dp),
        P(dp),
        P(dp),
        P(),
        P(),
        P(),
        P(),
        P(dp, mp),
        P(mp),
        P(mp, dp),
        P(),
        P(dp, mp),
        P(mp),
        P(mp, dp),
        P(),
        P(),
        P(),
        P(dp, mp),
    )
    outs = (
        P(),
        P(),
        P(dp, None),
        P(),
        P(),
        P(),
        P(),
        P(dp, mp),
        P(mp),
        P(mp, dp),
        P(),
        P(dp, mp),
        P(mp),
        P(mp, dp),
        P(),
        P(),
        P(),
        P(dp, mp),
    )
    return ins, outs


def solution(mesh):
    n_dp, n_mp = mesh.shape["dp"], mesh.shape["mp"]
    if n_dp == 8 and n_mp == 4:
        fine = jax.sharding.Mesh(mesh.devices.reshape(n_dp // 2, 2, n_mp // 2, 2), ALL)
        ins, outs = placed(DP, ("x", "c"))
        return jax.shard_map(fast_shards, mesh=fine, in_specs=ins, out_specs=outs, check_vma=False)
    ins, outs = placed("dp", "mp")
    return jax.shard_map(shards, mesh=mesh, in_specs=ins, out_specs=outs, check_vma=False)
```

```python
import functools
import math

import jax
import jax.numpy as jnp
from jax import lax
from jax.experimental import pallas as pl
from jax.experimental.layout import Layout, with_layout_constraint
from jax.experimental.pallas import tpu as pltpu
from jax.sharding import PartitionSpec as P

HD = 128
ROT = 32


kto_beta = 4.0
norm_eps = 1e-05
masked_score = -1e30


def joined(value, axis, join):
    pieces = jax.tree.map(lambda part: lax.all_gather(part, axis), value)
    head = jax.tree.map(lambda part: part[0], pieces)
    tail = jax.tree.map(lambda part: part[1:], pieces)
    subtotal, _ = lax.scan(lambda subtotal, piece: (join(subtotal, piece), None), head, tail)
    return subtotal


def layer_norm(values, norm_gain, norm_shift):
    centred = values - jnp.mean(values, axis=-1, keepdims=True)
    spread = jnp.mean(centred * centred, axis=-1, keepdims=True)
    return centred * lax.rsqrt(spread + norm_eps) * norm_gain + norm_shift


def rotate(values, position):
    half_rot = ROT // 2
    inverse = jnp.exp(jnp.arange(half_rot, dtype=jnp.float32) * (-2.0 * math.log(10000.0) / ROT))
    angles = position.astype(jnp.float32)[:, None] * inverse[None, :]
    cosine_table = jnp.cos(angles)[:, None, :]
    sine_table = jnp.sin(angles)[:, None, :]
    first_half = values[..., :half_rot]
    second_half = values[..., half_rot:ROT]
    return jnp.concatenate(
        [
            first_half * cosine_table - second_half * sine_table,
            second_half * cosine_table + first_half * sine_table,
            values[..., ROT:],
        ],
        axis=-1,
    )


def gelu_exact(values):
    return jax.nn.gelu(values, approximate=False)


def attention_scores(query_low, keys_low, allowed):
    raw_scores = jnp.einsum(
        "rhd,chd->hrc", query_low, keys_low, preferred_element_type=jnp.float32
    ) / math.sqrt(HD)
    return jnp.where(allowed[None], raw_scores, masked_score)


def combine_vocab(first, second):
    high_first, total_first, pick_first = first
    high_second, total_second, pick_second = second
    highest = jnp.maximum(high_first, high_second)
    merged_total = total_first * jnp.exp(high_first - highest) + total_second * jnp.exp(
        high_second - highest
    )
    return (highest, merged_total, pick_first + pick_second)


def gather_weights(weights_low):
    w_joined, w_up, w_vocab, w_dense, w_down = weights_low
    joined_all, up_all, vocab_all = (
        lax.all_gather(w_joined, "dp", axis=0, tiled=True),
        lax.all_gather(w_up, "dp", axis=0, tiled=True),
        lax.all_gather(w_vocab, "dp", axis=0, tiled=True),
    )
    dense_all, down_all = (
        lax.all_gather(w_dense, "dp", axis=1, tiled=True),
        lax.all_gather(w_down, "dp", axis=1, tiled=True),
    )
    return (joined_all, up_all, vocab_all, dense_all, down_all)


def forward_pass(gathered, smalls, rows_low, allowed, position, targets):
    joined_all, up_all, vocab_all, dense_all, down_all = gathered
    (
        attn_gain,
        attn_shift,
        mlp_gain,
        mlp_shift,
        b_joined,
        b_dense,
        b_up,
        b_down,
        final_gain,
        final_shift,
    ) = smalls
    rows_float = rows_low.astype(jnp.float32)
    count_rows = rows_float.shape[0]
    attn_low = layer_norm(rows_float, attn_gain, attn_shift).astype(jnp.bfloat16)
    mlp_low = layer_norm(rows_float, mlp_gain, mlp_shift).astype(jnp.bfloat16)
    joined_cols = jnp.dot(attn_low, joined_all, preferred_element_type=jnp.float32) + b_joined
    joined_cols = joined_cols.reshape(count_rows, -1, 3, HD)
    query_low = rotate(joined_cols[:, :, 0], position).astype(jnp.bfloat16)
    keys_low = rotate(joined_cols[:, :, 1], position).astype(jnp.bfloat16)
    values_low = joined_cols[:, :, 2].astype(jnp.bfloat16)
    scores = attention_scores(query_low, keys_low, allowed)
    highest = jnp.max(scores, axis=-1, keepdims=True)
    scaled_exp = jnp.exp(scores - highest)
    totals = jnp.sum(scaled_exp, axis=-1, keepdims=True)
    probs_low = (scaled_exp / totals).astype(jnp.bfloat16)
    score_lse = highest + jnp.log(totals)
    mixed_low = (
        jnp.einsum("hrc,chd->rhd", probs_low, values_low, preferred_element_type=jnp.float32)
        .reshape(count_rows, -1)
        .astype(jnp.bfloat16)
    )
    hidden = jnp.dot(mlp_low, up_all, preferred_element_type=jnp.float32) + b_up
    active_low = gelu_exact(hidden).astype(jnp.bfloat16)
    branch_part = jnp.dot(mixed_low, dense_all, preferred_element_type=jnp.float32) + jnp.dot(
        active_low, down_all, preferred_element_type=jnp.float32
    )
    branch = lax.psum(branch_part, "mp")
    resid_sum = rows_float + branch + b_dense + b_down
    final_low = layer_norm(resid_sum, final_gain, final_shift).astype(jnp.bfloat16)
    logits = jnp.dot(final_low, vocab_all, preferred_element_type=jnp.float32)
    local_high = jnp.max(logits, axis=-1)
    local_total = jnp.sum(jnp.exp(logits - local_high[:, None]), axis=-1)
    column = targets - lax.axis_index("mp") * logits.shape[1]
    target_hit = lax.broadcasted_iota(jnp.int32, logits.shape, 1) == column[:, None]
    local_pick = jnp.sum(jnp.where(target_hit, logits, 0.0), axis=-1)
    high_all, total_all, picked = joined((local_high, local_total, local_pick), "mp", combine_vocab)
    vocab_lse = high_all + jnp.log(total_all)
    return (
        attn_low,
        mlp_low,
        joined_cols,
        query_low,
        keys_low,
        values_low,
        score_lse,
        mixed_low,
        hidden,
        active_low,
        resid_sum,
        final_low,
        logits,
        vocab_lse,
        target_hit,
        picked - vocab_lse,
    )


def shards(
    residual,
    lengths,
    pair_order,
    token_ids,
    desirable,
    ref_match,
    ref_pair,
    attn_gain,
    attn_shift,
    mlp_gain,
    mlp_shift,
    w_joined,
    b_joined,
    w_dense,
    b_dense,
    w_up,
    b_up,
    w_down,
    b_down,
    final_gain,
    final_shift,
    w_vocab,
):
    dp_count = lax.axis_size("dp")
    tokens_here = residual.shape[0]
    piece_rows = tokens_here // 2
    width = residual.shape[1]
    seq_here = lengths.shape[1]
    block_count = 2 * dp_count
    my_index = lax.axis_index("dp")
    block_slots = jnp.arange(block_count, dtype=jnp.int32)
    my_blocks = 2 * my_index + jnp.arange(2, dtype=jnp.int32)
    my_targets = jnp.sum(
        jnp.where(block_slots[None, :] == my_blocks[:, None], pair_order[None, :], 0), axis=1
    )
    send_hot = my_targets[:, None] == block_slots[None, :]
    own_blocks = residual.reshape(2, piece_rows, width)
    own_ids = token_ids.reshape(2, piece_rows)
    sent_rows = jnp.einsum(
        "ht,hpd->tpd", send_hot.astype(jnp.bfloat16), own_blocks, preferred_element_type=jnp.float32
    ).astype(jnp.bfloat16)
    sent_ids = jnp.sum(jnp.where(send_hot[:, :, None], own_ids[:, None, :], 0), axis=0)
    got_rows, got_ids = (
        lax.all_to_all(
            sent_rows.reshape(dp_count, 2, piece_rows, width),
            "dp",
            split_axis=0,
            concat_axis=0,
            tiled=True,
        ),
        lax.all_to_all(
            sent_ids.reshape(dp_count, 2, piece_rows), "dp", split_axis=0, concat_axis=0, tiled=True
        ),
    )
    paired_rows = jnp.sum(got_rows.astype(jnp.float32), axis=0).astype(jnp.bfloat16)
    paired_ids = jnp.sum(got_ids, axis=0)
    rows_low = jnp.concatenate([residual, paired_rows.reshape(tokens_here, width)], axis=0)
    ids_all = jnp.concatenate([token_ids, paired_ids.reshape(tokens_here)], axis=0)
    seq_lengths = lengths[0]
    seq_slots = jnp.arange(seq_here, dtype=jnp.int32)
    seq_ends = jnp.sum(
        jnp.where(seq_slots[None, :] <= seq_slots[:, None], seq_lengths[None, :], 0), axis=1
    )
    seq_starts = seq_ends - seq_lengths
    places = jnp.arange(tokens_here, dtype=jnp.int32)
    segment = jnp.sum((places[:, None] >= seq_ends[None, :]).astype(jnp.int32), axis=1)
    own_start = jnp.sum(
        jnp.where(segment[:, None] == seq_slots[None, :], seq_starts[None, :], 0), axis=1
    )
    position_half = places - own_start
    segment_all = jnp.concatenate([segment, segment + seq_here])
    position = jnp.concatenate([position_half, position_half])
    count_rows = 2 * tokens_here
    row_index = jnp.arange(count_rows, dtype=jnp.int32)
    allowed = (segment_all[:, None] == segment_all[None, :]) & (
        row_index[None, :] <= row_index[:, None]
    )
    targets = jnp.concatenate([ids_all[1:], jnp.zeros((1,), jnp.int32)])
    scored = jnp.concatenate(
        [segment_all[1:] == segment_all[:-1], jnp.zeros((1,), jnp.bool_)]
    ).astype(jnp.float32)
    ref_rows = jnp.concatenate([ref_match, ref_pair])
    length_float = seq_lengths.astype(jnp.float32)
    length_both = jnp.concatenate([length_float, length_float])
    seq_match = segment_all[:, None] == jnp.arange(2 * seq_here, dtype=jnp.int32)[None, :]
    smalls = tuple(
        (
            value.astype(jnp.float32)
            for value in (
                attn_gain,
                attn_shift,
                mlp_gain,
                mlp_shift,
                b_joined,
                b_dense,
                b_up,
                b_down,
                final_gain,
                final_shift,
            )
        )
    )
    weights_low = (w_joined, w_up, w_vocab, w_dense, w_down)
    gathered = gather_weights(weights_low)
    first_pass = forward_pass(gathered, smalls, rows_low, allowed, position, targets)
    token_terms = (first_pass[15] - ref_rows) * scored
    seq_means = jnp.sum(jnp.where(seq_match, token_terms[:, None], 0.0), axis=0) / length_both
    kl_total = lax.psum(jnp.sum(seq_means[seq_here:]), "dp")
    seq_total = seq_here * dp_count
    kl_estimate = kl_total / seq_total
    signs = 2.0 * desirable.astype(jnp.float32) - 1.0
    sigmoid_val = jax.nn.sigmoid(kto_beta * signs * (seq_means[:seq_here] - kl_estimate))
    slope = -kto_beta * signs * sigmoid_val * (1.0 - sigmoid_val)
    kto_loss, slope_total = lax.psum((jnp.sum(1.0 - sigmoid_val), jnp.sum(slope)), "dp")
    seq_coef = (
        jnp.concatenate([slope, jnp.broadcast_to(-slope_total / seq_total, (seq_here,))])
        / length_both
    )
    token_coef = jnp.sum(jnp.where(seq_match, seq_coef[None, :], 0.0), axis=1) * scored
    matrices = gather_weights(weights_low)
    current = forward_pass(matrices, smalls, rows_low, allowed, position, targets)
    joined_all, up_all, vocab_all, dense_all, down_all = matrices
    (
        attn_low,
        mlp_low,
        joined_cols,
        query_low,
        keys_low,
        values_low,
        score_lse,
        mixed_low,
        hidden,
        active_low,
        resid_sum,
        final_low,
        logits,
        vocab_lse,
        target_hit,
        log_probs,
    ) = current
    softmax_local = jnp.exp(logits - vocab_lse[:, None])
    dlogits = (token_coef[:, None] * (jnp.where(target_hit, 1.0, 0.0) - softmax_local)).astype(
        jnp.bfloat16
    )
    grad_vocab = jnp.einsum("rd,rv->dv", final_low, dlogits, preferred_element_type=jnp.float32)
    dfinal_part = jnp.einsum("rv,dv->rd", dlogits, vocab_all, preferred_element_type=jnp.float32)
    dfinal = lax.psum(dfinal_part, "mp")
    _, final_pull = jax.vjp(layer_norm, resid_sum, smalls[8], smalls[9])
    dresid, grad_final_gain, grad_final_shift = final_pull(dfinal)
    grad_b_out = jnp.sum(dresid, axis=0)
    dbranch = dresid.astype(jnp.bfloat16)
    grad_dense = jnp.einsum("rk,rd->kd", mixed_low, dbranch, preferred_element_type=jnp.float32)
    grad_down = jnp.einsum("rf,rd->fd", active_low, dbranch, preferred_element_type=jnp.float32)
    dmixed = jnp.einsum("rd,kd->rk", dbranch, dense_all, preferred_element_type=jnp.float32).astype(
        jnp.bfloat16
    )
    dactive = jnp.einsum("rd,fd->rf", dbranch, down_all, preferred_element_type=jnp.float32)
    _, gelu_pull = jax.vjp(gelu_exact, hidden)
    dhidden = gelu_pull(dactive)[0].astype(jnp.bfloat16)
    grad_up = jnp.einsum("rd,rf->df", mlp_low, dhidden, preferred_element_type=jnp.float32)
    grad_b_up = jnp.sum(dhidden.astype(jnp.float32), axis=0)
    dmlp_part = jnp.einsum("rf,df->rd", dhidden, up_all, preferred_element_type=jnp.float32)
    dmixed_heads = dmixed.reshape(count_rows, -1, HD)
    scores = attention_scores(query_low, keys_low, allowed)
    probs_float = jnp.where(allowed[None], jnp.exp(scores - score_lse), 0.0)
    dvalues = jnp.einsum(
        "hrc,rhd->chd",
        probs_float.astype(jnp.bfloat16),
        dmixed_heads,
        preferred_element_type=jnp.float32,
    )
    dprobs = jnp.einsum(
        "rhd,chd->hrc", dmixed_heads, values_low, preferred_element_type=jnp.float32
    )
    inner_sum = jnp.sum(probs_float * dprobs, axis=-1, keepdims=True)
    dscores = (probs_float * (dprobs - inner_sum)).astype(jnp.bfloat16)
    dquery = jnp.einsum(
        "hrc,chd->rhd", dscores, keys_low, preferred_element_type=jnp.float32
    ) / math.sqrt(HD)
    dkeys = jnp.einsum(
        "hrc,rhd->chd", dscores, query_low, preferred_element_type=jnp.float32
    ) / math.sqrt(HD)
    _, rotate_pull = jax.vjp(lambda value: rotate(value, position), joined_cols[:, :, 0])
    dfused = jnp.stack([rotate_pull(dquery)[0], rotate_pull(dkeys)[0], dvalues], axis=2)
    dfused = dfused.reshape(count_rows, -1).astype(jnp.bfloat16)
    grad_joined = jnp.einsum("rd,re->de", attn_low, dfused, preferred_element_type=jnp.float32)
    grad_b_joined = jnp.sum(dfused.astype(jnp.float32), axis=0)
    dattn_part = jnp.einsum("re,de->rd", dfused, joined_all, preferred_element_type=jnp.float32)
    dattn, dmlp = lax.psum((dattn_part, dmlp_part), "mp")
    rows_float = rows_low.astype(jnp.float32)
    _, attn_pull = jax.vjp(layer_norm, rows_float, smalls[0], smalls[1])
    drows_attn, grad_attn_gain, grad_attn_shift = attn_pull(dattn)
    _, mlp_pull = jax.vjp(layer_norm, rows_float, smalls[2], smalls[3])
    drows_mlp, grad_mlp_gain, grad_mlp_shift = mlp_pull(dmlp)
    drows = dresid + drows_attn + drows_mlp
    my_slots = 2 * my_index + jnp.arange(2, dtype=jnp.int32)
    anchor = jnp.sum(
        jnp.where(pair_order[None, :] == my_slots[:, None], block_slots[None, :], 0), axis=1
    )
    back_hot = (anchor[:, None] == block_slots[None, :]).astype(jnp.float32)
    back_blocks = drows[tokens_here:].reshape(2, piece_rows, width)
    back_sent = jnp.einsum("st,spd->tpd", back_hot, back_blocks, precision=lax.Precision.HIGHEST)
    returned = lax.all_to_all(
        back_sent.reshape(dp_count, 2, piece_rows, width),
        "dp",
        split_axis=0,
        concat_axis=0,
        tiled=True,
    )
    grad_input = drows[:tokens_here] + jnp.sum(returned, axis=0).reshape(tokens_here, width)
    gw_joined, gw_up, gw_vocab = (
        lax.psum_scatter(grad_joined, "dp", scatter_dimension=0, tiled=True),
        lax.psum_scatter(grad_up, "dp", scatter_dimension=0, tiled=True),
        lax.psum_scatter(grad_vocab, "dp", scatter_dimension=0, tiled=True),
    )
    gw_dense, gw_down = (
        lax.psum_scatter(grad_dense, "dp", scatter_dimension=1, tiled=True),
        lax.psum_scatter(grad_down, "dp", scatter_dimension=1, tiled=True),
    )
    (
        sg_attn_gain,
        sg_attn_shift,
        sg_mlp_gain,
        sg_mlp_shift,
        sg_b_joined,
        sg_b_up,
        sg_b_out,
        sg_final_gain,
        sg_final_shift,
    ) = lax.psum(
        (
            grad_attn_gain,
            grad_attn_shift,
            grad_mlp_gain,
            grad_mlp_shift,
            grad_b_joined,
            grad_b_up,
            grad_b_out,
            grad_final_gain,
            grad_final_shift,
        ),
        "dp",
    )
    return (
        kto_loss,
        kl_estimate,
        grad_input,
        sg_attn_gain,
        sg_attn_shift,
        sg_mlp_gain,
        sg_mlp_shift,
        gw_joined,
        sg_b_joined,
        gw_dense,
        sg_b_out,
        gw_up,
        sg_b_up,
        gw_down,
        sg_b_out,
        sg_final_gain,
        sg_final_shift,
        gw_vocab,
    )


DP = ("z", "y")
CHIPS = ("z", "y", "x")
ALL = ("z", "y", "x", "c")
SWAP = ((0, 1), (1, 0))
F32, BF16 = jnp.float32, jnp.bfloat16
BY_X = (0, 2)
END_BY_X = (0,)


def dot(a, b, contract):
    return lax.dot_general(a, b, ((contract[:1], contract[1:]), ((), ())), preferred_element_type=F32)


def swap(value):
    return lax.ppermute(value, "c", SWAP)


def normed(values):
    centred = values - jnp.mean(values, axis=-1, keepdims=True)
    inverse = lax.rsqrt(jnp.mean(centred * centred, axis=-1, keepdims=True) + norm_eps)
    return centred * inverse, inverse


def norm_back(t, hat, inverse):
    return inverse * (
        t - jnp.mean(t, axis=-1, keepdims=True) - hat * jnp.mean(t * hat, axis=-1, keepdims=True)
    )


def exchange(value):
    return lax.all_to_all(value, DP, split_axis=0, concat_axis=0, tiled=True)


def here():
    return tuple(lax.axis_index(a) for a in ALL)


def send(source, target, out_sem, in_sem, device):
    copy = pltpu.make_async_remote_copy(
        src_ref=source,
        dst_ref=target,
        send_sem=out_sem,
        recv_sem=in_sem,
        device_id=device,
        device_id_type=pl.DeviceIdType.MESH,
    )
    copy.start()
    return copy


def arrived(target, out_sem, in_sem, device):
    pltpu.make_async_remote_copy(
        src_ref=target,
        dst_ref=target,
        send_sem=out_sem,
        recv_sem=in_sem,
        device_id=device,
        device_id_type=pl.DeviceIdType.MESH,
    ).wait_recv()


def left(source, out_sem, in_sem, device):
    pltpu.make_async_remote_copy(
        src_ref=source,
        dst_ref=source,
        send_sem=out_sem,
        recv_sem=in_sem,
        device_id=device,
        device_id_type=pl.DeviceIdType.MESH,
    ).wait_send()


PIECES = 1


def in_pieces(source, target, out_sem, in_sem, device):
    size = source.shape[1] // PIECES
    for i in range(PIECES):
        at = (slice(None), pl.ds(i * size, size))
        send(source.at[at], target.at[at], out_sem, in_sem, device)


def greet(devices):
    barrier = pltpu.get_barrier_semaphore()
    for device in devices:
        pl.semaphore_signal(barrier, inc=1, device_id=device, device_id_type=pl.DeviceIdType.MESH)
    pl.semaphore_wait(barrier, len(devices))


def neighbours(nz):
    iz, iy, ix, ic = here()
    return [(lax.rem(iz + k, nz), iy, ix, ic) for k in range(1, nz)] + [
        (iz, 1 - iy, ix, ic),
        (iz, iy, 1 - ix, ic),
    ]


def other_core():
    iz, iy, ix, ic = here()
    return (iz, iy, ix, 1 - ic)


class Reduce:
    @staticmethod
    def scratch(parts, nz, half, width):
        dma = pltpu.SemaphoreType.DMA
        return [
            pltpu.VMEM((parts, nz, 2, half, width), BF16),
            pltpu.VMEM((parts, nz, half, width), BF16),
            pltpu.VMEM((parts, nz, half, width), BF16),
            pltpu.VMEM((parts, nz, half, width), BF16),
            pltpu.VMEM((parts, nz, half, width), BF16),
            dma((parts, nz, 2)),
            dma((parts, nz, 2)),
            dma((parts, nz)),
            dma((parts, nz)),
            dma((parts, nz)),
            dma((parts, nz)),
        ]

    def __init__(self, nz, half, part, refs, by_x=(0,)):
        self.by_x = by_x
        self.nz, self.half, self.part = nz, half, part
        (
            self.in1,
            self.out2,
            self.in2,
            self.out3,
            self.in3,
            self.s1,
            self.r1,
            self.s2,
            self.r2,
            self.s3,
            self.r3,
        ) = refs
        self.copies = []

    def along(self, h):
        iz, iy, ix, ic = here()
        across_x, across_y = (iz, iy, 1 - ix, ic), (iz, 1 - iy, ix, ic)
        return (across_x, across_y) if h in self.by_x else (across_y, across_x)

    def block(self, h, z, first_mine, second):
        _, iy, ix, _ = here()
        rows = pl.ds(h * self.half, self.half)
        if h in self.by_x:
            return self.part.at[z, second, ix if first_mine else 1 - ix, rows]
        return self.part.at[z, iy if first_mine else 1 - iy, second, rows]

    def mine(self, h):
        _, iy, ix, _ = here()
        return iy if h in self.by_x else ix

    def plane(self, k):
        return lax.rem(here()[0] + k, self.nz)

    def start(self, h, far):
        first, _ = self.along(h)
        second = 1 - self.mine(h) if far else self.mine(h)
        for k in list(range(1, self.nz)) + [0]:
            z = self.plane(k)
            self.copies.append(
                send(
                    self.block(h, z, False, second),
                    self.in1.at[h, z, second],
                    self.s1.at[h, z, second],
                    self.r1.at[h, z, second],
                    first,
                )
            )

    def second(self, h):
        first, across = self.along(h)
        far = 1 - self.mine(h)
        for k in list(range(1, self.nz)) + [0]:
            z = self.plane(k)
            arrived(self.in1.at[h, z, far], self.s1.at[h, z, far], self.r1.at[h, z, far], first)
            self.out2[h, z] = (
                self.block(h, z, True, far)[...].astype(F32) + self.in1[h, z, far].astype(F32)
            ).astype(BF16)
            self.copies.append(
                send(self.out2.at[h, z], self.in2.at[h, z], self.s2.at[h, z], self.r2.at[h, z], across)
            )

    def third(self, h):
        iz, iy, ix, ic = here()
        first, across = self.along(h)
        near = self.mine(h)
        for k in list(range(1, self.nz)) + [0]:
            z = self.plane(k)
            arrived(self.in1.at[h, z, near], self.s1.at[h, z, near], self.r1.at[h, z, near], first)
            arrived(self.in2.at[h, z], self.s2.at[h, z], self.r2.at[h, z], across)
            total = (
                self.block(h, z, True, near)[...].astype(F32)
                + self.in1[h, z, near].astype(F32)
                + self.in2[h, z].astype(F32)
            )
            if k == 0:
                return total
            self.out3[h, k] = total.astype(BF16)
            far = (z, iy, ix, ic)
            in_pieces(self.out3.at[h, k], self.in3.at[h, k], self.s3.at[h, k], self.r3.at[h, k], far)

    def finish(self, h, total):
        _, iy, ix, ic = here()
        for k in range(1, self.nz):
            z = self.plane(self.nz - k)
            arrived(self.in3.at[h, k], self.s3.at[h, k], self.r3.at[h, k], (z, iy, ix, ic))
            total = total + self.in3[h, k].astype(F32)
        return total

    def end(self, parts):
        iz, iy, ix, ic = here()
        for copy in self.copies:
            copy.wait_send()
        for h in parts:
            for k in range(1, self.nz):
                far = (self.plane(k), iy, ix, ic)
                left(self.out3.at[h, k], self.s3.at[h, k], self.r3.at[h, k], far)


class Gather:
    @staticmethod
    def scratch(parts, nz):
        dma = pltpu.SemaphoreType.DMA
        return [dma((parts, nz)), dma((parts, nz)), dma((parts, nz, 2)), dma((parts, nz, 2, 2)), dma((parts,))]

    def __init__(self, nz, half, out, refs, forward=None, by_x=(0,)):
        self.by_x = by_x
        self.nz, self.half, self.out = nz, half, out
        self.sz, self.sp, self.sq, self.r, self.local = refs
        self.copies, self.locals, self.forward = [], [], forward

    def axes(self, h):
        iz, iy, ix, ic = here()
        across_x, across_y = (iz, iy, 1 - ix, ic), (iz, 1 - iy, ix, ic)
        return (across_y, across_x) if h in self.by_x else (across_x, across_y)

    def block(self, h, z, y, x):
        return self.out.at[z, y, x, pl.ds(h * self.half, self.half)]

    def on(self, h, source, z, y, x, which):
        iz, iy, ix, ic = here()
        p, q = self.axes(h)
        there, got = self.block(h, z, y, x), self.r.at[h, z, y, x]
        if "z" in which:
            for k in range(1, self.nz):
                far = (lax.rem(iz + k, self.nz), iy, ix, ic)
                in_pieces(source, there, self.sz.at[h, k], got, far)
        if "p" in which:
            self.copies.append(send(source, there, self.sp.at[h, z], got, p))
        if "q" in which:
            side = x if h not in self.by_x else y
            self.copies.append(send(source, there, self.sq.at[h, z, side], got, q))
        if self.forward is not None:
            self.forward(h, source, z, y, x)

    def start(self, h, source):
        iz, iy, ix, _ = here()
        copy = pltpu.make_async_copy(source, self.block(h, iz, iy, ix), self.local.at[h])
        copy.start()
        self.locals.append(copy)
        self.on(h, source, iz, iy, ix, "zpq")

    def got(self, h, z, y, x):
        arrived(self.block(h, z, y, x), self.sz.at[h, 0], self.r.at[h, z, y, x], self.axes(h)[0])

    def first(self, h, k):
        iz, iy, ix, _ = here()
        z = lax.rem(iz + k, self.nz)
        self.got(h, z, iy, ix)
        self.on(h, self.block(h, z, iy, ix), z, iy, ix, "pq")

    def second(self, h, k):
        iz, iy, ix, _ = here()
        z = lax.rem(iz + k, self.nz)
        y, x = (1 - iy, ix) if h in self.by_x else (iy, 1 - ix)
        self.got(h, z, y, x)
        self.on(h, self.block(h, z, y, x), z, y, x, "q")

    def third(self, h, k):
        iz, iy, ix, _ = here()
        z = lax.rem(iz + k, self.nz)
        for side in (0, 1):
            if h in self.by_x:
                y, x = (iy if side == 0 else 1 - iy), 1 - ix
            else:
                y, x = 1 - iy, (ix if side == 0 else 1 - ix)
            self.got(h, z, y, x)
            if self.forward is not None:
                self.forward(h, self.block(h, z, y, x), z, y, x)

    def turns(self):
        return [1, self.nz - 1] + [k for k in range(2, self.nz - 1)]

    def firsts(self, parts):
        for h in parts:
            self.second(h, 0)
        for k in self.turns():
            for h in parts:
                self.first(h, k)

    def seconds(self, parts):
        for k in self.turns():
            for h in parts:
                self.second(h, k)

    def thirds(self, parts):
        for k in [0] + self.turns():
            for h in parts:
                self.third(h, k)

    def rest(self):
        self.firsts((0, 1))
        self.seconds((0, 1))
        self.thirds((0, 1))

    def end(self, parts):
        iz, iy, ix, ic = here()
        for copy in self.locals:
            copy.wait()
        for copy in self.copies:
            copy.wait_send()
        for h in parts:
            for k in range(1, self.nz):
                far = (lax.rem(iz + k, self.nz), iy, ix, ic)
                left(self.block(h, iz, iy, ix), self.sz.at[h, k], self.r.at[h, iz, iy, ix], far)


def reduce_gather(nz, half, part, out, refs, finished):
    reduce = Reduce(nz, half, part, refs[:11], BY_X)
    gather = Gather(nz, half, out, refs[11:], None, BY_X)
    greet(neighbours(nz))
    early, late = (0, 1), (2, 3)

    def begin(parts):
        for far in (True, False):
            for h in parts:
                reduce.start(h, far)

    def finish(parts, kept):
        for h in parts:
            gather.start(h, finished(h, reduce.finish(h, kept[h])))

    begin(early)
    for h in early:
        reduce.second(h)
    begin(late)
    kept = {h: reduce.third(h) for h in early}
    for h in late:
        reduce.second(h)
    finish(early, kept)
    kept = {h: reduce.third(h) for h in late}
    gather.firsts(early)
    finish(late, kept)
    gather.seconds(early)
    gather.firsts(late)
    gather.thirds(early)
    gather.seconds(late)
    gather.thirds(late)
    gather.end(early + late)
    reduce.end(early + late)


def forward_kernel(nz, half, part, rows, bias, gain, shift, out, resid, fin, *refs):
    def finished(h, total):
        at = pl.ds(h * half, half)
        total = rows[at].astype(F32) + total + bias[...]
        resid[at] = total
        hat, _ = normed(total)
        fin[h] = (hat * gain[...] + shift[...]).astype(BF16)
        return fin.at[h]

    reduce_gather(nz, half, part, out, refs, finished)


def backward_kernel(nz, half, part, resid, gain, out, vectors, fin, *refs):
    sums = []

    def finished(h, total):
        hat, inverse = normed(resid[pl.ds(h * half, half)])
        dresid = norm_back(total * gain[...], hat, inverse)
        fin[h] = dresid.astype(BF16)
        sums.append([jnp.sum(v, axis=0, keepdims=True) for v in (total * hat, total, dresid)])
        return fin.at[h]

    reduce_gather(nz, half, part, out, refs, finished)
    for i in range(3):
        vectors[pl.ds(i, 1)] = sum(part_sums[i] for part_sums in sums)


def vmem():
    return pl.BlockSpec(memory_space=pltpu.VMEM)


def anywhere():
    return pl.BlockSpec(memory_space=pltpu.HBM)


def busy(us):
    return pl.CostEstimate(flops=0, bytes_accessed=us * 3_000_000, transcendentals=0)


def comm(which, limit=48):
    return pltpu.CompilerParams(collective_id=which, has_side_effects=True, vmem_limit_bytes=limit << 20)


def reduce_norm_gather(nz, part, rows, bias, gain, shift):
    share, width = rows.shape
    half = share // 4
    out, resid = pl.pallas_call(
        functools.partial(forward_kernel, nz, half),
        out_shape=[
            jax.ShapeDtypeStruct((nz, 2, 2, share, width), BF16),
            jax.ShapeDtypeStruct((share, width), F32),
        ],
        in_specs=[vmem()] * 5,
        out_specs=[anywhere(), vmem()],
        scratch_shapes=[pltpu.VMEM((4, half, width), BF16)]
        + Reduce.scratch(4, nz, half, width)
        + Gather.scratch(4, nz),
        cost_estimate=busy(90),
        compiler_params=comm(2, 62),
    )(part.reshape(nz, 2, 2, share, width), rows, bias, gain, shift)
    return out.reshape(4 * nz * share, width), resid


def reduce_back_gather(nz, part, resid, gain):
    share, width = resid.shape
    half = share // 4
    out, vectors = pl.pallas_call(
        functools.partial(backward_kernel, nz, half),
        out_shape=[
            jax.ShapeDtypeStruct((nz, 2, 2, share, width), BF16),
            jax.ShapeDtypeStruct((3, width), F32),
        ],
        in_specs=[vmem()] * 3,
        out_specs=[anywhere(), vmem()],
        scratch_shapes=[pltpu.VMEM((4, half, width), BF16)]
        + Reduce.scratch(4, nz, half, width)
        + Gather.scratch(4, nz),
        cost_estimate=busy(90),
        compiler_params=comm(3, 62),
    )(part.reshape(nz, 2, 2, share, width), resid, gain)
    return out.reshape(4 * nz * share, width), vectors


def merge(a, b):
    top = jnp.maximum(a[0], b[0])
    return (top, a[1] * jnp.exp(a[0] - top) + b[1] * jnp.exp(b[0] - top), a[2] + b[2])


def objective_kernel(
    nz, seqs, seq_total, stats, hot, scored, refs, lens, wanted, coef, lse_out, scalars, held, near, far, s1, r1, s2, r2
):
    iz, iy, ix, ic = here()
    plane = [(iz, iy, 1 - ix, ic), (iz, 1 - iy, ix, ic), (iz, 1 - iy, 1 - ix, ic)]
    line = [(lax.rem(iz + k, nz), iy, ix, c) for c in (ic, 1 - ic) for k in range(nz)][1:]
    greet(plane + line)
    copies = []
    for i, device in enumerate(plane):
        copies.append(send(stats, near.at[iy, ix], s1.at[i], r1.at[iy, ix], device))
    near[iy, ix] = stats[...]
    for _, y, x, _ in plane:
        arrived(near.at[y, x], s1.at[0], r1.at[y, x], plane[0])
    sides = [tuple(near[y, x, i] for i in range(3)) for y in (0, 1) for x in (0, 1)]
    current = merge(merge(sides[0], sides[1]), merge(sides[2], sides[3]))
    for i in range(3):
        held[i] = current[i]
        far[iz, ic, i] = current[i]
    for i, device in enumerate(line):
        copies.append(send(held, far.at[iz, ic], s2.at[i], r2.at[iz, ic], device))
    for z, _, _, c in line:
        arrived(far.at[z, c], s2.at[0], r2.at[z, c], line[0])

    def whole(c):
        total = tuple(far[0, c, i] for i in range(3))
        for z in range(1, nz):
            total = merge(total, tuple(far[z, c, i] for i in range(3)))
        lse = total[0] + jnp.log(total[1])
        return lse, total[2] - lse

    (own_lse, own), (pair_lse, pair) = whole(0), whole(1)
    lse_out[...] = jnp.where(ic == 0, own_lse, pair_lse)

    def means(values, ref):
        terms = (values - ref) * scored[...]
        return [
            jnp.sum(terms * hot[s], axis=1, keepdims=True) / lens[:, s : s + 1] for s in range(seqs)
        ]

    own_means, pair_means = means(own, refs[0]), means(pair, refs[1])
    kl = jnp.sum(sum(pair_means), axis=0, keepdims=True) / seq_total
    loss = jnp.zeros((1, 1), F32)
    slopes = []
    for s in range(seqs):
        sign = 2.0 * wanted[:, s : s + 1] - 1.0
        sigmoid = jax.nn.sigmoid(kto_beta * sign * (own_means[s] - kl))
        slopes.append(-kto_beta * sign * sigmoid * (1.0 - sigmoid))
        loss = loss + jnp.sum(1.0 - sigmoid, axis=0, keepdims=True)
    shared = -jnp.sum(sum(slopes), axis=0, keepdims=True) / seq_total
    total = jnp.zeros_like(own)
    for s in range(seqs):
        value = jnp.where(ic == 0, slopes[s], shared) / lens[:, s : s + 1]
        total = total + hot[s] * value
    coef[...] = total * scored[...]
    scalars[0] = jnp.broadcast_to(loss, scalars.shape[1:])
    scalars[1] = jnp.broadcast_to(kl, scalars.shape[1:])
    for copy in copies:
        copy.wait_send()


def objective(nz, seq_total, stats, hot, scored, refs, lens, wanted):
    shape = scored.shape
    dma = pltpu.SemaphoreType.DMA
    return pl.pallas_call(
        functools.partial(objective_kernel, nz, hot.shape[0], seq_total),
        out_shape=[
            jax.ShapeDtypeStruct(shape, F32),
            jax.ShapeDtypeStruct(shape, F32),
            jax.ShapeDtypeStruct((2, 8, 128), F32),
        ],
        in_specs=[vmem()] * 6,
        out_specs=[vmem()] * 3,
        scratch_shapes=[
            pltpu.VMEM((3,) + shape, F32),
            pltpu.VMEM((2, 2, 3) + shape, F32),
            pltpu.VMEM((nz, 2, 3) + shape, F32),
            dma((3,)),
            dma((2, 2)),
            dma((2 * nz - 1,)),
            dma((nz, 2)),
        ],
        cost_estimate=busy(15),
        compiler_params=comm(4),
    )(stats, hot, scored, refs, lens, wanted)


def diagonal(nz):
    iz, iy, ix, ic = here()
    return [(lax.rem(iz + k, nz), 1 - iy, ix, 1 - ic) for k in range(nz)]


def to_head(nz, k, pairs, local_sem, out_sem, in_sem):
    iz, iy, ix, ic = here()
    z = lax.rem(iz + k, nz)
    device = (z, ic, ix, iy)

    def remote():
        for i, (source, target) in enumerate(pairs):
            send(source, target, out_sem.at[i, z], in_sem.at[i, iz], device)

    if k:
        remote()
        return
    pl.when(iy != ic)(remote)

    @pl.when(iy == ic)
    def _():
        for i, (source, target) in enumerate(pairs):
            copy = pltpu.make_async_copy(source, target, local_sem.at[i])
            copy.start()
            copy.wait()


def from_head(nz, k, targets, out_sem, in_sem):
    iz, iy, ix, ic = here()
    z = lax.rem(iz + k, nz)

    def wait():
        for i, target in enumerate(targets):
            arrived(target, out_sem.at[i, z], in_sem.at[i, z], (z, ic, ix, iy))

    if k:
        wait()
    else:
        pl.when(iy != ic)(wait)


def sent_head(nz, k, sources, out_sem, in_sem):
    iz, iy, ix, ic = here()
    z = lax.rem(iz + k, nz)

    def wait():
        for i, source in enumerate(sources):
            pltpu.make_async_remote_copy(
                src_ref=source,
                dst_ref=source,
                send_sem=out_sem.at[i, z],
                recv_sem=in_sem.at[i, z],
                device_id=(z, ic, ix, iy),
                device_id_type=pl.DeviceIdType.MESH,
            ).wait_send()

    if k:
        wait()
    else:
        pl.when(iy != ic)(wait)


def lanes(index, size):
    return pl.ds(pl.multiple_of(index * size, size), size)


def front_kernel(
    nz,
    half,
    residual,
    info,
    bias,
    joined_in,
    dense_in,
    down_in,
    up_in,
    vocab_in,
    natural,
    info_out,
    bias_out,
    joined_out,
    out_all,
    up_all,
    vocab_out,
    vocab_here,
    vs,
    fs,
    fr,
    js,
    jr,
    jl,
    cs,
    cr,
    ms,
    mr,
    zs,
    zr,
    ps,
    ds,
    dr,
    dl,
    es,
    er,
    *refs,
):
    iz, iy, ix, ic = here()
    core = other_core()
    across = [(lax.rem(iz + k, nz), 1 - iy, ix, ic) for k in range(nz)]
    greet(neighbours(nz) + [core] + diagonal(nz) + across[1:])
    depth = joined_in.shape[0]
    cols = joined_out.shape[1]
    heads = dense_in.shape[0] // nz
    units = down_in.shape[0] // (2 * nz)
    dense_out = out_all.at[pl.ds(0, heads)]
    down_out, down_other = (out_all.at[pl.ds(heads + i * units, units)] for i in (0, 1))
    copies = []

    def rows_of(h, z, y, x, c):
        return natural.at[z, y, x, c, pl.ds(h * half, half)]

    def forward(h, source, z, y, x):
        send(source, rows_of(h, z, y, x, ic), fs.at[h, z, y, x], fr.at[h, z, y, x], core)

    class Rows(Gather):
        def block(self, h, z, y, x):
            return rows_of(h, z, y, x, ic)

    fetch = pltpu.make_async_copy(vocab_in, vocab_here, vs.at[0])
    fetch.start()
    gather = Rows(nz, half, natural, refs, forward)
    first = pl.multiple_of((ix * 2 + ic) * 2 * half, 2 * half)
    for h in (0, 1):
        gather.start(h, residual.at[pl.ds(first + h * half, half)])

    copies.append(send(bias, bias_out, ms.at[0], mr.at[0], core))
    info_out[iz, iy] = info[...]
    across_y = (iz, 1 - iy, ix, ic)
    for k in range(1, nz):
        far = (lax.rem(iz + k, nz), iy, ix, ic)
        copies.append(send(info, info_out.at[iz, iy], zs.at[k], zr.at[iz, iy], far))
    copies.append(send(info, info_out.at[iz, iy], ps.at[iz], zr.at[iz, iy], across_y))

    mine = iz * 2 + iy
    for k in list(range(1, nz)) + [0]:
        z = lax.rem(iz + k, nz)
        to_head(
            nz,
            k,
            [
                (joined_in.at[:, lanes(z, cols)], joined_out.at[lanes(mine, depth)]),
                (dense_in.at[lanes(z, heads)], dense_out.at[:, lanes(mine, depth)]),
            ],
            jl,
            js,
            jr,
        )

    for k in range(1, nz):
        z = lax.rem(iz + k, nz)
        arrived(info_out.at[z, iy], zs.at[k], zr.at[z, iy], across_y)
        copies.append(send(info_out.at[z, iy], info_out.at[z, iy], ps.at[z], zr.at[z, iy], across_y))

    gather.firsts((0, 1))

    def own_units(d):
        rows, own, other = lanes(d, depth), pl.ds(0, units), pl.ds(units, units)
        return [
            (up_all.at[rows, own], up_all.at[rows, other]),
            (down_out.at[:, rows], down_other.at[:, rows]),
        ]

    line = [(lax.rem(iz + k, nz), iy, ix, ic) for k in range(1, nz)]
    keep = []
    for i, source in enumerate((up_in.at[:, lanes(mine, units)], down_in.at[lanes(mine, units)])):
        copy = pltpu.make_async_copy(source, own_units(mine)[i][0], dl.at[i])
        copy.start()
        keep.append(copy)
    for i in (0, 1):
        for device in line + across:
            d = device[0] * 2 + device[1]
            source = up_in.at[:, lanes(d, units)] if i == 0 else down_in.at[lanes(d, units)]
            copies.append(send(source, own_units(mine)[i][0], ds.at[i, d], dr.at[i, mine], device))
    gather.seconds((0, 1))
    gather.thirds((0, 1))

    fetch.wait()

    def across_block(i, carry):
        at = lanes(i, depth)
        vocab_out[at] = vocab_here[:, at].T
        return carry

    lax.fori_loop(0, vocab_in.shape[1] // depth, across_block, 0)

    def head_parts(z, side):
        d = z * 2 + side
        return joined_out.at[lanes(d, depth)], dense_out.at[:, lanes(d, depth)]

    for k in [0] + list(range(1, nz)):
        z = lax.rem(iz + k, nz)
        parts = head_parts(z, ic)
        from_head(nz, k, parts, js, jr)
        for i, part in enumerate(parts):
            copies.append(send(part, part, cs.at[i, z], cr.at[i, z], core))
    for copy in keep:
        copy.wait()
    for i in (0, 1):
        for device in [None] + line + across:
            d = mine if device is None else device[0] * 2 + device[1]
            block, other = own_units(d)[i]
            if device is not None:
                arrived(block, ds.at[i, d], dr.at[i, d], device)
            copies.append(send(block, other, es.at[i, d], er.at[i, d], core))
        for d in range(2 * nz):
            arrived(own_units(d)[i][1], es.at[i, d], er.at[i, d], core)
    for k in range(nz):
        z = lax.rem(iz + k, nz)
        arrived(info_out.at[z, 1 - iy], ps.at[z], zr.at[z, 1 - iy], across_y)
    for z in range(nz):
        for y in (0, 1):
            for x in (0, 1):
                for h in (0, 1):
                    arrived(rows_of(h, z, y, x, 1 - ic), fs.at[h, z, y, x], fr.at[h, z, y, x], core)
                    left(rows_of(h, z, y, x, ic), fs.at[h, z, y, x], fr.at[h, z, y, x], core)
    for z in range(nz):
        for i, part in enumerate(head_parts(z, 1 - ic)):
            arrived(part, cs.at[i, z], cr.at[i, z], core)
    arrived(bias_out, ms.at[0], mr.at[0], core)
    gather.end((0, 1))
    for k in range(nz):
        z = lax.rem(iz + k, nz)
        sent_head(nz, k, [joined_in.at[:, lanes(z, cols)], dense_in.at[lanes(z, heads)]], js, jr)
    for copy in copies:
        copy.wait_send()


def front(nz, residual, info, bias, joined_in, dense_in, down_in, up_in, vocab_in):
    held, width = residual.shape
    half = held // 8
    depth, cols = joined_in.shape[0], joined_in.shape[1] // nz
    heads = dense_in.shape[0] // nz
    units = down_in.shape[0] // (2 * nz)
    dma = pltpu.SemaphoreType.DMA
    outs = pl.pallas_call(
        functools.partial(front_kernel, nz, half),
        out_shape=[
            jax.ShapeDtypeStruct((nz, 2, 2, 2, 2 * half, width), BF16),
            jax.ShapeDtypeStruct((nz, 2) + info.shape, F32),
            jax.ShapeDtypeStruct(bias.shape, F32),
            jax.ShapeDtypeStruct((2 * nz * depth, cols), BF16),
            jax.ShapeDtypeStruct((heads + 2 * units, 2 * nz * depth), BF16),
            jax.ShapeDtypeStruct((2 * nz * depth, 2 * units), BF16),
            jax.ShapeDtypeStruct(vocab_in.shape[::-1], BF16),
        ],
        in_specs=[anywhere(), vmem(), vmem(), anywhere(), anywhere(), anywhere(), anywhere(), anywhere()],
        out_specs=[anywhere(), vmem(), vmem(), anywhere(), anywhere(), anywhere(), vmem()],
        scratch_shapes=[
            pltpu.VMEM(vocab_in.shape, BF16),
            dma((1,)),
            dma((2, nz, 2, 2)),
            dma((2, nz, 2, 2)),
            dma((2, nz)),
            dma((2, nz)),
            dma((2,)),
            dma((2, nz)),
            dma((2, nz)),
            dma((1,)),
            dma((1,)),
            dma((nz,)),
            dma((nz, 2)),
            dma((nz,)),
            dma((2, 2 * nz)),
            dma((2, 2 * nz)),
            dma((2,)),
            dma((2, 2 * nz)),
            dma((2, 2 * nz)),
        ]
        + Gather.scratch(2, nz),
        cost_estimate=busy(45),
        compiler_params=comm(1, 62),
    )(residual, info, bias, joined_in, dense_in, down_in, up_in, vocab_in)
    natural = outs[0].reshape(8 * nz * 2 * half, width)
    return natural, outs[1].reshape((2 * nz,) + info.shape), outs[2], outs[3], outs[4], outs[5], outs[6]


def end_kernel(
    nz,
    half,
    part,
    mine_rows,
    other_rows,
    rows,
    vectors,
    keep,
    give,
    joined_in,
    dense_in,
    rows_out,
    vectors_out,
    bias_out,
    joined_out,
    dense_out,
    merged,
    came,
    rows_in,
    vector_in,
    vector_sum,
    give_in,
    joined_came,
    joined_sum,
    dense_came,
    dense_sum,
    ms,
    mr,
    vs,
    vr,
    bs,
    br,
    bp,
    js,
    jr,
    jl,
    cs,
    cr,
    os,
    orr,
    *refs,
):
    iz, iy, ix, ic = here()
    core = other_core()
    across_x, across_y = (iz, iy, 1 - ix, ic), (iz, 1 - iy, ix, ic)
    greet(neighbours(nz) + [core] + diagonal(nz))
    reduce = Reduce(nz, half, merged, refs, END_BY_X)
    copies = []
    depth = joined_in.shape[0] // (2 * nz)
    cols = joined_in.shape[1]
    heads = dense_in.shape[0]
    groups = [(1 - iy, 1 - ix), (iy, 1 - ix), (1 - iy, ix), (iy, ix)]

    for y, x in groups:
        for k in list(range(1, nz)) + [0]:
            z = lax.rem(iz + k, nz)
            copies.append(
                send(part.at[z, y, x, 1 - ic], came.at[z, y, x], ms.at[z, y, x], mr.at[z, y, x], core)
            )
    copies.append(send(vectors, vector_in.at[0], vs.at[0], vr.at[0], core))
    copies.append(send(give, give_in, bs.at[0], br.at[nz, 0], core))
    copies.append(send(other_rows, rows_in, os.at[0], orr.at[0], core))
    for k in range(nz):
        z = lax.rem(iz + k, nz)
        theirs = z * 2 + 1 - ic
        copies.append(
            send(joined_in.at[lanes(theirs, depth)], joined_came.at[z], cs.at[0, z], cr.at[0, z], core)
        )
        copies.append(
            send(dense_in.at[:, lanes(theirs, depth)], dense_came.at[z], cs.at[1, z], cr.at[1, z], core)
        )

    def merge_group(y, x):
        for k in list(range(1, nz)) + [0]:
            z = lax.rem(iz + k, nz)
            arrived(came.at[z, y, x], ms.at[z, y, x], mr.at[z, y, x], core)
            merged[z, y, x] = (part[z, y, x, ic].astype(F32) + came[z, y, x].astype(F32)).astype(BF16)

    merge_group(*groups[0])
    reduce.start(0, True)
    merge_group(*groups[1])
    reduce.start(0, False)
    merge_group(*groups[2])
    reduce.start(1, True)
    reduce.start(1, False)
    merge_group(*groups[3])

    arrived(vector_in.at[0], vs.at[0], vr.at[0], core)
    vector_sum[0] = vectors[...] + vector_in[0]
    copies.append(send(vector_sum.at[0], vector_in.at[1], vs.at[1], vr.at[1], across_x))
    arrived(give_in, bs.at[0], br.at[nz, 0], core)
    bias_out[iz, iy] = keep[...] + give_in[...]
    for k in range(1, nz):
        far = (lax.rem(iz + k, nz), iy, ix, ic)
        copies.append(send(bias_out.at[iz, iy], bias_out.at[iz, iy], bs.at[k], br.at[iz, iy], far))
    copies.append(send(bias_out.at[iz, iy], bias_out.at[iz, iy], bp.at[iz], br.at[iz, iy], across_y))

    for k in list(range(1, nz)) + [0]:
        z = lax.rem(iz + k, nz)
        ours = z * 2 + ic
        arrived(joined_came.at[z], cs.at[0, z], cr.at[0, z], core)
        joined_sum[z] = (joined_in[lanes(ours, depth)].astype(F32) + joined_came[z].astype(F32)).astype(BF16)
        arrived(dense_came.at[z], cs.at[1, z], cr.at[1, z], core)
        dense_sum[z] = (dense_in[:, lanes(ours, depth)].astype(F32) + dense_came[z].astype(F32)).astype(BF16)
        to_head(
            nz,
            k,
            [
                (joined_sum.at[z], joined_out.at[:, lanes(iz, cols)]),
                (dense_sum.at[z], dense_out.at[lanes(iz, heads)]),
            ],
            jl,
            js,
            jr,
        )

    for h in (0, 1):
        reduce.second(h)
    arrived(vector_in.at[1], vs.at[1], vr.at[1], across_x)
    vector_sum[1] = vector_sum[0] + vector_in[1]
    copies.append(send(vector_sum.at[1], vector_in.at[2], vs.at[2], vr.at[2], across_y))
    for k in range(1, nz):
        z = lax.rem(iz + k, nz)
        arrived(bias_out.at[z, iy], bs.at[k], br.at[z, iy], across_y)
        copies.append(send(bias_out.at[z, iy], bias_out.at[z, iy], bp.at[z], br.at[z, iy], across_y))
    kept = [reduce.third(h) for h in (0, 1)]
    arrived(vector_in.at[2], vs.at[2], vr.at[2], across_y)
    vector_sum[2] = vector_sum[1] + vector_in[2]
    for k in range(1, nz):
        far = (lax.rem(iz + k, nz), iy, ix, ic)
        copies.append(send(vector_sum.at[2], vector_in.at[3 + iz], vs.at[2 + k], vr.at[3 + iz], far))
    vector_in[3 + iz] = vector_sum[2]
    arrived(rows_in, os.at[0], orr.at[0], core)
    for h in (0, 1):
        at = pl.ds(h * half, half)
        hat, inverse = normed(rows[at].astype(F32))
        back = norm_back(reduce.finish(h, kept[h]), hat, inverse)
        block = rows_out.at[ix, ic, at]
        rows_out[ix, ic, at] = (
            mine_rows[at].astype(F32) + rows_in[at].astype(F32) + back
        ).astype(BF16)
        copies.append(send(block, block, os.at[1 + h], orr.at[1 + h], across_x))
        copies.append(send(block, block, os.at[3 + h], orr.at[3 + h], core))
    for h in (0, 1):
        block = rows_out.at[1 - ix, ic, pl.ds(h * half, half)]
        arrived(block, os.at[1 + h], orr.at[1 + h], across_x)
        copies.append(send(block, block, os.at[5 + h], orr.at[5 + h], core))
    for k in range(1, nz):
        z = lax.rem(iz + k, nz)
        arrived(vector_in.at[3 + z], vs.at[2 + k], vr.at[3 + z], (z, iy, ix, ic))
    total = vector_in[3]
    for z in range(1, nz):
        total = total + vector_in[3 + z]
    vectors_out[...] = total
    for k in range(nz):
        z = lax.rem(iz + k, nz)
        arrived(bias_out.at[z, 1 - iy], bp.at[z], br.at[z, 1 - iy], across_y)
        from_head(
            nz, k, [joined_out.at[:, lanes(z, cols)], dense_out.at[lanes(z, heads)]], js, jr
        )
        sent_head(nz, k, [joined_sum.at[z], dense_sum.at[z]], js, jr)
    for h in (0, 1):
        at = pl.ds(h * half, half)
        arrived(rows_out.at[ix, 1 - ic, at], os.at[3 + h], orr.at[3 + h], core)
        arrived(rows_out.at[1 - ix, 1 - ic, at], os.at[5 + h], orr.at[5 + h], core)
    reduce.end((0, 1))
    for copy in copies:
        copy.wait_send()


def end(nz, part, mine_rows, other_rows, rows, vectors, keep, give, joined_in, dense_in):
    share, width = rows.shape
    half = share // 2
    depth, cols, heads = joined_in.shape[0] // (2 * nz), joined_in.shape[1], dense_in.shape[0]
    dma = pltpu.SemaphoreType.DMA
    return pl.pallas_call(
        functools.partial(end_kernel, nz, half),
        out_shape=[
            jax.ShapeDtypeStruct((2, 2, share, width), BF16),
            jax.ShapeDtypeStruct(vectors.shape, F32),
            jax.ShapeDtypeStruct((nz, 2) + keep.shape, F32),
            jax.ShapeDtypeStruct((depth, nz * cols), BF16),
            jax.ShapeDtypeStruct((nz * heads, depth), BF16),
        ],
        in_specs=[vmem()] * 9,
        out_specs=[vmem(), vmem(), vmem(), vmem(), vmem()],
        scratch_shapes=[
            pltpu.VMEM((nz, 2, 2, share, width), BF16),
            pltpu.VMEM((nz, 2, 2, share, width), BF16),
            pltpu.VMEM((share, width), BF16),
            pltpu.VMEM((3 + nz,) + vectors.shape, F32),
            pltpu.VMEM((3,) + vectors.shape, F32),
            pltpu.VMEM(keep.shape, F32),
            pltpu.VMEM((nz, depth, cols), BF16),
            pltpu.VMEM((nz, depth, cols), BF16),
            pltpu.VMEM((nz, heads, depth), BF16),
            pltpu.VMEM((nz, heads, depth), BF16),
            dma((nz, 2, 2)),
            dma((nz, 2, 2)),
            dma((2 + nz,)),
            dma((3 + nz,)),
            dma((nz,)),
            dma((nz + 1, 2)),
            dma((nz,)),
            dma((2, nz)),
            dma((2, nz)),
            dma((2,)),
            dma((2, nz)),
            dma((2, nz)),
            dma((7,)),
            dma((7,)),
        ]
        + Reduce.scratch(2, nz, half, width),
        cost_estimate=busy(70),
        compiler_params=comm(5),
    )(part, mine_rows, other_rows, rows, vectors, keep, give, joined_in, dense_in)


def turned(values, cosine, low, high):
    half_rot = ROT // 2
    return (
        values * cosine
        + pltpu.roll(values, values.shape[1] - half_rot, 1) * low
        + pltpu.roll(values, half_rot, 1) * high
    )


def block_rows(order, ref, piece, first, count):
    return jnp.concatenate(
        [ref[pl.ds(pl.multiple_of(order[first + i] * piece, piece), piece), :] for i in range(count)], axis=0
    )


def attention_kernel(piece, order, fused, tables, allowed, qkv, probs_out, mixed):
    groups, held = allowed.shape[0], allowed.shape[1]
    per = held // piece
    for g in range(groups):
        at = pl.ds(g * held, held)
        rows = block_rows(order, fused, piece, g * per, per)
        turn_by = [tables[i, at] for i in range(3)]
        query = turned(rows[:, :HD], *turn_by).astype(BF16)
        keys = turned(rows[:, HD : 2 * HD], *turn_by).astype(BF16)
        values = rows[:, 2 * HD :].astype(BF16)
        qkv[at, :HD] = query
        qkv[at, HD : 2 * HD] = keys
        qkv[at, 2 * HD :] = values
        scores = jnp.where(allowed[g] > 0.5, dot(query, keys, (1, 1)) / math.sqrt(HD), masked_score)
        weights = jnp.exp(scores - jnp.max(scores, axis=-1, keepdims=True))
        probs = weights / jnp.sum(weights, axis=-1, keepdims=True)
        probs_out[g] = probs
        mixed[at] = dot(probs.astype(BF16), values, (1, 0)).astype(BF16)


def attention(order, fused, tables, allowed, piece):
    total = fused.shape[0]
    return pl.pallas_call(
        functools.partial(attention_kernel, piece),
        out_shape=[
            jax.ShapeDtypeStruct((total, 3 * HD), BF16),
            jax.ShapeDtypeStruct(allowed.shape, F32),
            jax.ShapeDtypeStruct((total, HD), BF16),
        ],
        in_specs=[pl.BlockSpec(memory_space=pltpu.SMEM)] + [vmem()] * 3,
        out_specs=[vmem()] * 3,
        compiler_params=pltpu.CompilerParams(vmem_limit_bytes=32 << 20),
    )(order, fused, tables, allowed)


def place_kernel(piece, order, mixed, active, out):
    per = 2
    out[:, :HD] = mixed[...]
    for g in range(mixed.shape[0] // (per * piece)):
        out[pl.ds(g * per * piece, per * piece), HD:] = block_rows(order, active, piece, g * per, per)


def place(order, mixed, active, piece):
    total = mixed.shape[0]
    return pl.pallas_call(
        functools.partial(place_kernel, piece),
        out_shape=jax.ShapeDtypeStruct((total, HD + active.shape[1]), BF16),
        in_specs=[pl.BlockSpec(memory_space=pltpu.SMEM)] + [vmem()] * 2,
        out_specs=vmem(),
        compiler_params=pltpu.CompilerParams(vmem_limit_bytes=32 << 20),
    )(order, mixed, active)


def attention_back_kernel(
    piece, order, dbranch, wout, slope, qkv, probs_in, tables, dfused, dhidden, sums, douts
):
    tile = 4 * piece

    def back(i, carry):
        at = pl.ds(pl.multiple_of(i * tile, tile), tile)
        douts[at] = dot(dbranch[at], wout[...], (1, 1))
        return carry

    lax.fori_loop(0, dbranch.shape[0] // tile, back, 0)
    groups, held = probs_in.shape[0], probs_in.shape[1]
    per = held // piece
    joined_sum = jnp.zeros((1, 3 * HD), F32)
    hidden_sum = jnp.zeros((1, slope.shape[1]), F32)
    for g in range(groups):
        at = pl.ds(g * held, held)
        query, keys, values = qkv[at, :HD], qkv[at, HD : 2 * HD], qkv[at, 2 * HD :]
        dmixed = douts[at, :HD].astype(BF16)
        probs = probs_in[g]
        dvalues = dot(probs.astype(BF16), dmixed, (0, 0))
        dprobs = dot(dmixed, values, (1, 1))
        dscores = (probs * (dprobs - jnp.sum(probs * dprobs, axis=-1, keepdims=True))).astype(BF16)
        turn_by = [tables[0, at], -tables[1, at], -tables[2, at]]
        dquery = turned(dot(dscores, keys, (1, 0)) / math.sqrt(HD), *turn_by)
        dkeys = turned(dot(dscores, query, (0, 0)) / math.sqrt(HD), *turn_by)
        whole = jnp.concatenate([dquery, dkeys, dvalues], axis=1).astype(BF16)
        joined_sum = joined_sum + jnp.sum(whole.astype(F32), axis=0, keepdims=True)
        for i in range(per):
            to = pl.ds(pl.multiple_of(order[g * per + i] * piece, piece), piece)
            dfused[to, :] = whole[i * piece : (i + 1) * piece]
            grown = (douts[pl.ds(g * held + i * piece, piece), HD:] * slope[to, :]).astype(BF16)
            dhidden[to, :] = grown
            hidden_sum = hidden_sum + jnp.sum(grown.astype(F32), axis=0, keepdims=True)
    sums[:, : 3 * HD] = joined_sum
    sums[:, 3 * HD :] = hidden_sum


def attention_back(order, dbranch, wout, slope, qkv, probs, tables, piece):
    total, units = slope.shape
    return pl.pallas_call(
        functools.partial(attention_back_kernel, piece),
        out_shape=[
            jax.ShapeDtypeStruct((total, 3 * HD), BF16),
            jax.ShapeDtypeStruct((total, units), BF16),
            jax.ShapeDtypeStruct((1, 3 * HD + units), F32),
        ],
        in_specs=[pl.BlockSpec(memory_space=pltpu.SMEM)] + [vmem()] * 6,
        out_specs=[vmem()] * 3,
        scratch_shapes=[pltpu.VMEM((total, wout.shape[0]), F32)],
        cost_estimate=pl.CostEstimate(flops=0, bytes_accessed=1000, transcendentals=0),
        compiler_params=pltpu.CompilerParams(vmem_limit_bytes=48 << 20),
    )(order, dbranch, wout, slope, qkv, probs, tables)


def fast_shards(
    residual,
    lengths,
    pair_order,
    token_ids,
    desirable,
    ref_match,
    ref_pair,
    attn_gain,
    attn_shift,
    mlp_gain,
    mlp_shift,
    w_joined,
    b_joined,
    w_dense,
    b_dense,
    w_up,
    b_up,
    w_down,
    b_down,
    final_gain,
    final_shift,
    w_vocab,
):
    nz, ny, nx = lax.axis_size("z"), lax.axis_size("y"), lax.axis_size("x")
    n = nz * ny
    chips = n * nx
    iz, iy, ix, ic = (lax.axis_index(a) for a in ALL)
    dp = iz * ny + iy
    held, width = residual.shape
    total = n * held
    blocks = 2 * n
    piece = held // 2
    seqs = lengths.shape[1]
    depth = width // n
    vcols = w_vocab.shape[1] // n
    ffs = w_up.shape[1] // n
    hcols = 3 * HD
    mine = ix * 2 + ic

    info = jnp.stack(
        [
            token_ids.astype(F32),
            ref_match,
            ref_pair,
            jnp.concatenate(
                [lengths[0].astype(F32), desirable.astype(F32), jnp.zeros((held - 2 * seqs,), F32)]
            ),
        ]
    )
    bias_own = jnp.concatenate([b_joined, b_up]).astype(F32)
    natural, info, bias_other, wj, wout, wup, vocab_across = front(
        nz, residual, info, bias_own.reshape(-1, HD), w_joined, w_dense, w_down, w_up, w_vocab
    )
    bias_other = bias_other.reshape(-1)

    send_vocab = vocab_across.reshape(n, vcols, depth)
    vocab_got = exchange(send_vocab)
    bias_first = jnp.where(ic == 0, bias_own, bias_other)
    bias_second = jnp.where(ic == 0, bias_other, bias_own)
    bj_all = jnp.where(iy == 0, bias_first, bias_second)[: nz * hcols].reshape(nz, hcols)
    bj = lax.dynamic_index_in_dim(bj_all, iz, 0, keepdims=False)
    bu_all = jnp.stack([bias_own[nz * hcols :], bias_other[nz * hcols :]]).reshape(2, n, ffs)
    bu = lax.dynamic_index_in_dim(bu_all, dp, 1, keepdims=False).reshape(2 * ffs)

    ids = info[:, 0].astype(jnp.int32)
    refs = jnp.stack([info[:, 1], info[:, 2]])
    lens = info[:, 3, :seqs].astype(jnp.int32)
    wanted = info[:, 3, seqs : 2 * seqs]
    slots = jnp.arange(blocks, dtype=jnp.int32)
    anchor = jnp.sum(
        jnp.where(pair_order[None, :] == slots[:, None], slots[None, :], 0), axis=1
    )
    order = jnp.where(ic == 0, slots, anchor)
    back = jnp.where(ic == 0, slots, pair_order)
    anchor_hot = (anchor[:, None] == slots[None, :])[:, :, None]
    pair_ids = jnp.sum(jnp.where(anchor_hot, ids.reshape(1, blocks, piece), 0), axis=1).reshape(n, held)
    all_ids = jnp.stack([ids, pair_ids])

    ends = jnp.stack([jnp.sum(lens[:, : s + 1], axis=1) for s in range(seqs)], axis=1)
    starts = ends - lens
    places = jnp.arange(held, dtype=jnp.int32)
    segment = jnp.sum((places[None, :, None] >= ends[:, None, :]).astype(jnp.int32), axis=2)
    hot = (segment[:, :, None] == jnp.arange(seqs, dtype=jnp.int32)).astype(F32)
    position = places[None, :] - jnp.sum(hot * starts[:, None, :].astype(F32), axis=2).astype(jnp.int32)
    allowed = (segment[:, :, None] == segment[:, None, :]) & (places[None, :, None] >= places[None, None, :])
    scored = jnp.concatenate(
        [segment[:, 1:] == segment[:, :-1], jnp.zeros((n, 1), jnp.bool_)], axis=1
    ).astype(F32)
    targets = jnp.concatenate([all_ids[:, :, 1:], jnp.zeros((2, n, 1), jnp.int32)], axis=2)

    hat, inverse = normed(natural.astype(F32))
    ga, sa, gm, sm, gf, sf = (
        v.astype(F32) for v in (attn_gain, attn_shift, mlp_gain, mlp_shift, final_gain, final_shift)
    )
    attn_low = (hat * ga + sa).astype(BF16)
    mlp_low = (hat * gm + sm).astype(BF16)
    lane = jnp.arange(HD, dtype=jnp.int32)
    frequency = jnp.exp((lane % (ROT // 2)).astype(F32) * (-2.0 * math.log(10000.0) / ROT))
    angles = position.reshape(total)[:, None].astype(F32) * frequency[None, :]
    cosine = jnp.where(lane < ROT, jnp.cos(angles), 1.0)
    sine = jnp.sin(angles)
    tables = jnp.stack(
        [
            cosine,
            jnp.where(lane < ROT // 2, -sine, 0.0),
            jnp.where((lane >= ROT // 2) & (lane < ROT), sine, 0.0),
        ]
    )
    fused = dot(attn_low, wj, (1, 0)) + bj
    qkv, probs, mixed = attention(order, fused, tables, allowed.astype(F32), piece)
    hidden = dot(mlp_low, wup, (1, 0)) + bu
    bell = 0.5 * (1.0 + lax.erf(hidden * math.sqrt(0.5)))
    active = (hidden * bell).astype(BF16)
    gelu_slope = bell + hidden * jnp.exp(-0.5 * hidden * hidden) * (1.0 / math.sqrt(2.0 * math.pi))
    outs_low = place(order, mixed, active, piece)
    branch_part = dot(outs_low, wout, (1, 0)).astype(BF16)
    share = total // chips
    chip = dp * nx + ix
    first_row = jnp.sum(jnp.where(slots == chip * share // piece, order, 0)) * piece + chip * share % piece
    rows_here = lax.dynamic_slice_in_dim(natural, first_row, share, 0)
    bias_out = (b_dense.astype(F32) + b_down.astype(F32))[None]
    final, resid = reduce_norm_gather(nz, branch_part, rows_here, bias_out, gf[None], sf[None])

    vocab_got, final = lax.optimization_barrier((vocab_got, final))
    vocab_own = vocab_got.transpose(1, 0, 2).reshape(vcols, width)
    vocab_other = swap(vocab_got).transpose(1, 0, 2).reshape(vcols, width)
    my_targets = jnp.where(ic == 0, targets[0], targets[1]).reshape(total)
    logits = [dot(final, w, (1, 1)) for w in (vocab_own, vocab_other)]
    hits = [
        lax.broadcasted_iota(jnp.int32, (total, vcols), 1)
        == (my_targets - ((ix * 2 + core) * n + dp) * vcols)[:, None]
        for core in (ic, 1 - ic)
    ]
    tops = [jnp.max(part, axis=1) for part in logits]
    top = jnp.maximum(tops[0], tops[1])
    sums = sum(jnp.sum(jnp.exp(part - top[:, None]), axis=1) for part in logits)
    picks = sum(jnp.sum(jnp.where(h, part, 0.0), axis=1) for h, part in zip(hits, logits))
    stats = jnp.stack([top, sums, picks]).reshape(3, n, held)
    coef, my_lse, scalars = objective(
        nz, n * seqs, stats, hot.transpose(2, 0, 1), scored, refs, lens.astype(F32), wanted
    )
    coef, my_lse = coef.reshape(total), my_lse.reshape(total)
    kto_loss, kl_estimate = scalars[0, 0, 0], scalars[1, 0, 0]

    dlogits = [
        (coef[:, None] * (jnp.where(h, 1.0, 0.0) - jnp.exp(part - my_lse[:, None]))).astype(BF16)
        for h, part in zip(hits, logits)
    ]
    gv_other = dot(dlogits[1], final, (0, 0)).astype(BF16)
    dfinal_other = dot(dlogits[1], vocab_other, (1, 0)).astype(F32)
    gv_own = dot(dlogits[0], final, (0, 0))
    gv = (gv_own + swap(gv_other).astype(F32)).astype(BF16)
    gv, dlogits_own = lax.optimization_barrier((gv, dlogits[0]))
    dfinal_part = (dot(dlogits_own, vocab_own, (1, 0)) + dfinal_other).astype(BF16)
    gv = gv.reshape(vcols, n, depth).transpose(1, 0, 2)
    early_cols = vcols * 368 // 800
    grad_early = exchange(gv[:, :early_cols])
    dbranch, final_vectors = reduce_back_gather(nz, dfinal_part, resid, gf[None])
    gv_late, dbranch, grad_early = lax.optimization_barrier((gv[:, early_cols:], dbranch, grad_early))
    grad_late = exchange(gv_late)
    grad_vocab = jnp.concatenate([grad_early, grad_late], axis=1).reshape(n * vcols, depth).T
    grad_vocab = with_layout_constraint(lax.optimization_barrier(grad_vocab).astype(F32), Layout((0, 1)))

    dfused, dhidden, bias_sums = attention_back(
        order, dbranch, wout, gelu_slope, qkv, probs, tables, piece
    )
    dhidden, outs_low = lax.optimization_barrier((dhidden, outs_low))
    gout = dot(outs_low, dbranch, (0, 0))
    gu = dot(mlp_low, dhidden, (0, 0))

    def to_send(up, down):
        return jnp.concatenate(
            [up.reshape(n, depth, ffs), down.reshape(ffs, n, depth).transpose(1, 0, 2)], axis=1
        )

    give_grads = to_send(gu[:, ffs:].astype(BF16), gout[HD + ffs :].astype(BF16))
    layer_grads = to_send(gu[:, :ffs], gout[HD : HD + ffs]) + swap(give_grads).astype(F32)
    layer_grads, dfused, dhidden = lax.optimization_barrier((layer_grads.astype(BF16), dfused, dhidden))
    layer_grads = exchange(layer_grads)
    gj = dot(attn_low, dfused, (0, 0)).astype(BF16)
    dattn = dot(dfused, wj, (1, 1))
    dmlp = dot(dhidden, wup, (1, 1))
    g_attn_gain = jnp.sum(dattn * hat, axis=0)
    g_attn_shift = jnp.sum(dattn, axis=0)
    g_mlp_gain = jnp.sum(dmlp * hat, axis=0)
    g_mlp_shift = jnp.sum(dmlp, axis=0)
    t_part = (dattn * ga + dmlp * gm).astype(BF16)
    grad_up = layer_grads[:, :depth].transpose(1, 0, 2).reshape(depth, n * ffs).astype(F32)
    grad_down = layer_grads[:, depth:].reshape(n * ffs, depth).astype(F32)

    share2 = total // (2 * chips)

    def natural_rows(core):
        first = dp * held + (ix * 2 + core) * share2
        place = jnp.sum(jnp.where(slots == first // piece, back, 0)) * piece + first % piece
        return lax.dynamic_slice_in_dim(dbranch, place, share2, 0)

    gbj, gbu = bias_sums[0, :hcols], bias_sums[0, hcols:]
    spare = jnp.zeros((8 * HD - hcols - ffs,), F32)
    keep = jnp.concatenate([gbj, gbu[:ffs], spare]).reshape(8, HD)
    give = jnp.concatenate([gbj, gbu[ffs:], spare]).reshape(8, HD)
    vectors = jnp.concatenate(
        [
            jnp.stack([g_attn_gain, g_attn_shift, g_mlp_gain, g_mlp_shift]),
            final_vectors,
            jnp.zeros((1, width), F32),
        ]
    )
    grad_vocab, t_part = lax.optimization_barrier((grad_vocab, t_part))
    rows_out, vectors, biases, grad_joined, grad_dense = end(
        nz,
        t_part.reshape(nz, 2, 2, 2, share2, width),
        natural_rows(ic),
        natural_rows(1 - ic),
        lax.dynamic_slice_in_dim(residual, mine * share2, share2, 0),
        vectors,
        keep,
        give,
        gj,
        gout[:HD].astype(BF16),
    )
    grad_input = rows_out.reshape(held, width).astype(F32)
    grad_joined, grad_dense = grad_joined.astype(F32), grad_dense.astype(F32)
    g_attn_gain, g_attn_shift, g_mlp_gain, g_mlp_shift, g_final_gain, g_final_shift, g_out = vectors[:7]
    biases = biases.reshape(nz, 2, 8 * HD)
    gb_joined = jnp.where(ic == 0, biases[:, 0, :hcols], biases[:, 1, :hcols]).reshape(nz * hcols)
    gb_up = biases[:, :, hcols : hcols + ffs].reshape(n * ffs)
    return (
        kto_loss,
        kl_estimate,
        grad_input,
        g_attn_gain,
        g_attn_shift,
        g_mlp_gain,
        g_mlp_shift,
        grad_joined,
        gb_joined,
        grad_dense,
        g_out,
        grad_up,
        gb_up,
        grad_down,
        g_out,
        g_final_gain,
        g_final_shift,
        grad_vocab,
    )


def placed(dp, mp):
    ins = (
        P(dp, None),
        P(dp, None),
        P(),
        P(dp),
        P(dp),
        P(dp),
        P(dp),
        P(),
        P(),
        P(),
        P(),
        P(dp, mp),
        P(mp),
        P(mp, dp),
        P(),
        P(dp, mp),
        P(mp),
        P(mp, dp),
        P(),
        P(),
        P(),
        P(dp, mp),
    )
    outs = (
        P(),
        P(),
        P(dp, None),
        P(),
        P(),
        P(),
        P(),
        P(dp, mp),
        P(mp),
        P(mp, dp),
        P(),
        P(dp, mp),
        P(mp),
        P(mp, dp),
        P(),
        P(),
        P(),
        P(dp, mp),
    )
    return ins, outs


def solution(mesh):
    n_dp, n_mp = mesh.shape["dp"], mesh.shape["mp"]
    if n_dp == 8 and n_mp == 4:
        fine = jax.sharding.Mesh(mesh.devices.reshape(n_dp // 2, 2, n_mp // 2, 2), ALL)
        ins, outs = placed(DP, ("x", "c"))
        return jax.shard_map(fast_shards, mesh=fine, in_specs=ins, out_specs=outs, check_vma=False)
    ins, outs = placed("dp", "mp")
    return jax.shard_map(shards, mesh=mesh, in_specs=ins, out_specs=outs, check_vma=False)
```

```python
import functools
import math

import jax
import jax.numpy as jnp
from jax import lax
from jax.experimental import pallas as pl
from jax.experimental.layout import Layout, with_layout_constraint
from jax.experimental.pallas import tpu as pltpu
from jax.sharding import PartitionSpec as P

HD = 128
ROT = 32


kto_beta = 4.0
norm_eps = 1e-05
masked_score = -1e30


def joined(value, axis, join):
    pieces = jax.tree.map(lambda part: lax.all_gather(part, axis), value)
    head = jax.tree.map(lambda part: part[0], pieces)
    tail = jax.tree.map(lambda part: part[1:], pieces)
    subtotal, _ = lax.scan(lambda subtotal, piece: (join(subtotal, piece), None), head, tail)
    return subtotal


def layer_norm(values, norm_gain, norm_shift):
    centred = values - jnp.mean(values, axis=-1, keepdims=True)
    spread = jnp.mean(centred * centred, axis=-1, keepdims=True)
    return centred * lax.rsqrt(spread + norm_eps) * norm_gain + norm_shift


def rotate(values, position):
    half_rot = ROT // 2
    inverse = jnp.exp(jnp.arange(half_rot, dtype=jnp.float32) * (-2.0 * math.log(10000.0) / ROT))
    angles = position.astype(jnp.float32)[:, None] * inverse[None, :]
    cosine_table = jnp.cos(angles)[:, None, :]
    sine_table = jnp.sin(angles)[:, None, :]
    first_half = values[..., :half_rot]
    second_half = values[..., half_rot:ROT]
    return jnp.concatenate(
        [
            first_half * cosine_table - second_half * sine_table,
            second_half * cosine_table + first_half * sine_table,
            values[..., ROT:],
        ],
        axis=-1,
    )


def gelu_exact(values):
    return jax.nn.gelu(values, approximate=False)


def attention_scores(query_low, keys_low, allowed):
    raw_scores = jnp.einsum(
        "rhd,chd->hrc", query_low, keys_low, preferred_element_type=jnp.float32
    ) / math.sqrt(HD)
    return jnp.where(allowed[None], raw_scores, masked_score)


def combine_vocab(first, second):
    high_first, total_first, pick_first = first
    high_second, total_second, pick_second = second
    highest = jnp.maximum(high_first, high_second)
    merged_total = total_first * jnp.exp(high_first - highest) + total_second * jnp.exp(
        high_second - highest
    )
    return (highest, merged_total, pick_first + pick_second)


def gather_weights(weights_low):
    w_joined, w_up, w_vocab, w_dense, w_down = weights_low
    joined_all, up_all, vocab_all = (
        lax.all_gather(w_joined, "dp", axis=0, tiled=True),
        lax.all_gather(w_up, "dp", axis=0, tiled=True),
        lax.all_gather(w_vocab, "dp", axis=0, tiled=True),
    )
    dense_all, down_all = (
        lax.all_gather(w_dense, "dp", axis=1, tiled=True),
        lax.all_gather(w_down, "dp", axis=1, tiled=True),
    )
    return (joined_all, up_all, vocab_all, dense_all, down_all)


def forward_pass(gathered, smalls, rows_low, allowed, position, targets):
    joined_all, up_all, vocab_all, dense_all, down_all = gathered
    (
        attn_gain,
        attn_shift,
        mlp_gain,
        mlp_shift,
        b_joined,
        b_dense,
        b_up,
        b_down,
        final_gain,
        final_shift,
    ) = smalls
    rows_float = rows_low.astype(jnp.float32)
    count_rows = rows_float.shape[0]
    attn_low = layer_norm(rows_float, attn_gain, attn_shift).astype(jnp.bfloat16)
    mlp_low = layer_norm(rows_float, mlp_gain, mlp_shift).astype(jnp.bfloat16)
    joined_cols = jnp.dot(attn_low, joined_all, preferred_element_type=jnp.float32) + b_joined
    joined_cols = joined_cols.reshape(count_rows, -1, 3, HD)
    query_low = rotate(joined_cols[:, :, 0], position).astype(jnp.bfloat16)
    keys_low = rotate(joined_cols[:, :, 1], position).astype(jnp.bfloat16)
    values_low = joined_cols[:, :, 2].astype(jnp.bfloat16)
    scores = attention_scores(query_low, keys_low, allowed)
    highest = jnp.max(scores, axis=-1, keepdims=True)
    scaled_exp = jnp.exp(scores - highest)
    totals = jnp.sum(scaled_exp, axis=-1, keepdims=True)
    probs_low = (scaled_exp / totals).astype(jnp.bfloat16)
    score_lse = highest + jnp.log(totals)
    mixed_low = (
        jnp.einsum("hrc,chd->rhd", probs_low, values_low, preferred_element_type=jnp.float32)
        .reshape(count_rows, -1)
        .astype(jnp.bfloat16)
    )
    hidden = jnp.dot(mlp_low, up_all, preferred_element_type=jnp.float32) + b_up
    active_low = gelu_exact(hidden).astype(jnp.bfloat16)
    branch_part = jnp.dot(mixed_low, dense_all, preferred_element_type=jnp.float32) + jnp.dot(
        active_low, down_all, preferred_element_type=jnp.float32
    )
    branch = lax.psum(branch_part, "mp")
    resid_sum = rows_float + branch + b_dense + b_down
    final_low = layer_norm(resid_sum, final_gain, final_shift).astype(jnp.bfloat16)
    logits = jnp.dot(final_low, vocab_all, preferred_element_type=jnp.float32)
    local_high = jnp.max(logits, axis=-1)
    local_total = jnp.sum(jnp.exp(logits - local_high[:, None]), axis=-1)
    column = targets - lax.axis_index("mp") * logits.shape[1]
    target_hit = lax.broadcasted_iota(jnp.int32, logits.shape, 1) == column[:, None]
    local_pick = jnp.sum(jnp.where(target_hit, logits, 0.0), axis=-1)
    high_all, total_all, picked = joined((local_high, local_total, local_pick), "mp", combine_vocab)
    vocab_lse = high_all + jnp.log(total_all)
    return (
        attn_low,
        mlp_low,
        joined_cols,
        query_low,
        keys_low,
        values_low,
        score_lse,
        mixed_low,
        hidden,
        active_low,
        resid_sum,
        final_low,
        logits,
        vocab_lse,
        target_hit,
        picked - vocab_lse,
    )


def shards(
    residual,
    lengths,
    pair_order,
    token_ids,
    desirable,
    ref_match,
    ref_pair,
    attn_gain,
    attn_shift,
    mlp_gain,
    mlp_shift,
    w_joined,
    b_joined,
    w_dense,
    b_dense,
    w_up,
    b_up,
    w_down,
    b_down,
    final_gain,
    final_shift,
    w_vocab,
):
    dp_count = lax.axis_size("dp")
    tokens_here = residual.shape[0]
    piece_rows = tokens_here // 2
    width = residual.shape[1]
    seq_here = lengths.shape[1]
    block_count = 2 * dp_count
    my_index = lax.axis_index("dp")
    block_slots = jnp.arange(block_count, dtype=jnp.int32)
    my_blocks = 2 * my_index + jnp.arange(2, dtype=jnp.int32)
    my_targets = jnp.sum(
        jnp.where(block_slots[None, :] == my_blocks[:, None], pair_order[None, :], 0), axis=1
    )
    send_hot = my_targets[:, None] == block_slots[None, :]
    own_blocks = residual.reshape(2, piece_rows, width)
    own_ids = token_ids.reshape(2, piece_rows)
    sent_rows = jnp.einsum(
        "ht,hpd->tpd", send_hot.astype(jnp.bfloat16), own_blocks, preferred_element_type=jnp.float32
    ).astype(jnp.bfloat16)
    sent_ids = jnp.sum(jnp.where(send_hot[:, :, None], own_ids[:, None, :], 0), axis=0)
    got_rows, got_ids = (
        lax.all_to_all(
            sent_rows.reshape(dp_count, 2, piece_rows, width),
            "dp",
            split_axis=0,
            concat_axis=0,
            tiled=True,
        ),
        lax.all_to_all(
            sent_ids.reshape(dp_count, 2, piece_rows), "dp", split_axis=0, concat_axis=0, tiled=True
        ),
    )
    paired_rows = jnp.sum(got_rows.astype(jnp.float32), axis=0).astype(jnp.bfloat16)
    paired_ids = jnp.sum(got_ids, axis=0)
    rows_low = jnp.concatenate([residual, paired_rows.reshape(tokens_here, width)], axis=0)
    ids_all = jnp.concatenate([token_ids, paired_ids.reshape(tokens_here)], axis=0)
    seq_lengths = lengths[0]
    seq_slots = jnp.arange(seq_here, dtype=jnp.int32)
    seq_ends = jnp.sum(
        jnp.where(seq_slots[None, :] <= seq_slots[:, None], seq_lengths[None, :], 0), axis=1
    )
    seq_starts = seq_ends - seq_lengths
    places = jnp.arange(tokens_here, dtype=jnp.int32)
    segment = jnp.sum((places[:, None] >= seq_ends[None, :]).astype(jnp.int32), axis=1)
    own_start = jnp.sum(
        jnp.where(segment[:, None] == seq_slots[None, :], seq_starts[None, :], 0), axis=1
    )
    position_half = places - own_start
    segment_all = jnp.concatenate([segment, segment + seq_here])
    position = jnp.concatenate([position_half, position_half])
    count_rows = 2 * tokens_here
    row_index = jnp.arange(count_rows, dtype=jnp.int32)
    allowed = (segment_all[:, None] == segment_all[None, :]) & (
        row_index[None, :] <= row_index[:, None]
    )
    targets = jnp.concatenate([ids_all[1:], jnp.zeros((1,), jnp.int32)])
    scored = jnp.concatenate(
        [segment_all[1:] == segment_all[:-1], jnp.zeros((1,), jnp.bool_)]
    ).astype(jnp.float32)
    ref_rows = jnp.concatenate([ref_match, ref_pair])
    length_float = seq_lengths.astype(jnp.float32)
    length_both = jnp.concatenate([length_float, length_float])
    seq_match = segment_all[:, None] == jnp.arange(2 * seq_here, dtype=jnp.int32)[None, :]
    smalls = tuple(
        (
            value.astype(jnp.float32)
            for value in (
                attn_gain,
                attn_shift,
                mlp_gain,
                mlp_shift,
                b_joined,
                b_dense,
                b_up,
                b_down,
                final_gain,
                final_shift,
            )
        )
    )
    weights_low = (w_joined, w_up, w_vocab, w_dense, w_down)
    gathered = gather_weights(weights_low)
    first_pass = forward_pass(gathered, smalls, rows_low, allowed, position, targets)
    token_terms = (first_pass[15] - ref_rows) * scored
    seq_means = jnp.sum(jnp.where(seq_match, token_terms[:, None], 0.0), axis=0) / length_both
    kl_total = lax.psum(jnp.sum(seq_means[seq_here:]), "dp")
    seq_total = seq_here * dp_count
    kl_estimate = kl_total / seq_total
    signs = 2.0 * desirable.astype(jnp.float32) - 1.0
    sigmoid_val = jax.nn.sigmoid(kto_beta * signs * (seq_means[:seq_here] - kl_estimate))
    slope = -kto_beta * signs * sigmoid_val * (1.0 - sigmoid_val)
    kto_loss, slope_total = lax.psum((jnp.sum(1.0 - sigmoid_val), jnp.sum(slope)), "dp")
    seq_coef = (
        jnp.concatenate([slope, jnp.broadcast_to(-slope_total / seq_total, (seq_here,))])
        / length_both
    )
    token_coef = jnp.sum(jnp.where(seq_match, seq_coef[None, :], 0.0), axis=1) * scored
    matrices = gather_weights(weights_low)
    current = forward_pass(matrices, smalls, rows_low, allowed, position, targets)
    joined_all, up_all, vocab_all, dense_all, down_all = matrices
    (
        attn_low,
        mlp_low,
        joined_cols,
        query_low,
        keys_low,
        values_low,
        score_lse,
        mixed_low,
        hidden,
        active_low,
        resid_sum,
        final_low,
        logits,
        vocab_lse,
        target_hit,
        log_probs,
    ) = current
    softmax_local = jnp.exp(logits - vocab_lse[:, None])
    dlogits = (token_coef[:, None] * (jnp.where(target_hit, 1.0, 0.0) - softmax_local)).astype(
        jnp.bfloat16
    )
    grad_vocab = jnp.einsum("rd,rv->dv", final_low, dlogits, preferred_element_type=jnp.float32)
    dfinal_part = jnp.einsum("rv,dv->rd", dlogits, vocab_all, preferred_element_type=jnp.float32)
    dfinal = lax.psum(dfinal_part, "mp")
    _, final_pull = jax.vjp(layer_norm, resid_sum, smalls[8], smalls[9])
    dresid, grad_final_gain, grad_final_shift = final_pull(dfinal)
    grad_b_out = jnp.sum(dresid, axis=0)
    dbranch = dresid.astype(jnp.bfloat16)
    grad_dense = jnp.einsum("rk,rd->kd", mixed_low, dbranch, preferred_element_type=jnp.float32)
    grad_down = jnp.einsum("rf,rd->fd", active_low, dbranch, preferred_element_type=jnp.float32)
    dmixed = jnp.einsum("rd,kd->rk", dbranch, dense_all, preferred_element_type=jnp.float32).astype(
        jnp.bfloat16
    )
    dactive = jnp.einsum("rd,fd->rf", dbranch, down_all, preferred_element_type=jnp.float32)
    _, gelu_pull = jax.vjp(gelu_exact, hidden)
    dhidden = gelu_pull(dactive)[0].astype(jnp.bfloat16)
    grad_up = jnp.einsum("rd,rf->df", mlp_low, dhidden, preferred_element_type=jnp.float32)
    grad_b_up = jnp.sum(dhidden.astype(jnp.float32), axis=0)
    dmlp_part = jnp.einsum("rf,df->rd", dhidden, up_all, preferred_element_type=jnp.float32)
    dmixed_heads = dmixed.reshape(count_rows, -1, HD)
    scores = attention_scores(query_low, keys_low, allowed)
    probs_float = jnp.where(allowed[None], jnp.exp(scores - score_lse), 0.0)
    dvalues = jnp.einsum(
        "hrc,rhd->chd",
        probs_float.astype(jnp.bfloat16),
        dmixed_heads,
        preferred_element_type=jnp.float32,
    )
    dprobs = jnp.einsum(
        "rhd,chd->hrc", dmixed_heads, values_low, preferred_element_type=jnp.float32
    )
    inner_sum = jnp.sum(probs_float * dprobs, axis=-1, keepdims=True)
    dscores = (probs_float * (dprobs - inner_sum)).astype(jnp.bfloat16)
    dquery = jnp.einsum(
        "hrc,chd->rhd", dscores, keys_low, preferred_element_type=jnp.float32
    ) / math.sqrt(HD)
    dkeys = jnp.einsum(
        "hrc,rhd->chd", dscores, query_low, preferred_element_type=jnp.float32
    ) / math.sqrt(HD)
    _, rotate_pull = jax.vjp(lambda value: rotate(value, position), joined_cols[:, :, 0])
    dfused = jnp.stack([rotate_pull(dquery)[0], rotate_pull(dkeys)[0], dvalues], axis=2)
    dfused = dfused.reshape(count_rows, -1).astype(jnp.bfloat16)
    grad_joined = jnp.einsum("rd,re->de", attn_low, dfused, preferred_element_type=jnp.float32)
    grad_b_joined = jnp.sum(dfused.astype(jnp.float32), axis=0)
    dattn_part = jnp.einsum("re,de->rd", dfused, joined_all, preferred_element_type=jnp.float32)
    dattn, dmlp = lax.psum((dattn_part, dmlp_part), "mp")
    rows_float = rows_low.astype(jnp.float32)
    _, attn_pull = jax.vjp(layer_norm, rows_float, smalls[0], smalls[1])
    drows_attn, grad_attn_gain, grad_attn_shift = attn_pull(dattn)
    _, mlp_pull = jax.vjp(layer_norm, rows_float, smalls[2], smalls[3])
    drows_mlp, grad_mlp_gain, grad_mlp_shift = mlp_pull(dmlp)
    drows = dresid + drows_attn + drows_mlp
    my_slots = 2 * my_index + jnp.arange(2, dtype=jnp.int32)
    anchor = jnp.sum(
        jnp.where(pair_order[None, :] == my_slots[:, None], block_slots[None, :], 0), axis=1
    )
    back_hot = (anchor[:, None] == block_slots[None, :]).astype(jnp.float32)
    back_blocks = drows[tokens_here:].reshape(2, piece_rows, width)
    back_sent = jnp.einsum("st,spd->tpd", back_hot, back_blocks, precision=lax.Precision.HIGHEST)
    returned = lax.all_to_all(
        back_sent.reshape(dp_count, 2, piece_rows, width),
        "dp",
        split_axis=0,
        concat_axis=0,
        tiled=True,
    )
    grad_input = drows[:tokens_here] + jnp.sum(returned, axis=0).reshape(tokens_here, width)
    gw_joined, gw_up, gw_vocab = (
        lax.psum_scatter(grad_joined, "dp", scatter_dimension=0, tiled=True),
        lax.psum_scatter(grad_up, "dp", scatter_dimension=0, tiled=True),
        lax.psum_scatter(grad_vocab, "dp", scatter_dimension=0, tiled=True),
    )
    gw_dense, gw_down = (
        lax.psum_scatter(grad_dense, "dp", scatter_dimension=1, tiled=True),
        lax.psum_scatter(grad_down, "dp", scatter_dimension=1, tiled=True),
    )
    (
        sg_attn_gain,
        sg_attn_shift,
        sg_mlp_gain,
        sg_mlp_shift,
        sg_b_joined,
        sg_b_up,
        sg_b_out,
        sg_final_gain,
        sg_final_shift,
    ) = lax.psum(
        (
            grad_attn_gain,
            grad_attn_shift,
            grad_mlp_gain,
            grad_mlp_shift,
            grad_b_joined,
            grad_b_up,
            grad_b_out,
            grad_final_gain,
            grad_final_shift,
        ),
        "dp",
    )
    return (
        kto_loss,
        kl_estimate,
        grad_input,
        sg_attn_gain,
        sg_attn_shift,
        sg_mlp_gain,
        sg_mlp_shift,
        gw_joined,
        sg_b_joined,
        gw_dense,
        sg_b_out,
        gw_up,
        sg_b_up,
        gw_down,
        sg_b_out,
        sg_final_gain,
        sg_final_shift,
        gw_vocab,
    )


DP = ("z", "y")
CHIPS = ("z", "y", "x")
ALL = ("z", "y", "x", "c")
SWAP = ((0, 1), (1, 0))
F32, BF16 = jnp.float32, jnp.bfloat16
BY_X = (0, 2)
END_BY_X = (0,)


def dot(a, b, contract):
    return lax.dot_general(a, b, ((contract[:1], contract[1:]), ((), ())), preferred_element_type=F32)


def swap(value):
    return lax.ppermute(value, "c", SWAP)


def normed(values):
    centred = values - jnp.mean(values, axis=-1, keepdims=True)
    inverse = lax.rsqrt(jnp.mean(centred * centred, axis=-1, keepdims=True) + norm_eps)
    return centred * inverse, inverse


def norm_back(t, hat, inverse):
    return inverse * (
        t - jnp.mean(t, axis=-1, keepdims=True) - hat * jnp.mean(t * hat, axis=-1, keepdims=True)
    )


def exchange(value):
    return lax.all_to_all(value, DP, split_axis=0, concat_axis=0, tiled=True)


def here():
    return tuple(lax.axis_index(a) for a in ALL)


def send(source, target, out_sem, in_sem, device):
    copy = pltpu.make_async_remote_copy(
        src_ref=source,
        dst_ref=target,
        send_sem=out_sem,
        recv_sem=in_sem,
        device_id=device,
        device_id_type=pl.DeviceIdType.MESH,
    )
    copy.start()
    return copy


def arrived(target, out_sem, in_sem, device):
    pltpu.make_async_remote_copy(
        src_ref=target,
        dst_ref=target,
        send_sem=out_sem,
        recv_sem=in_sem,
        device_id=device,
        device_id_type=pl.DeviceIdType.MESH,
    ).wait_recv()


def left(source, out_sem, in_sem, device):
    pltpu.make_async_remote_copy(
        src_ref=source,
        dst_ref=source,
        send_sem=out_sem,
        recv_sem=in_sem,
        device_id=device,
        device_id_type=pl.DeviceIdType.MESH,
    ).wait_send()


PIECES = 1


def in_pieces(source, target, out_sem, in_sem, device):
    size = source.shape[1] // PIECES
    for i in range(PIECES):
        at = (slice(None), pl.ds(i * size, size))
        send(source.at[at], target.at[at], out_sem, in_sem, device)


def greet(devices):
    barrier = pltpu.get_barrier_semaphore()
    for device in devices:
        pl.semaphore_signal(barrier, inc=1, device_id=device, device_id_type=pl.DeviceIdType.MESH)
    pl.semaphore_wait(barrier, len(devices))


def neighbours(nz):
    iz, iy, ix, ic = here()
    return [(lax.rem(iz + k, nz), iy, ix, ic) for k in range(1, nz)] + [
        (iz, 1 - iy, ix, ic),
        (iz, iy, 1 - ix, ic),
    ]


def other_core():
    iz, iy, ix, ic = here()
    return (iz, iy, ix, 1 - ic)


class Reduce:
    @staticmethod
    def scratch(parts, nz, half, width):
        dma = pltpu.SemaphoreType.DMA
        return [
            pltpu.VMEM((parts, nz, 2, half, width), BF16),
            pltpu.VMEM((parts, nz, half, width), BF16),
            pltpu.VMEM((parts, nz, half, width), BF16),
            pltpu.VMEM((parts, nz, half, width), BF16),
            pltpu.VMEM((parts, nz, half, width), BF16),
            dma((parts, nz, 2)),
            dma((parts, nz, 2)),
            dma((parts, nz)),
            dma((parts, nz)),
            dma((parts, nz)),
            dma((parts, nz)),
        ]

    def __init__(self, nz, half, part, refs, by_x=(0,)):
        self.by_x = by_x
        self.nz, self.half, self.part = nz, half, part
        (
            self.in1,
            self.out2,
            self.in2,
            self.out3,
            self.in3,
            self.s1,
            self.r1,
            self.s2,
            self.r2,
            self.s3,
            self.r3,
        ) = refs
        self.copies = []

    def along(self, h):
        iz, iy, ix, ic = here()
        across_x, across_y = (iz, iy, 1 - ix, ic), (iz, 1 - iy, ix, ic)
        return (across_x, across_y) if h in self.by_x else (across_y, across_x)

    def block(self, h, z, first_mine, second):
        _, iy, ix, _ = here()
        rows = pl.ds(h * self.half, self.half)
        if h in self.by_x:
            return self.part.at[z, second, ix if first_mine else 1 - ix, rows]
        return self.part.at[z, iy if first_mine else 1 - iy, second, rows]

    def mine(self, h):
        _, iy, ix, _ = here()
        return iy if h in self.by_x else ix

    def plane(self, k):
        return lax.rem(here()[0] + k, self.nz)

    def start(self, h, far):
        first, _ = self.along(h)
        second = 1 - self.mine(h) if far else self.mine(h)
        for k in list(range(1, self.nz)) + [0]:
            z = self.plane(k)
            self.copies.append(
                send(
                    self.block(h, z, False, second),
                    self.in1.at[h, z, second],
                    self.s1.at[h, z, second],
                    self.r1.at[h, z, second],
                    first,
                )
            )

    def second(self, h):
        first, across = self.along(h)
        far = 1 - self.mine(h)
        for k in list(range(1, self.nz)) + [0]:
            z = self.plane(k)
            arrived(self.in1.at[h, z, far], self.s1.at[h, z, far], self.r1.at[h, z, far], first)
            self.out2[h, z] = (
                self.block(h, z, True, far)[...].astype(F32) + self.in1[h, z, far].astype(F32)
            ).astype(BF16)
            self.copies.append(
                send(self.out2.at[h, z], self.in2.at[h, z], self.s2.at[h, z], self.r2.at[h, z], across)
            )

    def third(self, h):
        iz, iy, ix, ic = here()
        first, across = self.along(h)
        near = self.mine(h)
        for k in list(range(1, self.nz)) + [0]:
            z = self.plane(k)
            arrived(self.in1.at[h, z, near], self.s1.at[h, z, near], self.r1.at[h, z, near], first)
            arrived(self.in2.at[h, z], self.s2.at[h, z], self.r2.at[h, z], across)
            total = (
                self.block(h, z, True, near)[...].astype(F32)
                + self.in1[h, z, near].astype(F32)
                + self.in2[h, z].astype(F32)
            )
            if k == 0:
                return total
            self.out3[h, k] = total.astype(BF16)
            far = (z, iy, ix, ic)
            in_pieces(self.out3.at[h, k], self.in3.at[h, k], self.s3.at[h, k], self.r3.at[h, k], far)

    def finish(self, h, total):
        _, iy, ix, ic = here()
        for k in range(1, self.nz):
            z = self.plane(self.nz - k)
            arrived(self.in3.at[h, k], self.s3.at[h, k], self.r3.at[h, k], (z, iy, ix, ic))
            total = total + self.in3[h, k].astype(F32)
        return total

    def end(self, parts):
        iz, iy, ix, ic = here()
        for copy in self.copies:
            copy.wait_send()
        for h in parts:
            for k in range(1, self.nz):
                far = (self.plane(k), iy, ix, ic)
                left(self.out3.at[h, k], self.s3.at[h, k], self.r3.at[h, k], far)


class Gather:
    @staticmethod
    def scratch(parts, nz):
        dma = pltpu.SemaphoreType.DMA
        return [dma((parts, nz)), dma((parts, nz)), dma((parts, nz, 2)), dma((parts, nz, 2, 2)), dma((parts,))]

    def __init__(self, nz, half, out, refs, forward=None, by_x=(0,)):
        self.by_x = by_x
        self.nz, self.half, self.out = nz, half, out
        self.sz, self.sp, self.sq, self.r, self.local = refs
        self.copies, self.locals, self.forward = [], [], forward

    def axes(self, h):
        iz, iy, ix, ic = here()
        across_x, across_y = (iz, iy, 1 - ix, ic), (iz, 1 - iy, ix, ic)
        return (across_y, across_x) if h in self.by_x else (across_x, across_y)

    def block(self, h, z, y, x):
        return self.out.at[z, y, x, pl.ds(h * self.half, self.half)]

    def on(self, h, source, z, y, x, which):
        iz, iy, ix, ic = here()
        p, q = self.axes(h)
        there, got = self.block(h, z, y, x), self.r.at[h, z, y, x]
        if "z" in which:
            for k in range(1, self.nz):
                far = (lax.rem(iz + k, self.nz), iy, ix, ic)
                in_pieces(source, there, self.sz.at[h, k], got, far)
        if "p" in which:
            self.copies.append(send(source, there, self.sp.at[h, z], got, p))
        if "q" in which:
            side = x if h not in self.by_x else y
            self.copies.append(send(source, there, self.sq.at[h, z, side], got, q))
        if self.forward is not None:
            self.forward(h, source, z, y, x)

    def start(self, h, source):
        iz, iy, ix, _ = here()
        copy = pltpu.make_async_copy(source, self.block(h, iz, iy, ix), self.local.at[h])
        copy.start()
        self.locals.append(copy)
        self.on(h, source, iz, iy, ix, "zpq")

    def got(self, h, z, y, x):
        arrived(self.block(h, z, y, x), self.sz.at[h, 0], self.r.at[h, z, y, x], self.axes(h)[0])

    def first(self, h, k):
        iz, iy, ix, _ = here()
        z = lax.rem(iz + k, self.nz)
        self.got(h, z, iy, ix)
        self.on(h, self.block(h, z, iy, ix), z, iy, ix, "pq")

    def second(self, h, k):
        iz, iy, ix, _ = here()
        z = lax.rem(iz + k, self.nz)
        y, x = (1 - iy, ix) if h in self.by_x else (iy, 1 - ix)
        self.got(h, z, y, x)
        self.on(h, self.block(h, z, y, x), z, y, x, "q")

    def third(self, h, k):
        iz, iy, ix, _ = here()
        z = lax.rem(iz + k, self.nz)
        for side in (0, 1):
            if h in self.by_x:
                y, x = (iy if side == 0 else 1 - iy), 1 - ix
            else:
                y, x = 1 - iy, (ix if side == 0 else 1 - ix)
            self.got(h, z, y, x)
            if self.forward is not None:
                self.forward(h, self.block(h, z, y, x), z, y, x)

    def turns(self):
        return [1, self.nz - 1] + [k for k in range(2, self.nz - 1)]

    def firsts(self, parts):
        for h in parts:
            self.second(h, 0)
        for k in self.turns():
            for h in parts:
                self.first(h, k)

    def seconds(self, parts):
        for k in self.turns():
            for h in parts:
                self.second(h, k)

    def thirds(self, parts):
        for k in [0] + self.turns():
            for h in parts:
                self.third(h, k)

    def rest(self):
        self.firsts((0, 1))
        self.seconds((0, 1))
        self.thirds((0, 1))

    def end(self, parts):
        iz, iy, ix, ic = here()
        for copy in self.locals:
            copy.wait()
        for copy in self.copies:
            copy.wait_send()
        for h in parts:
            for k in range(1, self.nz):
                far = (lax.rem(iz + k, self.nz), iy, ix, ic)
                left(self.block(h, iz, iy, ix), self.sz.at[h, k], self.r.at[h, iz, iy, ix], far)


def reduce_gather(nz, half, part, out, refs, finished):
    reduce = Reduce(nz, half, part, refs[:11], BY_X)
    gather = Gather(nz, half, out, refs[11:], None, BY_X)
    greet(neighbours(nz))
    early, late = (0, 1), (2, 3)

    def begin(parts):
        for far in (True, False):
            for h in parts:
                reduce.start(h, far)

    def finish(parts, kept):
        for h in parts:
            gather.start(h, finished(h, reduce.finish(h, kept[h])))

    begin(early)
    for h in early:
        reduce.second(h)
    begin(late)
    kept = {h: reduce.third(h) for h in early}
    for h in late:
        reduce.second(h)
    finish(early, kept)
    kept = {h: reduce.third(h) for h in late}
    gather.firsts(early)
    finish(late, kept)
    gather.seconds(early)
    gather.firsts(late)
    gather.thirds(early)
    gather.seconds(late)
    gather.thirds(late)
    gather.end(early + late)
    reduce.end(early + late)


def forward_kernel(nz, half, part, rows, bias, gain, shift, out, resid, fin, *refs):
    def finished(h, total):
        at = pl.ds(h * half, half)
        total = rows[at].astype(F32) + total + bias[...]
        resid[at] = total
        hat, _ = normed(total)
        fin[h] = (hat * gain[...] + shift[...]).astype(BF16)
        return fin.at[h]

    reduce_gather(nz, half, part, out, refs, finished)


def backward_kernel(nz, half, part, resid, gain, out, vectors, fin, *refs):
    sums = []

    def finished(h, total):
        hat, inverse = normed(resid[pl.ds(h * half, half)])
        dresid = norm_back(total * gain[...], hat, inverse)
        fin[h] = dresid.astype(BF16)
        sums.append([jnp.sum(v, axis=0, keepdims=True) for v in (total * hat, total, dresid)])
        return fin.at[h]

    reduce_gather(nz, half, part, out, refs, finished)
    for i in range(3):
        vectors[pl.ds(i, 1)] = sum(part_sums[i] for part_sums in sums)


def vmem():
    return pl.BlockSpec(memory_space=pltpu.VMEM)


def anywhere():
    return pl.BlockSpec(memory_space=pltpu.HBM)


def busy(us):
    return pl.CostEstimate(flops=0, bytes_accessed=us * 3_000_000, transcendentals=0)


def comm(which, limit=28):
    return pltpu.CompilerParams(collective_id=which, has_side_effects=True, vmem_limit_bytes=limit << 20)


def reduce_norm_gather(nz, part, rows, bias, gain, shift):
    share, width = rows.shape
    half = share // 4
    out, resid = pl.pallas_call(
        functools.partial(forward_kernel, nz, half),
        out_shape=[
            jax.ShapeDtypeStruct((nz, 2, 2, share, width), BF16),
            jax.ShapeDtypeStruct((share, width), F32),
        ],
        in_specs=[vmem()] * 5,
        out_specs=[anywhere(), vmem()],
        scratch_shapes=[pltpu.VMEM((4, half, width), BF16)]
        + Reduce.scratch(4, nz, half, width)
        + Gather.scratch(4, nz),
        cost_estimate=busy(90),
        compiler_params=comm(2, 62),
    )(part.reshape(nz, 2, 2, share, width), rows, bias, gain, shift)
    return out.reshape(4 * nz * share, width), resid


def reduce_back_gather(nz, part, resid, gain):
    share, width = resid.shape
    half = share // 4
    out, vectors = pl.pallas_call(
        functools.partial(backward_kernel, nz, half),
        out_shape=[
            jax.ShapeDtypeStruct((nz, 2, 2, share, width), BF16),
            jax.ShapeDtypeStruct((3, width), F32),
        ],
        in_specs=[vmem()] * 3,
        out_specs=[anywhere(), vmem()],
        scratch_shapes=[pltpu.VMEM((4, half, width), BF16)]
        + Reduce.scratch(4, nz, half, width)
        + Gather.scratch(4, nz),
        cost_estimate=busy(90),
        compiler_params=comm(3, 62),
    )(part.reshape(nz, 2, 2, share, width), resid, gain)
    return out.reshape(4 * nz * share, width), vectors


def merge(a, b):
    top = jnp.maximum(a[0], b[0])
    return (top, a[1] * jnp.exp(a[0] - top) + b[1] * jnp.exp(b[0] - top), a[2] + b[2])


def objective_kernel(
    nz, seqs, seq_total, stats, hot, scored, refs, lens, wanted, coef, lse_out, scalars, held, near, far, s1, r1, s2, r2
):
    iz, iy, ix, ic = here()
    plane = [(iz, iy, 1 - ix, ic), (iz, 1 - iy, ix, ic), (iz, 1 - iy, 1 - ix, ic)]
    line = [(lax.rem(iz + k, nz), iy, ix, c) for c in (ic, 1 - ic) for k in range(nz)][1:]
    greet(plane + line)
    copies = []
    for i, device in enumerate(plane):
        copies.append(send(stats, near.at[iy, ix], s1.at[i], r1.at[iy, ix], device))
    near[iy, ix] = stats[...]
    for _, y, x, _ in plane:
        arrived(near.at[y, x], s1.at[0], r1.at[y, x], plane[0])
    sides = [tuple(near[y, x, i] for i in range(3)) for y in (0, 1) for x in (0, 1)]
    current = merge(merge(sides[0], sides[1]), merge(sides[2], sides[3]))
    for i in range(3):
        held[i] = current[i]
        far[iz, ic, i] = current[i]
    for i, device in enumerate(line):
        copies.append(send(held, far.at[iz, ic], s2.at[i], r2.at[iz, ic], device))
    for z, _, _, c in line:
        arrived(far.at[z, c], s2.at[0], r2.at[z, c], line[0])

    def whole(c):
        total = tuple(far[0, c, i] for i in range(3))
        for z in range(1, nz):
            total = merge(total, tuple(far[z, c, i] for i in range(3)))
        lse = total[0] + jnp.log(total[1])
        return lse, total[2] - lse

    (own_lse, own), (pair_lse, pair) = whole(0), whole(1)
    lse_out[...] = jnp.where(ic == 0, own_lse, pair_lse)

    def means(values, ref):
        terms = (values - ref) * scored[...]
        return [
            jnp.sum(terms * hot[s], axis=1, keepdims=True) / lens[:, s : s + 1] for s in range(seqs)
        ]

    own_means, pair_means = means(own, refs[0]), means(pair, refs[1])
    kl = jnp.sum(sum(pair_means), axis=0, keepdims=True) / seq_total
    loss = jnp.zeros((1, 1), F32)
    slopes = []
    for s in range(seqs):
        sign = 2.0 * wanted[:, s : s + 1] - 1.0
        sigmoid = jax.nn.sigmoid(kto_beta * sign * (own_means[s] - kl))
        slopes.append(-kto_beta * sign * sigmoid * (1.0 - sigmoid))
        loss = loss + jnp.sum(1.0 - sigmoid, axis=0, keepdims=True)
    shared = -jnp.sum(sum(slopes), axis=0, keepdims=True) / seq_total
    total = jnp.zeros_like(own)
    for s in range(seqs):
        value = jnp.where(ic == 0, slopes[s], shared) / lens[:, s : s + 1]
        total = total + hot[s] * value
    coef[...] = total * scored[...]
    scalars[0] = jnp.broadcast_to(loss, scalars.shape[1:])
    scalars[1] = jnp.broadcast_to(kl, scalars.shape[1:])
    for copy in copies:
        copy.wait_send()


def objective(nz, seq_total, stats, hot, scored, refs, lens, wanted):
    shape = scored.shape
    dma = pltpu.SemaphoreType.DMA
    return pl.pallas_call(
        functools.partial(objective_kernel, nz, hot.shape[0], seq_total),
        out_shape=[
            jax.ShapeDtypeStruct(shape, F32),
            jax.ShapeDtypeStruct(shape, F32),
            jax.ShapeDtypeStruct((2, 8, 128), F32),
        ],
        in_specs=[vmem()] * 6,
        out_specs=[vmem()] * 3,
        scratch_shapes=[
            pltpu.VMEM((3,) + shape, F32),
            pltpu.VMEM((2, 2, 3) + shape, F32),
            pltpu.VMEM((nz, 2, 3) + shape, F32),
            dma((3,)),
            dma((2, 2)),
            dma((2 * nz - 1,)),
            dma((nz, 2)),
        ],
        cost_estimate=busy(15),
        compiler_params=comm(4),
    )(stats, hot, scored, refs, lens, wanted)


def diagonal(nz):
    iz, iy, ix, ic = here()
    return [(lax.rem(iz + k, nz), 1 - iy, ix, 1 - ic) for k in range(nz)]


def to_head(nz, k, pairs, local_sem, out_sem, in_sem):
    iz, iy, ix, ic = here()
    z = lax.rem(iz + k, nz)
    device = (z, ic, ix, iy)

    def remote():
        for i, (source, target) in enumerate(pairs):
            send(source, target, out_sem.at[i, z], in_sem.at[i, iz], device)

    if k:
        remote()
        return
    pl.when(iy != ic)(remote)

    @pl.when(iy == ic)
    def _():
        for i, (source, target) in enumerate(pairs):
            copy = pltpu.make_async_copy(source, target, local_sem.at[i])
            copy.start()
            copy.wait()


def from_head(nz, k, targets, out_sem, in_sem):
    iz, iy, ix, ic = here()
    z = lax.rem(iz + k, nz)

    def wait():
        for i, target in enumerate(targets):
            arrived(target, out_sem.at[i, z], in_sem.at[i, z], (z, ic, ix, iy))

    if k:
        wait()
    else:
        pl.when(iy != ic)(wait)


def sent_head(nz, k, sources, out_sem, in_sem):
    iz, iy, ix, ic = here()
    z = lax.rem(iz + k, nz)

    def wait():
        for i, source in enumerate(sources):
            pltpu.make_async_remote_copy(
                src_ref=source,
                dst_ref=source,
                send_sem=out_sem.at[i, z],
                recv_sem=in_sem.at[i, z],
                device_id=(z, ic, ix, iy),
                device_id_type=pl.DeviceIdType.MESH,
            ).wait_send()

    if k:
        wait()
    else:
        pl.when(iy != ic)(wait)


def lanes(index, size):
    return pl.ds(pl.multiple_of(index * size, size), size)


def front_kernel(
    nz,
    half,
    residual,
    info,
    bias,
    joined_in,
    dense_in,
    down_in,
    up_in,
    vocab_in,
    natural,
    info_out,
    bias_out,
    joined_out,
    out_all,
    up_all,
    vocab_out,
    vocab_here,
    vs,
    fs,
    fr,
    js,
    jr,
    jl,
    cs,
    cr,
    ms,
    mr,
    zs,
    zr,
    ps,
    ds,
    dr,
    dl,
    es,
    er,
    *refs,
):
    iz, iy, ix, ic = here()
    core = other_core()
    across = [(lax.rem(iz + k, nz), 1 - iy, ix, ic) for k in range(nz)]
    greet(neighbours(nz) + [core] + diagonal(nz) + across[1:])
    depth = joined_in.shape[0]
    cols = joined_out.shape[1]
    heads = dense_in.shape[0] // nz
    units = down_in.shape[0] // (2 * nz)
    dense_out = out_all.at[pl.ds(0, heads)]
    down_out, down_other = (out_all.at[pl.ds(heads + i * units, units)] for i in (0, 1))
    copies = []

    def rows_of(h, z, y, x, c):
        return natural.at[z, y, x, c, pl.ds(h * half, half)]

    def forward(h, source, z, y, x):
        send(source, rows_of(h, z, y, x, ic), fs.at[h, z, y, x], fr.at[h, z, y, x], core)

    class Rows(Gather):
        def block(self, h, z, y, x):
            return rows_of(h, z, y, x, ic)

    fetch = pltpu.make_async_copy(vocab_in, vocab_here, vs.at[0])
    fetch.start()
    gather = Rows(nz, half, natural, refs, forward)
    first = pl.multiple_of((ix * 2 + ic) * 2 * half, 2 * half)
    for h in (0, 1):
        gather.start(h, residual.at[pl.ds(first + h * half, half)])

    copies.append(send(bias, bias_out, ms.at[0], mr.at[0], core))
    info_out[iz, iy] = info[...]
    across_y = (iz, 1 - iy, ix, ic)
    for k in range(1, nz):
        far = (lax.rem(iz + k, nz), iy, ix, ic)
        copies.append(send(info, info_out.at[iz, iy], zs.at[k], zr.at[iz, iy], far))
    copies.append(send(info, info_out.at[iz, iy], ps.at[iz], zr.at[iz, iy], across_y))

    mine = iz * 2 + iy
    for k in list(range(1, nz)) + [0]:
        z = lax.rem(iz + k, nz)
        to_head(
            nz,
            k,
            [
                (joined_in.at[:, lanes(z, cols)], joined_out.at[lanes(mine, depth)]),
                (dense_in.at[lanes(z, heads)], dense_out.at[:, lanes(mine, depth)]),
            ],
            jl,
            js,
            jr,
        )

    for k in range(1, nz):
        z = lax.rem(iz + k, nz)
        arrived(info_out.at[z, iy], zs.at[k], zr.at[z, iy], across_y)
        copies.append(send(info_out.at[z, iy], info_out.at[z, iy], ps.at[z], zr.at[z, iy], across_y))

    gather.firsts((0, 1))

    def own_units(d):
        rows, own, other = lanes(d, depth), pl.ds(0, units), pl.ds(units, units)
        return [
            (up_all.at[rows, own], up_all.at[rows, other]),
            (down_out.at[:, rows], down_other.at[:, rows]),
        ]

    line = [(lax.rem(iz + k, nz), iy, ix, ic) for k in range(1, nz)]
    keep = []
    for i, source in enumerate((up_in.at[:, lanes(mine, units)], down_in.at[lanes(mine, units)])):
        copy = pltpu.make_async_copy(source, own_units(mine)[i][0], dl.at[i])
        copy.start()
        keep.append(copy)
    for i in (0, 1):
        for device in line + across:
            d = device[0] * 2 + device[1]
            source = up_in.at[:, lanes(d, units)] if i == 0 else down_in.at[lanes(d, units)]
            copies.append(send(source, own_units(mine)[i][0], ds.at[i, d], dr.at[i, mine], device))
    gather.seconds((0, 1))
    gather.thirds((0, 1))

    fetch.wait()

    def across_block(i, carry):
        at = lanes(i, depth)
        vocab_out[at] = vocab_here[:, at].T
        return carry

    lax.fori_loop(0, vocab_in.shape[1] // depth, across_block, 0)

    def head_parts(z, side):
        d = z * 2 + side
        return joined_out.at[lanes(d, depth)], dense_out.at[:, lanes(d, depth)]

    for k in [0] + list(range(1, nz)):
        z = lax.rem(iz + k, nz)
        parts = head_parts(z, ic)
        from_head(nz, k, parts, js, jr)
        for i, part in enumerate(parts):
            copies.append(send(part, part, cs.at[i, z], cr.at[i, z], core))
    for copy in keep:
        copy.wait()
    for i in (0, 1):
        for device in [None] + line + across:
            d = mine if device is None else device[0] * 2 + device[1]
            block, other = own_units(d)[i]
            if device is not None:
                arrived(block, ds.at[i, d], dr.at[i, d], device)
            copies.append(send(block, other, es.at[i, d], er.at[i, d], core))
        for d in range(2 * nz):
            arrived(own_units(d)[i][1], es.at[i, d], er.at[i, d], core)
    for k in range(nz):
        z = lax.rem(iz + k, nz)
        arrived(info_out.at[z, 1 - iy], ps.at[z], zr.at[z, 1 - iy], across_y)
    for z in range(nz):
        for y in (0, 1):
            for x in (0, 1):
                for h in (0, 1):
                    arrived(rows_of(h, z, y, x, 1 - ic), fs.at[h, z, y, x], fr.at[h, z, y, x], core)
                    left(rows_of(h, z, y, x, ic), fs.at[h, z, y, x], fr.at[h, z, y, x], core)
    for z in range(nz):
        for i, part in enumerate(head_parts(z, 1 - ic)):
            arrived(part, cs.at[i, z], cr.at[i, z], core)
    arrived(bias_out, ms.at[0], mr.at[0], core)
    gather.end((0, 1))
    for k in range(nz):
        z = lax.rem(iz + k, nz)
        sent_head(nz, k, [joined_in.at[:, lanes(z, cols)], dense_in.at[lanes(z, heads)]], js, jr)
    for copy in copies:
        copy.wait_send()


def front(nz, residual, info, bias, joined_in, dense_in, down_in, up_in, vocab_in):
    held, width = residual.shape
    half = held // 8
    depth, cols = joined_in.shape[0], joined_in.shape[1] // nz
    heads = dense_in.shape[0] // nz
    units = down_in.shape[0] // (2 * nz)
    dma = pltpu.SemaphoreType.DMA
    outs = pl.pallas_call(
        functools.partial(front_kernel, nz, half),
        out_shape=[
            jax.ShapeDtypeStruct((nz, 2, 2, 2, 2 * half, width), BF16),
            jax.ShapeDtypeStruct((nz, 2) + info.shape, F32),
            jax.ShapeDtypeStruct(bias.shape, F32),
            jax.ShapeDtypeStruct((2 * nz * depth, cols), BF16),
            jax.ShapeDtypeStruct((heads + 2 * units, 2 * nz * depth), BF16),
            jax.ShapeDtypeStruct((2 * nz * depth, 2 * units), BF16),
            jax.ShapeDtypeStruct(vocab_in.shape[::-1], BF16),
        ],
        in_specs=[anywhere(), vmem(), vmem(), anywhere(), anywhere(), anywhere(), anywhere(), anywhere()],
        out_specs=[anywhere(), vmem(), vmem(), anywhere(), anywhere(), anywhere(), vmem()],
        scratch_shapes=[
            pltpu.VMEM(vocab_in.shape, BF16),
            dma((1,)),
            dma((2, nz, 2, 2)),
            dma((2, nz, 2, 2)),
            dma((2, nz)),
            dma((2, nz)),
            dma((2,)),
            dma((2, nz)),
            dma((2, nz)),
            dma((1,)),
            dma((1,)),
            dma((nz,)),
            dma((nz, 2)),
            dma((nz,)),
            dma((2, 2 * nz)),
            dma((2, 2 * nz)),
            dma((2,)),
            dma((2, 2 * nz)),
            dma((2, 2 * nz)),
        ]
        + Gather.scratch(2, nz),
        cost_estimate=busy(45),
        compiler_params=comm(1, 62),
    )(residual, info, bias, joined_in, dense_in, down_in, up_in, vocab_in)
    natural = outs[0].reshape(8 * nz * 2 * half, width)
    return natural, outs[1].reshape((2 * nz,) + info.shape), outs[2], outs[3], outs[4], outs[5], outs[6]


def end_kernel(
    nz,
    half,
    part,
    mine_rows,
    other_rows,
    rows,
    vectors,
    keep,
    give,
    joined_in,
    dense_in,
    rows_out,
    vectors_out,
    bias_out,
    joined_out,
    dense_out,
    merged,
    came,
    rows_in,
    vector_in,
    vector_sum,
    give_in,
    joined_came,
    joined_sum,
    dense_came,
    dense_sum,
    ms,
    mr,
    vs,
    vr,
    bs,
    br,
    bp,
    js,
    jr,
    jl,
    cs,
    cr,
    os,
    orr,
    *refs,
):
    iz, iy, ix, ic = here()
    core = other_core()
    across_x, across_y = (iz, iy, 1 - ix, ic), (iz, 1 - iy, ix, ic)
    greet(neighbours(nz) + [core] + diagonal(nz))
    reduce = Reduce(nz, half, merged, refs, END_BY_X)
    copies = []
    depth = joined_in.shape[0] // (2 * nz)
    cols = joined_in.shape[1]
    heads = dense_in.shape[0]
    groups = [(1 - iy, 1 - ix), (iy, 1 - ix), (1 - iy, ix), (iy, ix)]

    for y, x in groups:
        for k in list(range(1, nz)) + [0]:
            z = lax.rem(iz + k, nz)
            copies.append(
                send(part.at[z, y, x, 1 - ic], came.at[z, y, x], ms.at[z, y, x], mr.at[z, y, x], core)
            )
    copies.append(send(vectors, vector_in.at[0], vs.at[0], vr.at[0], core))
    copies.append(send(give, give_in, bs.at[0], br.at[nz, 0], core))
    copies.append(send(other_rows, rows_in, os.at[0], orr.at[0], core))
    for k in range(nz):
        z = lax.rem(iz + k, nz)
        theirs = z * 2 + 1 - ic
        copies.append(
            send(joined_in.at[lanes(theirs, depth)], joined_came.at[z], cs.at[0, z], cr.at[0, z], core)
        )
        copies.append(
            send(dense_in.at[:, lanes(theirs, depth)], dense_came.at[z], cs.at[1, z], cr.at[1, z], core)
        )

    def merge_group(y, x):
        for k in list(range(1, nz)) + [0]:
            z = lax.rem(iz + k, nz)
            arrived(came.at[z, y, x], ms.at[z, y, x], mr.at[z, y, x], core)
            merged[z, y, x] = (part[z, y, x, ic].astype(F32) + came[z, y, x].astype(F32)).astype(BF16)

    merge_group(*groups[0])
    reduce.start(0, True)
    merge_group(*groups[1])
    reduce.start(0, False)
    merge_group(*groups[2])
    reduce.start(1, True)
    reduce.start(1, False)
    merge_group(*groups[3])

    arrived(vector_in.at[0], vs.at[0], vr.at[0], core)
    vector_sum[0] = vectors[...] + vector_in[0]
    copies.append(send(vector_sum.at[0], vector_in.at[1], vs.at[1], vr.at[1], across_x))
    arrived(give_in, bs.at[0], br.at[nz, 0], core)
    bias_out[iz, iy] = keep[...] + give_in[...]
    for k in range(1, nz):
        far = (lax.rem(iz + k, nz), iy, ix, ic)
        copies.append(send(bias_out.at[iz, iy], bias_out.at[iz, iy], bs.at[k], br.at[iz, iy], far))
    copies.append(send(bias_out.at[iz, iy], bias_out.at[iz, iy], bp.at[iz], br.at[iz, iy], across_y))

    for k in list(range(1, nz)) + [0]:
        z = lax.rem(iz + k, nz)
        ours = z * 2 + ic
        arrived(joined_came.at[z], cs.at[0, z], cr.at[0, z], core)
        joined_sum[z] = (joined_in[lanes(ours, depth)].astype(F32) + joined_came[z].astype(F32)).astype(BF16)
        arrived(dense_came.at[z], cs.at[1, z], cr.at[1, z], core)
        dense_sum[z] = (dense_in[:, lanes(ours, depth)].astype(F32) + dense_came[z].astype(F32)).astype(BF16)
        to_head(
            nz,
            k,
            [
                (joined_sum.at[z], joined_out.at[:, lanes(iz, cols)]),
                (dense_sum.at[z], dense_out.at[lanes(iz, heads)]),
            ],
            jl,
            js,
            jr,
        )

    for h in (0, 1):
        reduce.second(h)
    arrived(vector_in.at[1], vs.at[1], vr.at[1], across_x)
    vector_sum[1] = vector_sum[0] + vector_in[1]
    copies.append(send(vector_sum.at[1], vector_in.at[2], vs.at[2], vr.at[2], across_y))
    for k in range(1, nz):
        z = lax.rem(iz + k, nz)
        arrived(bias_out.at[z, iy], bs.at[k], br.at[z, iy], across_y)
        copies.append(send(bias_out.at[z, iy], bias_out.at[z, iy], bp.at[z], br.at[z, iy], across_y))
    kept = [reduce.third(h) for h in (0, 1)]
    arrived(vector_in.at[2], vs.at[2], vr.at[2], across_y)
    vector_sum[2] = vector_sum[1] + vector_in[2]
    for k in range(1, nz):
        far = (lax.rem(iz + k, nz), iy, ix, ic)
        copies.append(send(vector_sum.at[2], vector_in.at[3 + iz], vs.at[2 + k], vr.at[3 + iz], far))
    vector_in[3 + iz] = vector_sum[2]
    arrived(rows_in, os.at[0], orr.at[0], core)
    for h in (0, 1):
        at = pl.ds(h * half, half)
        hat, inverse = normed(rows[at].astype(F32))
        back = norm_back(reduce.finish(h, kept[h]), hat, inverse)
        block = rows_out.at[ix, ic, at]
        rows_out[ix, ic, at] = (
            mine_rows[at].astype(F32) + rows_in[at].astype(F32) + back
        ).astype(BF16)
        copies.append(send(block, block, os.at[1 + h], orr.at[1 + h], across_x))
        copies.append(send(block, block, os.at[3 + h], orr.at[3 + h], core))
    for h in (0, 1):
        block = rows_out.at[1 - ix, ic, pl.ds(h * half, half)]
        arrived(block, os.at[1 + h], orr.at[1 + h], across_x)
        copies.append(send(block, block, os.at[5 + h], orr.at[5 + h], core))
    for k in range(1, nz):
        z = lax.rem(iz + k, nz)
        arrived(vector_in.at[3 + z], vs.at[2 + k], vr.at[3 + z], (z, iy, ix, ic))
    total = vector_in[3]
    for z in range(1, nz):
        total = total + vector_in[3 + z]
    vectors_out[...] = total
    for k in range(nz):
        z = lax.rem(iz + k, nz)
        arrived(bias_out.at[z, 1 - iy], bp.at[z], br.at[z, 1 - iy], across_y)
        from_head(
            nz, k, [joined_out.at[:, lanes(z, cols)], dense_out.at[lanes(z, heads)]], js, jr
        )
        sent_head(nz, k, [joined_sum.at[z], dense_sum.at[z]], js, jr)
    for h in (0, 1):
        at = pl.ds(h * half, half)
        arrived(rows_out.at[ix, 1 - ic, at], os.at[3 + h], orr.at[3 + h], core)
        arrived(rows_out.at[1 - ix, 1 - ic, at], os.at[5 + h], orr.at[5 + h], core)
    reduce.end((0, 1))
    for copy in copies:
        copy.wait_send()


def end(nz, part, mine_rows, other_rows, rows, vectors, keep, give, joined_in, dense_in):
    share, width = rows.shape
    half = share // 2
    depth, cols, heads = joined_in.shape[0] // (2 * nz), joined_in.shape[1], dense_in.shape[0]
    dma = pltpu.SemaphoreType.DMA
    return pl.pallas_call(
        functools.partial(end_kernel, nz, half),
        out_shape=[
            jax.ShapeDtypeStruct((2, 2, share, width), BF16),
            jax.ShapeDtypeStruct(vectors.shape, F32),
            jax.ShapeDtypeStruct((nz, 2) + keep.shape, F32),
            jax.ShapeDtypeStruct((depth, nz * cols), BF16),
            jax.ShapeDtypeStruct((nz * heads, depth), BF16),
        ],
        in_specs=[vmem()] * 9,
        out_specs=[vmem(), vmem(), vmem(), vmem(), vmem()],
        scratch_shapes=[
            pltpu.VMEM((nz, 2, 2, share, width), BF16),
            pltpu.VMEM((nz, 2, 2, share, width), BF16),
            pltpu.VMEM((share, width), BF16),
            pltpu.VMEM((3 + nz,) + vectors.shape, F32),
            pltpu.VMEM((3,) + vectors.shape, F32),
            pltpu.VMEM(keep.shape, F32),
            pltpu.VMEM((nz, depth, cols), BF16),
            pltpu.VMEM((nz, depth, cols), BF16),
            pltpu.VMEM((nz, heads, depth), BF16),
            pltpu.VMEM((nz, heads, depth), BF16),
            dma((nz, 2, 2)),
            dma((nz, 2, 2)),
            dma((2 + nz,)),
            dma((3 + nz,)),
            dma((nz,)),
            dma((nz + 1, 2)),
            dma((nz,)),
            dma((2, nz)),
            dma((2, nz)),
            dma((2,)),
            dma((2, nz)),
            dma((2, nz)),
            dma((7,)),
            dma((7,)),
        ]
        + Reduce.scratch(2, nz, half, width),
        cost_estimate=busy(70),
        compiler_params=comm(5),
    )(part, mine_rows, other_rows, rows, vectors, keep, give, joined_in, dense_in)


def turned(values, cosine, low, high):
    half_rot = ROT // 2
    return (
        values * cosine
        + pltpu.roll(values, values.shape[1] - half_rot, 1) * low
        + pltpu.roll(values, half_rot, 1) * high
    )


def block_rows(order, ref, piece, first, count):
    return jnp.concatenate(
        [ref[pl.ds(pl.multiple_of(order[first + i] * piece, piece), piece), :] for i in range(count)], axis=0
    )


def attention_kernel(piece, order, fused, tables, allowed, qkv, probs_out, mixed):
    groups, held = allowed.shape[0], allowed.shape[1]
    per = held // piece
    for g in range(groups):
        at = pl.ds(g * held, held)
        rows = block_rows(order, fused, piece, g * per, per)
        turn_by = [tables[i, at] for i in range(3)]
        query = turned(rows[:, :HD], *turn_by).astype(BF16)
        keys = turned(rows[:, HD : 2 * HD], *turn_by).astype(BF16)
        values = rows[:, 2 * HD :].astype(BF16)
        qkv[at, :HD] = query
        qkv[at, HD : 2 * HD] = keys
        qkv[at, 2 * HD :] = values
        scores = jnp.where(allowed[g] > 0.5, dot(query, keys, (1, 1)) / math.sqrt(HD), masked_score)
        weights = jnp.exp(scores - jnp.max(scores, axis=-1, keepdims=True))
        probs = weights / jnp.sum(weights, axis=-1, keepdims=True)
        probs_out[g] = probs
        mixed[at] = dot(probs.astype(BF16), values, (1, 0)).astype(BF16)


def attention(order, fused, tables, allowed, piece):
    total = fused.shape[0]
    return pl.pallas_call(
        functools.partial(attention_kernel, piece),
        out_shape=[
            jax.ShapeDtypeStruct((total, 3 * HD), BF16),
            jax.ShapeDtypeStruct(allowed.shape, F32),
            jax.ShapeDtypeStruct((total, HD), BF16),
        ],
        in_specs=[pl.BlockSpec(memory_space=pltpu.SMEM)] + [vmem()] * 3,
        out_specs=[vmem()] * 3,
        compiler_params=pltpu.CompilerParams(vmem_limit_bytes=32 << 20),
    )(order, fused, tables, allowed)


def place_kernel(piece, order, mixed, active, out):
    per = 2
    out[:, :HD] = mixed[...]
    for g in range(mixed.shape[0] // (per * piece)):
        out[pl.ds(g * per * piece, per * piece), HD:] = block_rows(order, active, piece, g * per, per)


def place(order, mixed, active, piece):
    total = mixed.shape[0]
    return pl.pallas_call(
        functools.partial(place_kernel, piece),
        out_shape=jax.ShapeDtypeStruct((total, HD + active.shape[1]), BF16),
        in_specs=[pl.BlockSpec(memory_space=pltpu.SMEM)] + [vmem()] * 2,
        out_specs=vmem(),
        compiler_params=pltpu.CompilerParams(vmem_limit_bytes=32 << 20),
    )(order, mixed, active)


def attention_back_kernel(
    piece, order, dbranch, wout, slope, qkv, probs_in, tables, dfused, dhidden, sums, douts
):
    tile = 4 * piece

    def back(i, carry):
        at = pl.ds(pl.multiple_of(i * tile, tile), tile)
        douts[at] = dot(dbranch[at], wout[...], (1, 1))
        return carry

    lax.fori_loop(0, dbranch.shape[0] // tile, back, 0)
    groups, held = probs_in.shape[0], probs_in.shape[1]
    per = held // piece
    joined_sum = jnp.zeros((1, 3 * HD), F32)
    hidden_sum = jnp.zeros((1, slope.shape[1]), F32)
    for g in range(groups):
        at = pl.ds(g * held, held)
        query, keys, values = qkv[at, :HD], qkv[at, HD : 2 * HD], qkv[at, 2 * HD :]
        dmixed = douts[at, :HD].astype(BF16)
        probs = probs_in[g]
        dvalues = dot(probs.astype(BF16), dmixed, (0, 0))
        dprobs = dot(dmixed, values, (1, 1))
        dscores = (probs * (dprobs - jnp.sum(probs * dprobs, axis=-1, keepdims=True))).astype(BF16)
        turn_by = [tables[0, at], -tables[1, at], -tables[2, at]]
        dquery = turned(dot(dscores, keys, (1, 0)) / math.sqrt(HD), *turn_by)
        dkeys = turned(dot(dscores, query, (0, 0)) / math.sqrt(HD), *turn_by)
        whole = jnp.concatenate([dquery, dkeys, dvalues], axis=1).astype(BF16)
        joined_sum = joined_sum + jnp.sum(whole.astype(F32), axis=0, keepdims=True)
        for i in range(per):
            to = pl.ds(pl.multiple_of(order[g * per + i] * piece, piece), piece)
            dfused[to, :] = whole[i * piece : (i + 1) * piece]
            grown = (douts[pl.ds(g * held + i * piece, piece), HD:] * slope[to, :]).astype(BF16)
            dhidden[to, :] = grown
            hidden_sum = hidden_sum + jnp.sum(grown.astype(F32), axis=0, keepdims=True)
    sums[:, : 3 * HD] = joined_sum
    sums[:, 3 * HD :] = hidden_sum


def attention_back(order, dbranch, wout, slope, qkv, probs, tables, piece):
    total, units = slope.shape
    return pl.pallas_call(
        functools.partial(attention_back_kernel, piece),
        out_shape=[
            jax.ShapeDtypeStruct((total, 3 * HD), BF16),
            jax.ShapeDtypeStruct((total, units), BF16),
            jax.ShapeDtypeStruct((1, 3 * HD + units), F32),
        ],
        in_specs=[pl.BlockSpec(memory_space=pltpu.SMEM)] + [vmem()] * 6,
        out_specs=[vmem()] * 3,
        scratch_shapes=[pltpu.VMEM((total, wout.shape[0]), F32)],
        cost_estimate=pl.CostEstimate(flops=0, bytes_accessed=1000, transcendentals=0),
        compiler_params=pltpu.CompilerParams(vmem_limit_bytes=48 << 20),
    )(order, dbranch, wout, slope, qkv, probs, tables)


def fast_shards(
    residual,
    lengths,
    pair_order,
    token_ids,
    desirable,
    ref_match,
    ref_pair,
    attn_gain,
    attn_shift,
    mlp_gain,
    mlp_shift,
    w_joined,
    b_joined,
    w_dense,
    b_dense,
    w_up,
    b_up,
    w_down,
    b_down,
    final_gain,
    final_shift,
    w_vocab,
):
    nz, ny, nx = lax.axis_size("z"), lax.axis_size("y"), lax.axis_size("x")
    n = nz * ny
    chips = n * nx
    iz, iy, ix, ic = (lax.axis_index(a) for a in ALL)
    dp = iz * ny + iy
    held, width = residual.shape
    total = n * held
    blocks = 2 * n
    piece = held // 2
    seqs = lengths.shape[1]
    depth = width // n
    vcols = w_vocab.shape[1] // n
    ffs = w_up.shape[1] // n
    hcols = 3 * HD
    mine = ix * 2 + ic

    info = jnp.stack(
        [
            token_ids.astype(F32),
            ref_match,
            ref_pair,
            jnp.concatenate(
                [lengths[0].astype(F32), desirable.astype(F32), jnp.zeros((held - 2 * seqs,), F32)]
            ),
        ]
    )
    bias_own = jnp.concatenate([b_joined, b_up]).astype(F32)
    natural, info, bias_other, wj, wout, wup, vocab_across = front(
        nz, residual, info, bias_own.reshape(-1, HD), w_joined, w_dense, w_down, w_up, w_vocab
    )
    bias_other = bias_other.reshape(-1)

    send_vocab = vocab_across.reshape(n, vcols, depth)
    vocab_got = exchange(send_vocab)
    bias_first = jnp.where(ic == 0, bias_own, bias_other)
    bias_second = jnp.where(ic == 0, bias_other, bias_own)
    bj_all = jnp.where(iy == 0, bias_first, bias_second)[: nz * hcols].reshape(nz, hcols)
    bj = lax.dynamic_index_in_dim(bj_all, iz, 0, keepdims=False)
    bu_all = jnp.stack([bias_own[nz * hcols :], bias_other[nz * hcols :]]).reshape(2, n, ffs)
    bu = lax.dynamic_index_in_dim(bu_all, dp, 1, keepdims=False).reshape(2 * ffs)

    ids = info[:, 0].astype(jnp.int32)
    refs = jnp.stack([info[:, 1], info[:, 2]])
    lens = info[:, 3, :seqs].astype(jnp.int32)
    wanted = info[:, 3, seqs : 2 * seqs]
    slots = jnp.arange(blocks, dtype=jnp.int32)
    anchor = jnp.sum(
        jnp.where(pair_order[None, :] == slots[:, None], slots[None, :], 0), axis=1
    )
    order = jnp.where(ic == 0, slots, anchor)
    back = jnp.where(ic == 0, slots, pair_order)
    anchor_hot = (anchor[:, None] == slots[None, :])[:, :, None]
    pair_ids = jnp.sum(jnp.where(anchor_hot, ids.reshape(1, blocks, piece), 0), axis=1).reshape(n, held)
    all_ids = jnp.stack([ids, pair_ids])

    ends = jnp.stack([jnp.sum(lens[:, : s + 1], axis=1) for s in range(seqs)], axis=1)
    starts = ends - lens
    places = jnp.arange(held, dtype=jnp.int32)
    segment = jnp.sum((places[None, :, None] >= ends[:, None, :]).astype(jnp.int32), axis=2)
    hot = (segment[:, :, None] == jnp.arange(seqs, dtype=jnp.int32)).astype(F32)
    position = places[None, :] - jnp.sum(hot * starts[:, None, :].astype(F32), axis=2).astype(jnp.int32)
    allowed = (segment[:, :, None] == segment[:, None, :]) & (places[None, :, None] >= places[None, None, :])
    scored = jnp.concatenate(
        [segment[:, 1:] == segment[:, :-1], jnp.zeros((n, 1), jnp.bool_)], axis=1
    ).astype(F32)
    targets = jnp.concatenate([all_ids[:, :, 1:], jnp.zeros((2, n, 1), jnp.int32)], axis=2)

    hat, inverse = normed(natural.astype(F32))
    ga, sa, gm, sm, gf, sf = (
        v.astype(F32) for v in (attn_gain, attn_shift, mlp_gain, mlp_shift, final_gain, final_shift)
    )
    attn_low = (hat * ga + sa).astype(BF16)
    mlp_low = (hat * gm + sm).astype(BF16)
    lane = jnp.arange(HD, dtype=jnp.int32)
    frequency = jnp.exp((lane % (ROT // 2)).astype(F32) * (-2.0 * math.log(10000.0) / ROT))
    angles = position.reshape(total)[:, None].astype(F32) * frequency[None, :]
    cosine = jnp.where(lane < ROT, jnp.cos(angles), 1.0)
    sine = jnp.sin(angles)
    tables = jnp.stack(
        [
            cosine,
            jnp.where(lane < ROT // 2, -sine, 0.0),
            jnp.where((lane >= ROT // 2) & (lane < ROT), sine, 0.0),
        ]
    )
    fused = dot(attn_low, wj, (1, 0)) + bj
    qkv, probs, mixed = attention(order, fused, tables, allowed.astype(F32), piece)
    hidden = dot(mlp_low, wup, (1, 0)) + bu
    bell = 0.5 * (1.0 + lax.erf(hidden * math.sqrt(0.5)))
    active = (hidden * bell).astype(BF16)
    gelu_slope = bell + hidden * jnp.exp(-0.5 * hidden * hidden) * (1.0 / math.sqrt(2.0 * math.pi))
    outs_low = place(order, mixed, active, piece)
    branch_part = dot(outs_low, wout, (1, 0)).astype(BF16)
    share = total // chips
    chip = dp * nx + ix
    first_row = jnp.sum(jnp.where(slots == chip * share // piece, order, 0)) * piece + chip * share % piece
    rows_here = lax.dynamic_slice_in_dim(natural, first_row, share, 0)
    bias_out = (b_dense.astype(F32) + b_down.astype(F32))[None]
    final, resid = reduce_norm_gather(nz, branch_part, rows_here, bias_out, gf[None], sf[None])

    vocab_got, final = lax.optimization_barrier((vocab_got, final))
    vocab_own = vocab_got.transpose(1, 0, 2).reshape(vcols, width)
    vocab_other = swap(vocab_got).transpose(1, 0, 2).reshape(vcols, width)
    my_targets = jnp.where(ic == 0, targets[0], targets[1]).reshape(total)
    logits = [dot(final, w, (1, 1)) for w in (vocab_own, vocab_other)]
    hits = [
        lax.broadcasted_iota(jnp.int32, (total, vcols), 1)
        == (my_targets - ((ix * 2 + core) * n + dp) * vcols)[:, None]
        for core in (ic, 1 - ic)
    ]
    tops = [jnp.max(part, axis=1) for part in logits]
    top = jnp.maximum(tops[0], tops[1])
    sums = sum(jnp.sum(jnp.exp(part - top[:, None]), axis=1) for part in logits)
    picks = sum(jnp.sum(jnp.where(h, part, 0.0), axis=1) for h, part in zip(hits, logits))
    stats = jnp.stack([top, sums, picks]).reshape(3, n, held)
    coef, my_lse, scalars = objective(
        nz, n * seqs, stats, hot.transpose(2, 0, 1), scored, refs, lens.astype(F32), wanted
    )
    coef, my_lse = coef.reshape(total), my_lse.reshape(total)
    kto_loss, kl_estimate = scalars[0, 0, 0], scalars[1, 0, 0]

    dlogits = [
        (coef[:, None] * (jnp.where(h, 1.0, 0.0) - jnp.exp(part - my_lse[:, None]))).astype(BF16)
        for h, part in zip(hits, logits)
    ]
    gv_other = dot(dlogits[1], final, (0, 0)).astype(BF16)
    dfinal_other = dot(dlogits[1], vocab_other, (1, 0)).astype(F32)
    gv_own = dot(dlogits[0], final, (0, 0))
    gv = (gv_own + swap(gv_other).astype(F32)).astype(BF16)
    gv, dlogits_own = lax.optimization_barrier((gv, dlogits[0]))
    dfinal_part = (dot(dlogits_own, vocab_own, (1, 0)) + dfinal_other).astype(BF16)
    gv = gv.reshape(vcols, n, depth).transpose(1, 0, 2)
    early_cols = vcols * 336 // 800
    grad_early = exchange(gv[:, :early_cols])
    dbranch, final_vectors = reduce_back_gather(nz, dfinal_part, resid, gf[None])
    gv_late, dbranch, grad_early = lax.optimization_barrier((gv[:, early_cols:], dbranch, grad_early))
    grad_late = exchange(gv_late)
    grad_vocab = jnp.concatenate([grad_early, grad_late], axis=1).reshape(n * vcols, depth).T
    grad_vocab = with_layout_constraint(lax.optimization_barrier(grad_vocab).astype(F32), Layout((0, 1)))

    dfused, dhidden, bias_sums = attention_back(
        order, dbranch, wout, gelu_slope, qkv, probs, tables, piece
    )
    dhidden, outs_low = lax.optimization_barrier((dhidden, outs_low))
    gout = dot(outs_low, dbranch, (0, 0))
    gu = dot(mlp_low, dhidden, (0, 0))

    def to_send(up, down):
        return jnp.concatenate(
            [up.reshape(n, depth, ffs), down.reshape(ffs, n, depth).transpose(1, 0, 2)], axis=1
        )

    give_grads = to_send(gu[:, ffs:].astype(BF16), gout[HD + ffs :].astype(BF16))
    layer_grads = to_send(gu[:, :ffs], gout[HD : HD + ffs]) + swap(give_grads).astype(F32)
    layer_grads, dfused, dhidden = lax.optimization_barrier((layer_grads.astype(BF16), dfused, dhidden))
    layer_grads = exchange(layer_grads)
    gj = dot(attn_low, dfused, (0, 0)).astype(BF16)
    dattn = dot(dfused, wj, (1, 1))
    dmlp = dot(dhidden, wup, (1, 1))
    g_attn_gain = jnp.sum(dattn * hat, axis=0)
    g_attn_shift = jnp.sum(dattn, axis=0)
    g_mlp_gain = jnp.sum(dmlp * hat, axis=0)
    g_mlp_shift = jnp.sum(dmlp, axis=0)
    t_part = (dattn * ga + dmlp * gm).astype(BF16)
    grad_up = layer_grads[:, :depth].transpose(1, 0, 2).reshape(depth, n * ffs).astype(F32)
    grad_down = layer_grads[:, depth:].reshape(n * ffs, depth).astype(F32)

    share2 = total // (2 * chips)

    def natural_rows(core):
        first = dp * held + (ix * 2 + core) * share2
        place = jnp.sum(jnp.where(slots == first // piece, back, 0)) * piece + first % piece
        return lax.dynamic_slice_in_dim(dbranch, place, share2, 0)

    gbj, gbu = bias_sums[0, :hcols], bias_sums[0, hcols:]
    spare = jnp.zeros((8 * HD - hcols - ffs,), F32)
    keep = jnp.concatenate([gbj, gbu[:ffs], spare]).reshape(8, HD)
    give = jnp.concatenate([gbj, gbu[ffs:], spare]).reshape(8, HD)
    vectors = jnp.concatenate(
        [
            jnp.stack([g_attn_gain, g_attn_shift, g_mlp_gain, g_mlp_shift]),
            final_vectors,
            jnp.zeros((1, width), F32),
        ]
    )
    grad_vocab, t_part = lax.optimization_barrier((grad_vocab, t_part))
    rows_out, vectors, biases, grad_joined, grad_dense = end(
        nz,
        t_part.reshape(nz, 2, 2, 2, share2, width),
        natural_rows(ic),
        natural_rows(1 - ic),
        lax.dynamic_slice_in_dim(residual, mine * share2, share2, 0),
        vectors,
        keep,
        give,
        gj,
        gout[:HD].astype(BF16),
    )
    grad_input = rows_out.reshape(held, width).astype(F32)
    grad_joined, grad_dense = grad_joined.astype(F32), grad_dense.astype(F32)
    g_attn_gain, g_attn_shift, g_mlp_gain, g_mlp_shift, g_final_gain, g_final_shift, g_out = vectors[:7]
    biases = biases.reshape(nz, 2, 8 * HD)
    gb_joined = jnp.where(ic == 0, biases[:, 0, :hcols], biases[:, 1, :hcols]).reshape(nz * hcols)
    gb_up = biases[:, :, hcols : hcols + ffs].reshape(n * ffs)
    return (
        kto_loss,
        kl_estimate,
        grad_input,
        g_attn_gain,
        g_attn_shift,
        g_mlp_gain,
        g_mlp_shift,
        grad_joined,
        gb_joined,
        grad_dense,
        g_out,
        grad_up,
        gb_up,
        grad_down,
        g_out,
        g_final_gain,
        g_final_shift,
        grad_vocab,
    )


def placed(dp, mp):
    ins = (
        P(dp, None),
        P(dp, None),
        P(),
        P(dp),
        P(dp),
        P(dp),
        P(dp),
        P(),
        P(),
        P(),
        P(),
        P(dp, mp),
        P(mp),
        P(mp, dp),
        P(),
        P(dp, mp),
        P(mp),
        P(mp, dp),
        P(),
        P(),
        P(),
        P(dp, mp),
    )
    outs = (
        P(),
        P(),
        P(dp, None),
        P(),
        P(),
        P(),
        P(),
        P(dp, mp),
        P(mp),
        P(mp, dp),
        P(),
        P(dp, mp),
        P(mp),
        P(mp, dp),
        P(),
        P(),
        P(),
        P(dp, mp),
    )
    return ins, outs


def solution(mesh):
    n_dp, n_mp = mesh.shape["dp"], mesh.shape["mp"]
    if n_dp == 8 and n_mp == 4:
        fine = jax.sharding.Mesh(mesh.devices.reshape(n_dp // 2, 2, n_mp // 2, 2), ALL)
        ins, outs = placed(DP, ("x", "c"))
        return jax.shard_map(fast_shards, mesh=fine, in_specs=ins, out_specs=outs, check_vma=False)
    ins, outs = placed("dp", "mp")
    return jax.shard_map(shards, mesh=mesh, in_specs=ins, out_specs=outs, check_vma=False)
```

```python
import functools
import math

import jax
import jax.numpy as jnp
from jax import lax
from jax.experimental import pallas as pl
from jax.experimental.layout import Layout, with_layout_constraint
from jax.experimental.pallas import tpu as pltpu
from jax.sharding import PartitionSpec as P

HD = 128
ROT = 32


kto_beta = 4.0
norm_eps = 1e-05
masked_score = -1e30


def joined(value, axis, join):
    pieces = jax.tree.map(lambda part: lax.all_gather(part, axis), value)
    head = jax.tree.map(lambda part: part[0], pieces)
    tail = jax.tree.map(lambda part: part[1:], pieces)
    subtotal, _ = lax.scan(lambda subtotal, piece: (join(subtotal, piece), None), head, tail)
    return subtotal


def layer_norm(values, norm_gain, norm_shift):
    centred = values - jnp.mean(values, axis=-1, keepdims=True)
    spread = jnp.mean(centred * centred, axis=-1, keepdims=True)
    return centred * lax.rsqrt(spread + norm_eps) * norm_gain + norm_shift


def rotate(values, position):
    half_rot = ROT // 2
    inverse = jnp.exp(jnp.arange(half_rot, dtype=jnp.float32) * (-2.0 * math.log(10000.0) / ROT))
    angles = position.astype(jnp.float32)[:, None] * inverse[None, :]
    cosine_table = jnp.cos(angles)[:, None, :]
    sine_table = jnp.sin(angles)[:, None, :]
    first_half = values[..., :half_rot]
    second_half = values[..., half_rot:ROT]
    return jnp.concatenate(
        [
            first_half * cosine_table - second_half * sine_table,
            second_half * cosine_table + first_half * sine_table,
            values[..., ROT:],
        ],
        axis=-1,
    )


def gelu_exact(values):
    return jax.nn.gelu(values, approximate=False)


def attention_scores(query_low, keys_low, allowed):
    raw_scores = jnp.einsum(
        "rhd,chd->hrc", query_low, keys_low, preferred_element_type=jnp.float32
    ) / math.sqrt(HD)
    return jnp.where(allowed[None], raw_scores, masked_score)


def combine_vocab(first, second):
    high_first, total_first, pick_first = first
    high_second, total_second, pick_second = second
    highest = jnp.maximum(high_first, high_second)
    merged_total = total_first * jnp.exp(high_first - highest) + total_second * jnp.exp(
        high_second - highest
    )
    return (highest, merged_total, pick_first + pick_second)


def gather_weights(weights_low):
    w_joined, w_up, w_vocab, w_dense, w_down = weights_low
    joined_all, up_all, vocab_all = (
        lax.all_gather(w_joined, "dp", axis=0, tiled=True),
        lax.all_gather(w_up, "dp", axis=0, tiled=True),
        lax.all_gather(w_vocab, "dp", axis=0, tiled=True),
    )
    dense_all, down_all = (
        lax.all_gather(w_dense, "dp", axis=1, tiled=True),
        lax.all_gather(w_down, "dp", axis=1, tiled=True),
    )
    return (joined_all, up_all, vocab_all, dense_all, down_all)


def forward_pass(gathered, smalls, rows_low, allowed, position, targets):
    joined_all, up_all, vocab_all, dense_all, down_all = gathered
    (
        attn_gain,
        attn_shift,
        mlp_gain,
        mlp_shift,
        b_joined,
        b_dense,
        b_up,
        b_down,
        final_gain,
        final_shift,
    ) = smalls
    rows_float = rows_low.astype(jnp.float32)
    count_rows = rows_float.shape[0]
    attn_low = layer_norm(rows_float, attn_gain, attn_shift).astype(jnp.bfloat16)
    mlp_low = layer_norm(rows_float, mlp_gain, mlp_shift).astype(jnp.bfloat16)
    joined_cols = jnp.dot(attn_low, joined_all, preferred_element_type=jnp.float32) + b_joined
    joined_cols = joined_cols.reshape(count_rows, -1, 3, HD)
    query_low = rotate(joined_cols[:, :, 0], position).astype(jnp.bfloat16)
    keys_low = rotate(joined_cols[:, :, 1], position).astype(jnp.bfloat16)
    values_low = joined_cols[:, :, 2].astype(jnp.bfloat16)
    scores = attention_scores(query_low, keys_low, allowed)
    highest = jnp.max(scores, axis=-1, keepdims=True)
    scaled_exp = jnp.exp(scores - highest)
    totals = jnp.sum(scaled_exp, axis=-1, keepdims=True)
    probs_low = (scaled_exp / totals).astype(jnp.bfloat16)
    score_lse = highest + jnp.log(totals)
    mixed_low = (
        jnp.einsum("hrc,chd->rhd", probs_low, values_low, preferred_element_type=jnp.float32)
        .reshape(count_rows, -1)
        .astype(jnp.bfloat16)
    )
    hidden = jnp.dot(mlp_low, up_all, preferred_element_type=jnp.float32) + b_up
    active_low = gelu_exact(hidden).astype(jnp.bfloat16)
    branch_part = jnp.dot(mixed_low, dense_all, preferred_element_type=jnp.float32) + jnp.dot(
        active_low, down_all, preferred_element_type=jnp.float32
    )
    branch = lax.psum(branch_part, "mp")
    resid_sum = rows_float + branch + b_dense + b_down
    final_low = layer_norm(resid_sum, final_gain, final_shift).astype(jnp.bfloat16)
    logits = jnp.dot(final_low, vocab_all, preferred_element_type=jnp.float32)
    local_high = jnp.max(logits, axis=-1)
    local_total = jnp.sum(jnp.exp(logits - local_high[:, None]), axis=-1)
    column = targets - lax.axis_index("mp") * logits.shape[1]
    target_hit = lax.broadcasted_iota(jnp.int32, logits.shape, 1) == column[:, None]
    local_pick = jnp.sum(jnp.where(target_hit, logits, 0.0), axis=-1)
    high_all, total_all, picked = joined((local_high, local_total, local_pick), "mp", combine_vocab)
    vocab_lse = high_all + jnp.log(total_all)
    return (
        attn_low,
        mlp_low,
        joined_cols,
        query_low,
        keys_low,
        values_low,
        score_lse,
        mixed_low,
        hidden,
        active_low,
        resid_sum,
        final_low,
        logits,
        vocab_lse,
        target_hit,
        picked - vocab_lse,
    )


def shards(
    residual,
    lengths,
    pair_order,
    token_ids,
    desirable,
    ref_match,
    ref_pair,
    attn_gain,
    attn_shift,
    mlp_gain,
    mlp_shift,
    w_joined,
    b_joined,
    w_dense,
    b_dense,
    w_up,
    b_up,
    w_down,
    b_down,
    final_gain,
    final_shift,
    w_vocab,
):
    dp_count = lax.axis_size("dp")
    tokens_here = residual.shape[0]
    piece_rows = tokens_here // 2
    width = residual.shape[1]
    seq_here = lengths.shape[1]
    block_count = 2 * dp_count
    my_index = lax.axis_index("dp")
    block_slots = jnp.arange(block_count, dtype=jnp.int32)
    my_blocks = 2 * my_index + jnp.arange(2, dtype=jnp.int32)
    my_targets = jnp.sum(
        jnp.where(block_slots[None, :] == my_blocks[:, None], pair_order[None, :], 0), axis=1
    )
    send_hot = my_targets[:, None] == block_slots[None, :]
    own_blocks = residual.reshape(2, piece_rows, width)
    own_ids = token_ids.reshape(2, piece_rows)
    sent_rows = jnp.einsum(
        "ht,hpd->tpd", send_hot.astype(jnp.bfloat16), own_blocks, preferred_element_type=jnp.float32
    ).astype(jnp.bfloat16)
    sent_ids = jnp.sum(jnp.where(send_hot[:, :, None], own_ids[:, None, :], 0), axis=0)
    got_rows, got_ids = (
        lax.all_to_all(
            sent_rows.reshape(dp_count, 2, piece_rows, width),
            "dp",
            split_axis=0,
            concat_axis=0,
            tiled=True,
        ),
        lax.all_to_all(
            sent_ids.reshape(dp_count, 2, piece_rows), "dp", split_axis=0, concat_axis=0, tiled=True
        ),
    )
    paired_rows = jnp.sum(got_rows.astype(jnp.float32), axis=0).astype(jnp.bfloat16)
    paired_ids = jnp.sum(got_ids, axis=0)
    rows_low = jnp.concatenate([residual, paired_rows.reshape(tokens_here, width)], axis=0)
    ids_all = jnp.concatenate([token_ids, paired_ids.reshape(tokens_here)], axis=0)
    seq_lengths = lengths[0]
    seq_slots = jnp.arange(seq_here, dtype=jnp.int32)
    seq_ends = jnp.sum(
        jnp.where(seq_slots[None, :] <= seq_slots[:, None], seq_lengths[None, :], 0), axis=1
    )
    seq_starts = seq_ends - seq_lengths
    places = jnp.arange(tokens_here, dtype=jnp.int32)
    segment = jnp.sum((places[:, None] >= seq_ends[None, :]).astype(jnp.int32), axis=1)
    own_start = jnp.sum(
        jnp.where(segment[:, None] == seq_slots[None, :], seq_starts[None, :], 0), axis=1
    )
    position_half = places - own_start
    segment_all = jnp.concatenate([segment, segment + seq_here])
    position = jnp.concatenate([position_half, position_half])
    count_rows = 2 * tokens_here
    row_index = jnp.arange(count_rows, dtype=jnp.int32)
    allowed = (segment_all[:, None] == segment_all[None, :]) & (
        row_index[None, :] <= row_index[:, None]
    )
    targets = jnp.concatenate([ids_all[1:], jnp.zeros((1,), jnp.int32)])
    scored = jnp.concatenate(
        [segment_all[1:] == segment_all[:-1], jnp.zeros((1,), jnp.bool_)]
    ).astype(jnp.float32)
    ref_rows = jnp.concatenate([ref_match, ref_pair])
    length_float = seq_lengths.astype(jnp.float32)
    length_both = jnp.concatenate([length_float, length_float])
    seq_match = segment_all[:, None] == jnp.arange(2 * seq_here, dtype=jnp.int32)[None, :]
    smalls = tuple(
        (
            value.astype(jnp.float32)
            for value in (
                attn_gain,
                attn_shift,
                mlp_gain,
                mlp_shift,
                b_joined,
                b_dense,
                b_up,
                b_down,
                final_gain,
                final_shift,
            )
        )
    )
    weights_low = (w_joined, w_up, w_vocab, w_dense, w_down)
    gathered = gather_weights(weights_low)
    first_pass = forward_pass(gathered, smalls, rows_low, allowed, position, targets)
    token_terms = (first_pass[15] - ref_rows) * scored
    seq_means = jnp.sum(jnp.where(seq_match, token_terms[:, None], 0.0), axis=0) / length_both
    kl_total = lax.psum(jnp.sum(seq_means[seq_here:]), "dp")
    seq_total = seq_here * dp_count
    kl_estimate = kl_total / seq_total
    signs = 2.0 * desirable.astype(jnp.float32) - 1.0
    sigmoid_val = jax.nn.sigmoid(kto_beta * signs * (seq_means[:seq_here] - kl_estimate))
    slope = -kto_beta * signs * sigmoid_val * (1.0 - sigmoid_val)
    kto_loss, slope_total = lax.psum((jnp.sum(1.0 - sigmoid_val), jnp.sum(slope)), "dp")
    seq_coef = (
        jnp.concatenate([slope, jnp.broadcast_to(-slope_total / seq_total, (seq_here,))])
        / length_both
    )
    token_coef = jnp.sum(jnp.where(seq_match, seq_coef[None, :], 0.0), axis=1) * scored
    matrices = gather_weights(weights_low)
    current = forward_pass(matrices, smalls, rows_low, allowed, position, targets)
    joined_all, up_all, vocab_all, dense_all, down_all = matrices
    (
        attn_low,
        mlp_low,
        joined_cols,
        query_low,
        keys_low,
        values_low,
        score_lse,
        mixed_low,
        hidden,
        active_low,
        resid_sum,
        final_low,
        logits,
        vocab_lse,
        target_hit,
        log_probs,
    ) = current
    softmax_local = jnp.exp(logits - vocab_lse[:, None])
    dlogits = (token_coef[:, None] * (jnp.where(target_hit, 1.0, 0.0) - softmax_local)).astype(
        jnp.bfloat16
    )
    grad_vocab = jnp.einsum("rd,rv->dv", final_low, dlogits, preferred_element_type=jnp.float32)
    dfinal_part = jnp.einsum("rv,dv->rd", dlogits, vocab_all, preferred_element_type=jnp.float32)
    dfinal = lax.psum(dfinal_part, "mp")
    _, final_pull = jax.vjp(layer_norm, resid_sum, smalls[8], smalls[9])
    dresid, grad_final_gain, grad_final_shift = final_pull(dfinal)
    grad_b_out = jnp.sum(dresid, axis=0)
    dbranch = dresid.astype(jnp.bfloat16)
    grad_dense = jnp.einsum("rk,rd->kd", mixed_low, dbranch, preferred_element_type=jnp.float32)
    grad_down = jnp.einsum("rf,rd->fd", active_low, dbranch, preferred_element_type=jnp.float32)
    dmixed = jnp.einsum("rd,kd->rk", dbranch, dense_all, preferred_element_type=jnp.float32).astype(
        jnp.bfloat16
    )
    dactive = jnp.einsum("rd,fd->rf", dbranch, down_all, preferred_element_type=jnp.float32)
    _, gelu_pull = jax.vjp(gelu_exact, hidden)
    dhidden = gelu_pull(dactive)[0].astype(jnp.bfloat16)
    grad_up = jnp.einsum("rd,rf->df", mlp_low, dhidden, preferred_element_type=jnp.float32)
    grad_b_up = jnp.sum(dhidden.astype(jnp.float32), axis=0)
    dmlp_part = jnp.einsum("rf,df->rd", dhidden, up_all, preferred_element_type=jnp.float32)
    dmixed_heads = dmixed.reshape(count_rows, -1, HD)
    scores = attention_scores(query_low, keys_low, allowed)
    probs_float = jnp.where(allowed[None], jnp.exp(scores - score_lse), 0.0)
    dvalues = jnp.einsum(
        "hrc,rhd->chd",
        probs_float.astype(jnp.bfloat16),
        dmixed_heads,
        preferred_element_type=jnp.float32,
    )
    dprobs = jnp.einsum(
        "rhd,chd->hrc", dmixed_heads, values_low, preferred_element_type=jnp.float32
    )
    inner_sum = jnp.sum(probs_float * dprobs, axis=-1, keepdims=True)
    dscores = (probs_float * (dprobs - inner_sum)).astype(jnp.bfloat16)
    dquery = jnp.einsum(
        "hrc,chd->rhd", dscores, keys_low, preferred_element_type=jnp.float32
    ) / math.sqrt(HD)
    dkeys = jnp.einsum(
        "hrc,rhd->chd", dscores, query_low, preferred_element_type=jnp.float32
    ) / math.sqrt(HD)
    _, rotate_pull = jax.vjp(lambda value: rotate(value, position), joined_cols[:, :, 0])
    dfused = jnp.stack([rotate_pull(dquery)[0], rotate_pull(dkeys)[0], dvalues], axis=2)
    dfused = dfused.reshape(count_rows, -1).astype(jnp.bfloat16)
    grad_joined = jnp.einsum("rd,re->de", attn_low, dfused, preferred_element_type=jnp.float32)
    grad_b_joined = jnp.sum(dfused.astype(jnp.float32), axis=0)
    dattn_part = jnp.einsum("re,de->rd", dfused, joined_all, preferred_element_type=jnp.float32)
    dattn, dmlp = lax.psum((dattn_part, dmlp_part), "mp")
    rows_float = rows_low.astype(jnp.float32)
    _, attn_pull = jax.vjp(layer_norm, rows_float, smalls[0], smalls[1])
    drows_attn, grad_attn_gain, grad_attn_shift = attn_pull(dattn)
    _, mlp_pull = jax.vjp(layer_norm, rows_float, smalls[2], smalls[3])
    drows_mlp, grad_mlp_gain, grad_mlp_shift = mlp_pull(dmlp)
    drows = dresid + drows_attn + drows_mlp
    my_slots = 2 * my_index + jnp.arange(2, dtype=jnp.int32)
    anchor = jnp.sum(
        jnp.where(pair_order[None, :] == my_slots[:, None], block_slots[None, :], 0), axis=1
    )
    back_hot = (anchor[:, None] == block_slots[None, :]).astype(jnp.float32)
    back_blocks = drows[tokens_here:].reshape(2, piece_rows, width)
    back_sent = jnp.einsum("st,spd->tpd", back_hot, back_blocks, precision=lax.Precision.HIGHEST)
    returned = lax.all_to_all(
        back_sent.reshape(dp_count, 2, piece_rows, width),
        "dp",
        split_axis=0,
        concat_axis=0,
        tiled=True,
    )
    grad_input = drows[:tokens_here] + jnp.sum(returned, axis=0).reshape(tokens_here, width)
    gw_joined, gw_up, gw_vocab = (
        lax.psum_scatter(grad_joined, "dp", scatter_dimension=0, tiled=True),
        lax.psum_scatter(grad_up, "dp", scatter_dimension=0, tiled=True),
        lax.psum_scatter(grad_vocab, "dp", scatter_dimension=0, tiled=True),
    )
    gw_dense, gw_down = (
        lax.psum_scatter(grad_dense, "dp", scatter_dimension=1, tiled=True),
        lax.psum_scatter(grad_down, "dp", scatter_dimension=1, tiled=True),
    )
    (
        sg_attn_gain,
        sg_attn_shift,
        sg_mlp_gain,
        sg_mlp_shift,
        sg_b_joined,
        sg_b_up,
        sg_b_out,
        sg_final_gain,
        sg_final_shift,
    ) = lax.psum(
        (
            grad_attn_gain,
            grad_attn_shift,
            grad_mlp_gain,
            grad_mlp_shift,
            grad_b_joined,
            grad_b_up,
            grad_b_out,
            grad_final_gain,
            grad_final_shift,
        ),
        "dp",
    )
    return (
        kto_loss,
        kl_estimate,
        grad_input,
        sg_attn_gain,
        sg_attn_shift,
        sg_mlp_gain,
        sg_mlp_shift,
        gw_joined,
        sg_b_joined,
        gw_dense,
        sg_b_out,
        gw_up,
        sg_b_up,
        gw_down,
        sg_b_out,
        sg_final_gain,
        sg_final_shift,
        gw_vocab,
    )


DP = ("z", "y")
CHIPS = ("z", "y", "x")
ALL = ("z", "y", "x", "c")
SWAP = ((0, 1), (1, 0))
F32, BF16 = jnp.float32, jnp.bfloat16
BY_X = (0, 2)
END_BY_X = (0,)


def dot(a, b, contract):
    return lax.dot_general(a, b, ((contract[:1], contract[1:]), ((), ())), preferred_element_type=F32)


def swap(value):
    return lax.ppermute(value, "c", SWAP)


def normed(values):
    centred = values - jnp.mean(values, axis=-1, keepdims=True)
    inverse = lax.rsqrt(jnp.mean(centred * centred, axis=-1, keepdims=True) + norm_eps)
    return centred * inverse, inverse


def norm_back(t, hat, inverse):
    return inverse * (
        t - jnp.mean(t, axis=-1, keepdims=True) - hat * jnp.mean(t * hat, axis=-1, keepdims=True)
    )


def exchange(value):
    return lax.all_to_all(value, DP, split_axis=0, concat_axis=0, tiled=True)


def here():
    return tuple(lax.axis_index(a) for a in ALL)


def send(source, target, out_sem, in_sem, device):
    copy = pltpu.make_async_remote_copy(
        src_ref=source,
        dst_ref=target,
        send_sem=out_sem,
        recv_sem=in_sem,
        device_id=device,
        device_id_type=pl.DeviceIdType.MESH,
    )
    copy.start()
    return copy


def arrived(target, out_sem, in_sem, device):
    pltpu.make_async_remote_copy(
        src_ref=target,
        dst_ref=target,
        send_sem=out_sem,
        recv_sem=in_sem,
        device_id=device,
        device_id_type=pl.DeviceIdType.MESH,
    ).wait_recv()


def left(source, out_sem, in_sem, device):
    pltpu.make_async_remote_copy(
        src_ref=source,
        dst_ref=source,
        send_sem=out_sem,
        recv_sem=in_sem,
        device_id=device,
        device_id_type=pl.DeviceIdType.MESH,
    ).wait_send()


PIECES = 1


def in_pieces(source, target, out_sem, in_sem, device):
    size = source.shape[1] // PIECES
    for i in range(PIECES):
        at = (slice(None), pl.ds(i * size, size))
        send(source.at[at], target.at[at], out_sem, in_sem, device)


def greet(devices):
    barrier = pltpu.get_barrier_semaphore()
    for device in devices:
        pl.semaphore_signal(barrier, inc=1, device_id=device, device_id_type=pl.DeviceIdType.MESH)
    pl.semaphore_wait(barrier, len(devices))


def neighbours(nz):
    iz, iy, ix, ic = here()
    return [(lax.rem(iz + k, nz), iy, ix, ic) for k in range(1, nz)] + [
        (iz, 1 - iy, ix, ic),
        (iz, iy, 1 - ix, ic),
    ]


def other_core():
    iz, iy, ix, ic = here()
    return (iz, iy, ix, 1 - ic)


class Reduce:
    @staticmethod
    def scratch(parts, nz, half, width):
        dma = pltpu.SemaphoreType.DMA
        return [
            pltpu.VMEM((parts, nz, 2, half, width), BF16),
            pltpu.VMEM((parts, nz, half, width), BF16),
            pltpu.VMEM((parts, nz, half, width), BF16),
            pltpu.VMEM((parts, nz, half, width), BF16),
            pltpu.VMEM((parts, nz, half, width), BF16),
            dma((parts, nz, 2)),
            dma((parts, nz, 2)),
            dma((parts, nz)),
            dma((parts, nz)),
            dma((parts, nz)),
            dma((parts, nz)),
        ]

    def __init__(self, nz, half, part, refs, by_x=(0,)):
        self.by_x = by_x
        self.nz, self.half, self.part = nz, half, part
        (
            self.in1,
            self.out2,
            self.in2,
            self.out3,
            self.in3,
            self.s1,
            self.r1,
            self.s2,
            self.r2,
            self.s3,
            self.r3,
        ) = refs
        self.copies = []

    def along(self, h):
        iz, iy, ix, ic = here()
        across_x, across_y = (iz, iy, 1 - ix, ic), (iz, 1 - iy, ix, ic)
        return (across_x, across_y) if h in self.by_x else (across_y, across_x)

    def block(self, h, z, first_mine, second):
        _, iy, ix, _ = here()
        rows = pl.ds(h * self.half, self.half)
        if h in self.by_x:
            return self.part.at[z, second, ix if first_mine else 1 - ix, rows]
        return self.part.at[z, iy if first_mine else 1 - iy, second, rows]

    def mine(self, h):
        _, iy, ix, _ = here()
        return iy if h in self.by_x else ix

    def plane(self, k):
        return lax.rem(here()[0] + k, self.nz)

    def start(self, h, far):
        first, _ = self.along(h)
        second = 1 - self.mine(h) if far else self.mine(h)
        for k in list(range(1, self.nz)) + [0]:
            z = self.plane(k)
            self.copies.append(
                send(
                    self.block(h, z, False, second),
                    self.in1.at[h, z, second],
                    self.s1.at[h, z, second],
                    self.r1.at[h, z, second],
                    first,
                )
            )

    def second(self, h):
        first, across = self.along(h)
        far = 1 - self.mine(h)
        for k in list(range(1, self.nz)) + [0]:
            z = self.plane(k)
            arrived(self.in1.at[h, z, far], self.s1.at[h, z, far], self.r1.at[h, z, far], first)
            self.out2[h, z] = (
                self.block(h, z, True, far)[...].astype(F32) + self.in1[h, z, far].astype(F32)
            ).astype(BF16)
            self.copies.append(
                send(self.out2.at[h, z], self.in2.at[h, z], self.s2.at[h, z], self.r2.at[h, z], across)
            )

    def third(self, h):
        iz, iy, ix, ic = here()
        first, across = self.along(h)
        near = self.mine(h)
        for k in list(range(1, self.nz)) + [0]:
            z = self.plane(k)
            arrived(self.in1.at[h, z, near], self.s1.at[h, z, near], self.r1.at[h, z, near], first)
            arrived(self.in2.at[h, z], self.s2.at[h, z], self.r2.at[h, z], across)
            total = (
                self.block(h, z, True, near)[...].astype(F32)
                + self.in1[h, z, near].astype(F32)
                + self.in2[h, z].astype(F32)
            )
            if k == 0:
                return total
            self.out3[h, k] = total.astype(BF16)
            far = (z, iy, ix, ic)
            in_pieces(self.out3.at[h, k], self.in3.at[h, k], self.s3.at[h, k], self.r3.at[h, k], far)

    def finish(self, h, total):
        _, iy, ix, ic = here()
        for k in range(1, self.nz):
            z = self.plane(self.nz - k)
            arrived(self.in3.at[h, k], self.s3.at[h, k], self.r3.at[h, k], (z, iy, ix, ic))
            total = total + self.in3[h, k].astype(F32)
        return total

    def end(self, parts):
        iz, iy, ix, ic = here()
        for copy in self.copies:
            copy.wait_send()
        for h in parts:
            for k in range(1, self.nz):
                far = (self.plane(k), iy, ix, ic)
                left(self.out3.at[h, k], self.s3.at[h, k], self.r3.at[h, k], far)


class Gather:
    @staticmethod
    def scratch(parts, nz):
        dma = pltpu.SemaphoreType.DMA
        return [dma((parts, nz)), dma((parts, nz)), dma((parts, nz, 2)), dma((parts, nz, 2, 2)), dma((parts,))]

    def __init__(self, nz, half, out, refs, forward=None, by_x=(0,)):
        self.by_x = by_x
        self.nz, self.half, self.out = nz, half, out
        self.sz, self.sp, self.sq, self.r, self.local = refs
        self.copies, self.locals, self.forward = [], [], forward

    def axes(self, h):
        iz, iy, ix, ic = here()
        across_x, across_y = (iz, iy, 1 - ix, ic), (iz, 1 - iy, ix, ic)
        return (across_y, across_x) if h in self.by_x else (across_x, across_y)

    def block(self, h, z, y, x):
        return self.out.at[z, y, x, pl.ds(h * self.half, self.half)]

    def on(self, h, source, z, y, x, which):
        iz, iy, ix, ic = here()
        p, q = self.axes(h)
        there, got = self.block(h, z, y, x), self.r.at[h, z, y, x]
        if "z" in which:
            for k in range(1, self.nz):
                far = (lax.rem(iz + k, self.nz), iy, ix, ic)
                in_pieces(source, there, self.sz.at[h, k], got, far)
        if "p" in which:
            self.copies.append(send(source, there, self.sp.at[h, z], got, p))
        if "q" in which:
            side = x if h not in self.by_x else y
            self.copies.append(send(source, there, self.sq.at[h, z, side], got, q))
        if self.forward is not None:
            self.forward(h, source, z, y, x)

    def start(self, h, source):
        iz, iy, ix, _ = here()
        copy = pltpu.make_async_copy(source, self.block(h, iz, iy, ix), self.local.at[h])
        copy.start()
        self.locals.append(copy)
        self.on(h, source, iz, iy, ix, "zpq")

    def got(self, h, z, y, x):
        arrived(self.block(h, z, y, x), self.sz.at[h, 0], self.r.at[h, z, y, x], self.axes(h)[0])

    def first(self, h, k):
        iz, iy, ix, _ = here()
        z = lax.rem(iz + k, self.nz)
        self.got(h, z, iy, ix)
        self.on(h, self.block(h, z, iy, ix), z, iy, ix, "pq")

    def second(self, h, k):
        iz, iy, ix, _ = here()
        z = lax.rem(iz + k, self.nz)
        y, x = (1 - iy, ix) if h in self.by_x else (iy, 1 - ix)
        self.got(h, z, y, x)
        self.on(h, self.block(h, z, y, x), z, y, x, "q")

    def third(self, h, k):
        iz, iy, ix, _ = here()
        z = lax.rem(iz + k, self.nz)
        for side in (0, 1):
            if h in self.by_x:
                y, x = (iy if side == 0 else 1 - iy), 1 - ix
            else:
                y, x = 1 - iy, (ix if side == 0 else 1 - ix)
            self.got(h, z, y, x)
            if self.forward is not None:
                self.forward(h, self.block(h, z, y, x), z, y, x)

    def turns(self):
        return [1, self.nz - 1] + [k for k in range(2, self.nz - 1)]

    def firsts(self, parts):
        for h in parts:
            self.second(h, 0)
        for k in self.turns():
            for h in parts:
                self.first(h, k)

    def seconds(self, parts):
        for k in self.turns():
            for h in parts:
                self.second(h, k)

    def thirds(self, parts):
        for k in [0] + self.turns():
            for h in parts:
                self.third(h, k)

    def rest(self):
        self.firsts((0, 1))
        self.seconds((0, 1))
        self.thirds((0, 1))

    def end(self, parts):
        iz, iy, ix, ic = here()
        for copy in self.locals:
            copy.wait()
        for copy in self.copies:
            copy.wait_send()
        for h in parts:
            for k in range(1, self.nz):
                far = (lax.rem(iz + k, self.nz), iy, ix, ic)
                left(self.block(h, iz, iy, ix), self.sz.at[h, k], self.r.at[h, iz, iy, ix], far)


def reduce_gather(nz, half, part, out, refs, finished):
    reduce = Reduce(nz, half, part, refs[:11], BY_X)
    gather = Gather(nz, half, out, refs[11:], None, BY_X)
    greet(neighbours(nz))
    early, late = (0, 1), (2, 3)

    def begin(parts):
        for far in (True, False):
            for h in parts:
                reduce.start(h, far)

    def finish(parts, kept):
        for h in parts:
            gather.start(h, finished(h, reduce.finish(h, kept[h])))

    begin(early)
    for h in early:
        reduce.second(h)
    begin(late)
    kept = {h: reduce.third(h) for h in early}
    for h in late:
        reduce.second(h)
    finish(early, kept)
    kept = {h: reduce.third(h) for h in late}
    gather.firsts(early)
    finish(late, kept)
    gather.seconds(early)
    gather.firsts(late)
    gather.thirds(early)
    gather.seconds(late)
    gather.thirds(late)
    gather.end(early + late)
    reduce.end(early + late)


def forward_kernel(nz, half, part, rows, bias, gain, shift, out, resid, fin, *refs):
    def finished(h, total):
        at = pl.ds(h * half, half)
        total = rows[at].astype(F32) + total + bias[...]
        resid[at] = total
        hat, _ = normed(total)
        fin[h] = (hat * gain[...] + shift[...]).astype(BF16)
        return fin.at[h]

    reduce_gather(nz, half, part, out, refs, finished)


def backward_kernel(nz, half, part, resid, gain, out, vectors, fin, *refs):
    sums = []

    def finished(h, total):
        hat, inverse = normed(resid[pl.ds(h * half, half)])
        dresid = norm_back(total * gain[...], hat, inverse)
        fin[h] = dresid.astype(BF16)
        sums.append([jnp.sum(v, axis=0, keepdims=True) for v in (total * hat, total, dresid)])
        return fin.at[h]

    reduce_gather(nz, half, part, out, refs, finished)
    for i in range(3):
        vectors[pl.ds(i, 1)] = sum(part_sums[i] for part_sums in sums)


def vmem():
    return pl.BlockSpec(memory_space=pltpu.VMEM)


def anywhere():
    return pl.BlockSpec(memory_space=pltpu.HBM)


def busy(us):
    return pl.CostEstimate(flops=0, bytes_accessed=us * 3_000_000, transcendentals=0)


def comm(which, limit=22):
    return pltpu.CompilerParams(collective_id=which, has_side_effects=True, vmem_limit_bytes=limit << 20)


def reduce_norm_gather(nz, part, rows, bias, gain, shift):
    share, width = rows.shape
    half = share // 4
    out, resid = pl.pallas_call(
        functools.partial(forward_kernel, nz, half),
        out_shape=[
            jax.ShapeDtypeStruct((nz, 2, 2, share, width), BF16),
            jax.ShapeDtypeStruct((share, width), F32),
        ],
        in_specs=[vmem()] * 5,
        out_specs=[anywhere(), vmem()],
        scratch_shapes=[pltpu.VMEM((4, half, width), BF16)]
        + Reduce.scratch(4, nz, half, width)
        + Gather.scratch(4, nz),
        cost_estimate=busy(90),
        compiler_params=comm(2, 62),
    )(part.reshape(nz, 2, 2, share, width), rows, bias, gain, shift)
    return out.reshape(4 * nz * share, width), resid


def reduce_back_gather(nz, part, resid, gain):
    share, width = resid.shape
    half = share // 4
    out, vectors = pl.pallas_call(
        functools.partial(backward_kernel, nz, half),
        out_shape=[
            jax.ShapeDtypeStruct((nz, 2, 2, share, width), BF16),
            jax.ShapeDtypeStruct((3, width), F32),
        ],
        in_specs=[vmem()] * 3,
        out_specs=[anywhere(), vmem()],
        scratch_shapes=[pltpu.VMEM((4, half, width), BF16)]
        + Reduce.scratch(4, nz, half, width)
        + Gather.scratch(4, nz),
        cost_estimate=busy(90),
        compiler_params=comm(3, 62),
    )(part.reshape(nz, 2, 2, share, width), resid, gain)
    return out.reshape(4 * nz * share, width), vectors


def merge(a, b):
    top = jnp.maximum(a[0], b[0])
    return (top, a[1] * jnp.exp(a[0] - top) + b[1] * jnp.exp(b[0] - top), a[2] + b[2])


def objective_kernel(
    nz, seqs, seq_total, stats, hot, scored, refs, lens, wanted, coef, lse_out, scalars, held, near, far, s1, r1, s2, r2
):
    iz, iy, ix, ic = here()
    plane = [(iz, iy, 1 - ix, ic), (iz, 1 - iy, ix, ic), (iz, 1 - iy, 1 - ix, ic)]
    line = [(lax.rem(iz + k, nz), iy, ix, c) for c in (ic, 1 - ic) for k in range(nz)][1:]
    greet(plane + line)
    copies = []
    for i, device in enumerate(plane):
        copies.append(send(stats, near.at[iy, ix], s1.at[i], r1.at[iy, ix], device))
    near[iy, ix] = stats[...]
    for _, y, x, _ in plane:
        arrived(near.at[y, x], s1.at[0], r1.at[y, x], plane[0])
    sides = [tuple(near[y, x, i] for i in range(3)) for y in (0, 1) for x in (0, 1)]
    current = merge(merge(sides[0], sides[1]), merge(sides[2], sides[3]))
    for i in range(3):
        held[i] = current[i]
        far[iz, ic, i] = current[i]
    for i, device in enumerate(line):
        copies.append(send(held, far.at[iz, ic], s2.at[i], r2.at[iz, ic], device))
    for z, _, _, c in line:
        arrived(far.at[z, c], s2.at[0], r2.at[z, c], line[0])

    def whole(c):
        total = tuple(far[0, c, i] for i in range(3))
        for z in range(1, nz):
            total = merge(total, tuple(far[z, c, i] for i in range(3)))
        lse = total[0] + jnp.log(total[1])
        return lse, total[2] - lse

    (own_lse, own), (pair_lse, pair) = whole(0), whole(1)
    lse_out[...] = jnp.where(ic == 0, own_lse, pair_lse)

    def means(values, ref):
        terms = (values - ref) * scored[...]
        return [
            jnp.sum(terms * hot[s], axis=1, keepdims=True) / lens[:, s : s + 1] for s in range(seqs)
        ]

    own_means, pair_means = means(own, refs[0]), means(pair, refs[1])
    kl = jnp.sum(sum(pair_means), axis=0, keepdims=True) / seq_total
    loss = jnp.zeros((1, 1), F32)
    slopes = []
    for s in range(seqs):
        sign = 2.0 * wanted[:, s : s + 1] - 1.0
        sigmoid = jax.nn.sigmoid(kto_beta * sign * (own_means[s] - kl))
        slopes.append(-kto_beta * sign * sigmoid * (1.0 - sigmoid))
        loss = loss + jnp.sum(1.0 - sigmoid, axis=0, keepdims=True)
    shared = -jnp.sum(sum(slopes), axis=0, keepdims=True) / seq_total
    total = jnp.zeros_like(own)
    for s in range(seqs):
        value = jnp.where(ic == 0, slopes[s], shared) / lens[:, s : s + 1]
        total = total + hot[s] * value
    coef[...] = total * scored[...]
    scalars[0] = jnp.broadcast_to(loss, scalars.shape[1:])
    scalars[1] = jnp.broadcast_to(kl, scalars.shape[1:])
    for copy in copies:
        copy.wait_send()


def objective(nz, seq_total, stats, hot, scored, refs, lens, wanted):
    shape = scored.shape
    dma = pltpu.SemaphoreType.DMA
    return pl.pallas_call(
        functools.partial(objective_kernel, nz, hot.shape[0], seq_total),
        out_shape=[
            jax.ShapeDtypeStruct(shape, F32),
            jax.ShapeDtypeStruct(shape, F32),
            jax.ShapeDtypeStruct((2, 8, 128), F32),
        ],
        in_specs=[vmem()] * 6,
        out_specs=[vmem()] * 3,
        scratch_shapes=[
            pltpu.VMEM((3,) + shape, F32),
            pltpu.VMEM((2, 2, 3) + shape, F32),
            pltpu.VMEM((nz, 2, 3) + shape, F32),
            dma((3,)),
            dma((2, 2)),
            dma((2 * nz - 1,)),
            dma((nz, 2)),
        ],
        cost_estimate=busy(15),
        compiler_params=comm(4),
    )(stats, hot, scored, refs, lens, wanted)


def diagonal(nz):
    iz, iy, ix, ic = here()
    return [(lax.rem(iz + k, nz), 1 - iy, ix, 1 - ic) for k in range(nz)]


def to_head(nz, k, pairs, local_sem, out_sem, in_sem):
    iz, iy, ix, ic = here()
    z = lax.rem(iz + k, nz)
    device = (z, ic, ix, iy)

    def remote():
        for i, (source, target) in enumerate(pairs):
            send(source, target, out_sem.at[i, z], in_sem.at[i, iz], device)

    if k:
        remote()
        return
    pl.when(iy != ic)(remote)

    @pl.when(iy == ic)
    def _():
        for i, (source, target) in enumerate(pairs):
            copy = pltpu.make_async_copy(source, target, local_sem.at[i])
            copy.start()
            copy.wait()


def from_head(nz, k, targets, out_sem, in_sem):
    iz, iy, ix, ic = here()
    z = lax.rem(iz + k, nz)

    def wait():
        for i, target in enumerate(targets):
            arrived(target, out_sem.at[i, z], in_sem.at[i, z], (z, ic, ix, iy))

    if k:
        wait()
    else:
        pl.when(iy != ic)(wait)


def sent_head(nz, k, sources, out_sem, in_sem):
    iz, iy, ix, ic = here()
    z = lax.rem(iz + k, nz)

    def wait():
        for i, source in enumerate(sources):
            pltpu.make_async_remote_copy(
                src_ref=source,
                dst_ref=source,
                send_sem=out_sem.at[i, z],
                recv_sem=in_sem.at[i, z],
                device_id=(z, ic, ix, iy),
                device_id_type=pl.DeviceIdType.MESH,
            ).wait_send()

    if k:
        wait()
    else:
        pl.when(iy != ic)(wait)


def lanes(index, size):
    return pl.ds(pl.multiple_of(index * size, size), size)


def front_kernel(
    nz,
    half,
    residual,
    info,
    bias,
    joined_in,
    dense_in,
    down_in,
    up_in,
    vocab_in,
    natural,
    info_out,
    bias_out,
    joined_out,
    out_all,
    up_all,
    vocab_out,
    vocab_here,
    vs,
    fs,
    fr,
    js,
    jr,
    jl,
    cs,
    cr,
    ms,
    mr,
    zs,
    zr,
    ps,
    ds,
    dr,
    dl,
    es,
    er,
    *refs,
):
    iz, iy, ix, ic = here()
    core = other_core()
    across = [(lax.rem(iz + k, nz), 1 - iy, ix, ic) for k in range(nz)]
    greet(neighbours(nz) + [core] + diagonal(nz) + across[1:])
    depth = joined_in.shape[0]
    cols = joined_out.shape[1]
    heads = dense_in.shape[0] // nz
    units = down_in.shape[0] // (2 * nz)
    dense_out = out_all.at[pl.ds(0, heads)]
    down_out, down_other = (out_all.at[pl.ds(heads + i * units, units)] for i in (0, 1))
    copies = []

    def rows_of(h, z, y, x, c):
        return natural.at[z, y, x, c, pl.ds(h * half, half)]

    def forward(h, source, z, y, x):
        send(source, rows_of(h, z, y, x, ic), fs.at[h, z, y, x], fr.at[h, z, y, x], core)

    class Rows(Gather):
        def block(self, h, z, y, x):
            return rows_of(h, z, y, x, ic)

    fetch = pltpu.make_async_copy(vocab_in, vocab_here, vs.at[0])
    fetch.start()
    gather = Rows(nz, half, natural, refs, forward)
    first = pl.multiple_of((ix * 2 + ic) * 2 * half, 2 * half)
    for h in (0, 1):
        gather.start(h, residual.at[pl.ds(first + h * half, half)])

    copies.append(send(bias, bias_out, ms.at[0], mr.at[0], core))
    info_out[iz, iy] = info[...]
    across_y = (iz, 1 - iy, ix, ic)
    for k in range(1, nz):
        far = (lax.rem(iz + k, nz), iy, ix, ic)
        copies.append(send(info, info_out.at[iz, iy], zs.at[k], zr.at[iz, iy], far))
    copies.append(send(info, info_out.at[iz, iy], ps.at[iz], zr.at[iz, iy], across_y))

    mine = iz * 2 + iy
    for k in list(range(1, nz)) + [0]:
        z = lax.rem(iz + k, nz)
        to_head(
            nz,
            k,
            [
                (joined_in.at[:, lanes(z, cols)], joined_out.at[lanes(mine, depth)]),
                (dense_in.at[lanes(z, heads)], dense_out.at[:, lanes(mine, depth)]),
            ],
            jl,
            js,
            jr,
        )

    for k in range(1, nz):
        z = lax.rem(iz + k, nz)
        arrived(info_out.at[z, iy], zs.at[k], zr.at[z, iy], across_y)
        copies.append(send(info_out.at[z, iy], info_out.at[z, iy], ps.at[z], zr.at[z, iy], across_y))

    gather.firsts((0, 1))

    def own_units(d):
        rows, own, other = lanes(d, depth), pl.ds(0, units), pl.ds(units, units)
        return [
            (up_all.at[rows, own], up_all.at[rows, other]),
            (down_out.at[:, rows], down_other.at[:, rows]),
        ]

    line = [(lax.rem(iz + k, nz), iy, ix, ic) for k in range(1, nz)]
    keep = []
    for i, source in enumerate((up_in.at[:, lanes(mine, units)], down_in.at[lanes(mine, units)])):
        copy = pltpu.make_async_copy(source, own_units(mine)[i][0], dl.at[i])
        copy.start()
        keep.append(copy)
    for i in (0, 1):
        for device in line + across:
            d = device[0] * 2 + device[1]
            source = up_in.at[:, lanes(d, units)] if i == 0 else down_in.at[lanes(d, units)]
            copies.append(send(source, own_units(mine)[i][0], ds.at[i, d], dr.at[i, mine], device))
    gather.seconds((0, 1))
    gather.thirds((0, 1))

    fetch.wait()

    def across_block(i, carry):
        at = lanes(i, depth)
        vocab_out[at] = vocab_here[:, at].T
        return carry

    lax.fori_loop(0, vocab_in.shape[1] // depth, across_block, 0)

    def head_parts(z, side):
        d = z * 2 + side
        return joined_out.at[lanes(d, depth)], dense_out.at[:, lanes(d, depth)]

    for k in [0] + list(range(1, nz)):
        z = lax.rem(iz + k, nz)
        parts = head_parts(z, ic)
        from_head(nz, k, parts, js, jr)
        for i, part in enumerate(parts):
            copies.append(send(part, part, cs.at[i, z], cr.at[i, z], core))
    for copy in keep:
        copy.wait()
    for i in (0, 1):
        for device in [None] + line + across:
            d = mine if device is None else device[0] * 2 + device[1]
            block, other = own_units(d)[i]
            if device is not None:
                arrived(block, ds.at[i, d], dr.at[i, d], device)
            copies.append(send(block, other, es.at[i, d], er.at[i, d], core))
        for d in range(2 * nz):
            arrived(own_units(d)[i][1], es.at[i, d], er.at[i, d], core)
    for k in range(nz):
        z = lax.rem(iz + k, nz)
        arrived(info_out.at[z, 1 - iy], ps.at[z], zr.at[z, 1 - iy], across_y)
    for z in range(nz):
        for y in (0, 1):
            for x in (0, 1):
                for h in (0, 1):
                    arrived(rows_of(h, z, y, x, 1 - ic), fs.at[h, z, y, x], fr.at[h, z, y, x], core)
                    left(rows_of(h, z, y, x, ic), fs.at[h, z, y, x], fr.at[h, z, y, x], core)
    for z in range(nz):
        for i, part in enumerate(head_parts(z, 1 - ic)):
            arrived(part, cs.at[i, z], cr.at[i, z], core)
    arrived(bias_out, ms.at[0], mr.at[0], core)
    gather.end((0, 1))
    for k in range(nz):
        z = lax.rem(iz + k, nz)
        sent_head(nz, k, [joined_in.at[:, lanes(z, cols)], dense_in.at[lanes(z, heads)]], js, jr)
    for copy in copies:
        copy.wait_send()


def front(nz, residual, info, bias, joined_in, dense_in, down_in, up_in, vocab_in):
    held, width = residual.shape
    half = held // 8
    depth, cols = joined_in.shape[0], joined_in.shape[1] // nz
    heads = dense_in.shape[0] // nz
    units = down_in.shape[0] // (2 * nz)
    dma = pltpu.SemaphoreType.DMA
    outs = pl.pallas_call(
        functools.partial(front_kernel, nz, half),
        out_shape=[
            jax.ShapeDtypeStruct((nz, 2, 2, 2, 2 * half, width), BF16),
            jax.ShapeDtypeStruct((nz, 2) + info.shape, F32),
            jax.ShapeDtypeStruct(bias.shape, F32),
            jax.ShapeDtypeStruct((2 * nz * depth, cols), BF16),
            jax.ShapeDtypeStruct((heads + 2 * units, 2 * nz * depth), BF16),
            jax.ShapeDtypeStruct((2 * nz * depth, 2 * units), BF16),
            jax.ShapeDtypeStruct(vocab_in.shape[::-1], BF16),
        ],
        in_specs=[anywhere(), vmem(), vmem(), anywhere(), anywhere(), anywhere(), anywhere(), anywhere()],
        out_specs=[anywhere(), vmem(), vmem(), anywhere(), anywhere(), anywhere(), vmem()],
        scratch_shapes=[
            pltpu.VMEM(vocab_in.shape, BF16),
            dma((1,)),
            dma((2, nz, 2, 2)),
            dma((2, nz, 2, 2)),
            dma((2, nz)),
            dma((2, nz)),
            dma((2,)),
            dma((2, nz)),
            dma((2, nz)),
            dma((1,)),
            dma((1,)),
            dma((nz,)),
            dma((nz, 2)),
            dma((nz,)),
            dma((2, 2 * nz)),
            dma((2, 2 * nz)),
            dma((2,)),
            dma((2, 2 * nz)),
            dma((2, 2 * nz)),
        ]
        + Gather.scratch(2, nz),
        cost_estimate=busy(45),
        compiler_params=comm(1, 62),
    )(residual, info, bias, joined_in, dense_in, down_in, up_in, vocab_in)
    natural = outs[0].reshape(8 * nz * 2 * half, width)
    return natural, outs[1].reshape((2 * nz,) + info.shape), outs[2], outs[3], outs[4], outs[5], outs[6]


def end_kernel(
    nz,
    half,
    part,
    mine_rows,
    other_rows,
    rows,
    vectors,
    keep,
    give,
    joined_in,
    dense_in,
    rows_out,
    vectors_out,
    bias_out,
    joined_out,
    dense_out,
    merged,
    came,
    rows_in,
    vector_in,
    vector_sum,
    give_in,
    joined_came,
    joined_sum,
    dense_came,
    dense_sum,
    ms,
    mr,
    vs,
    vr,
    bs,
    br,
    bp,
    js,
    jr,
    jl,
    cs,
    cr,
    os,
    orr,
    *refs,
):
    iz, iy, ix, ic = here()
    core = other_core()
    across_x, across_y = (iz, iy, 1 - ix, ic), (iz, 1 - iy, ix, ic)
    greet(neighbours(nz) + [core] + diagonal(nz))
    reduce = Reduce(nz, half, merged, refs, END_BY_X)
    copies = []
    depth = joined_in.shape[0] // (2 * nz)
    cols = joined_in.shape[1]
    heads = dense_in.shape[0]
    groups = [(1 - iy, 1 - ix), (iy, 1 - ix), (1 - iy, ix), (iy, ix)]

    for y, x in groups:
        for k in list(range(1, nz)) + [0]:
            z = lax.rem(iz + k, nz)
            copies.append(
                send(part.at[z, y, x, 1 - ic], came.at[z, y, x], ms.at[z, y, x], mr.at[z, y, x], core)
            )
    copies.append(send(vectors, vector_in.at[0], vs.at[0], vr.at[0], core))
    copies.append(send(give, give_in, bs.at[0], br.at[nz, 0], core))
    copies.append(send(other_rows, rows_in, os.at[0], orr.at[0], core))
    for k in range(nz):
        z = lax.rem(iz + k, nz)
        theirs = z * 2 + 1 - ic
        copies.append(
            send(joined_in.at[lanes(theirs, depth)], joined_came.at[z], cs.at[0, z], cr.at[0, z], core)
        )
        copies.append(
            send(dense_in.at[:, lanes(theirs, depth)], dense_came.at[z], cs.at[1, z], cr.at[1, z], core)
        )

    def merge_group(y, x):
        for k in list(range(1, nz)) + [0]:
            z = lax.rem(iz + k, nz)
            arrived(came.at[z, y, x], ms.at[z, y, x], mr.at[z, y, x], core)
            merged[z, y, x] = (part[z, y, x, ic].astype(F32) + came[z, y, x].astype(F32)).astype(BF16)

    merge_group(*groups[0])
    reduce.start(0, True)
    merge_group(*groups[1])
    reduce.start(0, False)
    merge_group(*groups[2])
    reduce.start(1, True)
    reduce.start(1, False)
    merge_group(*groups[3])

    arrived(vector_in.at[0], vs.at[0], vr.at[0], core)
    vector_sum[0] = vectors[...] + vector_in[0]
    copies.append(send(vector_sum.at[0], vector_in.at[1], vs.at[1], vr.at[1], across_x))
    arrived(give_in, bs.at[0], br.at[nz, 0], core)
    bias_out[iz, iy] = keep[...] + give_in[...]
    for k in range(1, nz):
        far = (lax.rem(iz + k, nz), iy, ix, ic)
        copies.append(send(bias_out.at[iz, iy], bias_out.at[iz, iy], bs.at[k], br.at[iz, iy], far))
    copies.append(send(bias_out.at[iz, iy], bias_out.at[iz, iy], bp.at[iz], br.at[iz, iy], across_y))

    for k in list(range(1, nz)) + [0]:
        z = lax.rem(iz + k, nz)
        ours = z * 2 + ic
        arrived(joined_came.at[z], cs.at[0, z], cr.at[0, z], core)
        joined_sum[z] = (joined_in[lanes(ours, depth)].astype(F32) + joined_came[z].astype(F32)).astype(BF16)
        arrived(dense_came.at[z], cs.at[1, z], cr.at[1, z], core)
        dense_sum[z] = (dense_in[:, lanes(ours, depth)].astype(F32) + dense_came[z].astype(F32)).astype(BF16)
        to_head(
            nz,
            k,
            [
                (joined_sum.at[z], joined_out.at[:, lanes(iz, cols)]),
                (dense_sum.at[z], dense_out.at[lanes(iz, heads)]),
            ],
            jl,
            js,
            jr,
        )

    for h in (0, 1):
        reduce.second(h)
    arrived(vector_in.at[1], vs.at[1], vr.at[1], across_x)
    vector_sum[1] = vector_sum[0] + vector_in[1]
    copies.append(send(vector_sum.at[1], vector_in.at[2], vs.at[2], vr.at[2], across_y))
    for k in range(1, nz):
        z = lax.rem(iz + k, nz)
        arrived(bias_out.at[z, iy], bs.at[k], br.at[z, iy], across_y)
        copies.append(send(bias_out.at[z, iy], bias_out.at[z, iy], bp.at[z], br.at[z, iy], across_y))
    kept = [reduce.third(h) for h in (0, 1)]
    arrived(vector_in.at[2], vs.at[2], vr.at[2], across_y)
    vector_sum[2] = vector_sum[1] + vector_in[2]
    for k in range(1, nz):
        far = (lax.rem(iz + k, nz), iy, ix, ic)
        copies.append(send(vector_sum.at[2], vector_in.at[3 + iz], vs.at[2 + k], vr.at[3 + iz], far))
    vector_in[3 + iz] = vector_sum[2]
    arrived(rows_in, os.at[0], orr.at[0], core)
    for h in (0, 1):
        at = pl.ds(h * half, half)
        hat, inverse = normed(rows[at].astype(F32))
        back = norm_back(reduce.finish(h, kept[h]), hat, inverse)
        block = rows_out.at[ix, ic, at]
        rows_out[ix, ic, at] = (
            mine_rows[at].astype(F32) + rows_in[at].astype(F32) + back
        ).astype(BF16)
        copies.append(send(block, block, os.at[1 + h], orr.at[1 + h], across_x))
        copies.append(send(block, block, os.at[3 + h], orr.at[3 + h], core))
    for h in (0, 1):
        block = rows_out.at[1 - ix, ic, pl.ds(h * half, half)]
        arrived(block, os.at[1 + h], orr.at[1 + h], across_x)
        copies.append(send(block, block, os.at[5 + h], orr.at[5 + h], core))
    for k in range(1, nz):
        z = lax.rem(iz + k, nz)
        arrived(vector_in.at[3 + z], vs.at[2 + k], vr.at[3 + z], (z, iy, ix, ic))
    total = vector_in[3]
    for z in range(1, nz):
        total = total + vector_in[3 + z]
    vectors_out[...] = total
    for k in range(nz):
        z = lax.rem(iz + k, nz)
        arrived(bias_out.at[z, 1 - iy], bp.at[z], br.at[z, 1 - iy], across_y)
        from_head(
            nz, k, [joined_out.at[:, lanes(z, cols)], dense_out.at[lanes(z, heads)]], js, jr
        )
        sent_head(nz, k, [joined_sum.at[z], dense_sum.at[z]], js, jr)
    for h in (0, 1):
        at = pl.ds(h * half, half)
        arrived(rows_out.at[ix, 1 - ic, at], os.at[3 + h], orr.at[3 + h], core)
        arrived(rows_out.at[1 - ix, 1 - ic, at], os.at[5 + h], orr.at[5 + h], core)
    reduce.end((0, 1))
    for copy in copies:
        copy.wait_send()


def end(nz, part, mine_rows, other_rows, rows, vectors, keep, give, joined_in, dense_in):
    share, width = rows.shape
    half = share // 2
    depth, cols, heads = joined_in.shape[0] // (2 * nz), joined_in.shape[1], dense_in.shape[0]
    dma = pltpu.SemaphoreType.DMA
    return pl.pallas_call(
        functools.partial(end_kernel, nz, half),
        out_shape=[
            jax.ShapeDtypeStruct((2, 2, share, width), BF16),
            jax.ShapeDtypeStruct(vectors.shape, F32),
            jax.ShapeDtypeStruct((nz, 2) + keep.shape, F32),
            jax.ShapeDtypeStruct((depth, nz * cols), BF16),
            jax.ShapeDtypeStruct((nz * heads, depth), BF16),
        ],
        in_specs=[vmem()] * 9,
        out_specs=[vmem(), vmem(), vmem(), vmem(), vmem()],
        scratch_shapes=[
            pltpu.VMEM((nz, 2, 2, share, width), BF16),
            pltpu.VMEM((nz, 2, 2, share, width), BF16),
            pltpu.VMEM((share, width), BF16),
            pltpu.VMEM((3 + nz,) + vectors.shape, F32),
            pltpu.VMEM((3,) + vectors.shape, F32),
            pltpu.VMEM(keep.shape, F32),
            pltpu.VMEM((nz, depth, cols), BF16),
            pltpu.VMEM((nz, depth, cols), BF16),
            pltpu.VMEM((nz, heads, depth), BF16),
            pltpu.VMEM((nz, heads, depth), BF16),
            dma((nz, 2, 2)),
            dma((nz, 2, 2)),
            dma((2 + nz,)),
            dma((3 + nz,)),
            dma((nz,)),
            dma((nz + 1, 2)),
            dma((nz,)),
            dma((2, nz)),
            dma((2, nz)),
            dma((2,)),
            dma((2, nz)),
            dma((2, nz)),
            dma((7,)),
            dma((7,)),
        ]
        + Reduce.scratch(2, nz, half, width),
        cost_estimate=busy(70),
        compiler_params=comm(5),
    )(part, mine_rows, other_rows, rows, vectors, keep, give, joined_in, dense_in)


def turned(values, cosine, low, high):
    half_rot = ROT // 2
    return (
        values * cosine
        + pltpu.roll(values, values.shape[1] - half_rot, 1) * low
        + pltpu.roll(values, half_rot, 1) * high
    )


def block_rows(order, ref, piece, first, count):
    return jnp.concatenate(
        [ref[pl.ds(pl.multiple_of(order[first + i] * piece, piece), piece), :] for i in range(count)], axis=0
    )


def attention_kernel(piece, order, fused, tables, allowed, qkv, probs_out, mixed):
    groups, held = allowed.shape[0], allowed.shape[1]
    per = held // piece
    for g in range(groups):
        at = pl.ds(g * held, held)
        rows = block_rows(order, fused, piece, g * per, per)
        turn_by = [tables[i, at] for i in range(3)]
        query = turned(rows[:, :HD], *turn_by).astype(BF16)
        keys = turned(rows[:, HD : 2 * HD], *turn_by).astype(BF16)
        values = rows[:, 2 * HD :].astype(BF16)
        qkv[at, :HD] = query
        qkv[at, HD : 2 * HD] = keys
        qkv[at, 2 * HD :] = values
        scores = jnp.where(allowed[g] > 0.5, dot(query, keys, (1, 1)) / math.sqrt(HD), masked_score)
        weights = jnp.exp(scores - jnp.max(scores, axis=-1, keepdims=True))
        probs = weights / jnp.sum(weights, axis=-1, keepdims=True)
        probs_out[g] = probs
        mixed[at] = dot(probs.astype(BF16), values, (1, 0)).astype(BF16)


def attention(order, fused, tables, allowed, piece):
    total = fused.shape[0]
    return pl.pallas_call(
        functools.partial(attention_kernel, piece),
        out_shape=[
            jax.ShapeDtypeStruct((total, 3 * HD), BF16),
            jax.ShapeDtypeStruct(allowed.shape, F32),
            jax.ShapeDtypeStruct((total, HD), BF16),
        ],
        in_specs=[pl.BlockSpec(memory_space=pltpu.SMEM)] + [vmem()] * 3,
        out_specs=[vmem()] * 3,
        compiler_params=pltpu.CompilerParams(vmem_limit_bytes=32 << 20),
    )(order, fused, tables, allowed)


def place_kernel(piece, order, mixed, active, out):
    per = 2
    out[:, :HD] = mixed[...]
    for g in range(mixed.shape[0] // (per * piece)):
        out[pl.ds(g * per * piece, per * piece), HD:] = block_rows(order, active, piece, g * per, per)


def place(order, mixed, active, piece):
    total = mixed.shape[0]
    return pl.pallas_call(
        functools.partial(place_kernel, piece),
        out_shape=jax.ShapeDtypeStruct((total, HD + active.shape[1]), BF16),
        in_specs=[pl.BlockSpec(memory_space=pltpu.SMEM)] + [vmem()] * 2,
        out_specs=vmem(),
        compiler_params=pltpu.CompilerParams(vmem_limit_bytes=32 << 20),
    )(order, mixed, active)


def attention_back_kernel(
    piece, order, dbranch, wout, slope, qkv, probs_in, tables, dfused, dhidden, sums, douts
):
    tile = 4 * piece

    def back(i, carry):
        at = pl.ds(pl.multiple_of(i * tile, tile), tile)
        douts[at] = dot(dbranch[at], wout[...], (1, 1))
        return carry

    lax.fori_loop(0, dbranch.shape[0] // tile, back, 0)
    groups, held = probs_in.shape[0], probs_in.shape[1]
    per = held // piece
    joined_sum = jnp.zeros((1, 3 * HD), F32)
    hidden_sum = jnp.zeros((1, slope.shape[1]), F32)
    for g in range(groups):
        at = pl.ds(g * held, held)
        query, keys, values = qkv[at, :HD], qkv[at, HD : 2 * HD], qkv[at, 2 * HD :]
        dmixed = douts[at, :HD].astype(BF16)
        probs = probs_in[g]
        dvalues = dot(probs.astype(BF16), dmixed, (0, 0))
        dprobs = dot(dmixed, values, (1, 1))
        dscores = (probs * (dprobs - jnp.sum(probs * dprobs, axis=-1, keepdims=True))).astype(BF16)
        turn_by = [tables[0, at], -tables[1, at], -tables[2, at]]
        dquery = turned(dot(dscores, keys, (1, 0)) / math.sqrt(HD), *turn_by)
        dkeys = turned(dot(dscores, query, (0, 0)) / math.sqrt(HD), *turn_by)
        whole = jnp.concatenate([dquery, dkeys, dvalues], axis=1).astype(BF16)
        joined_sum = joined_sum + jnp.sum(whole.astype(F32), axis=0, keepdims=True)
        for i in range(per):
            to = pl.ds(pl.multiple_of(order[g * per + i] * piece, piece), piece)
            dfused[to, :] = whole[i * piece : (i + 1) * piece]
            grown = (douts[pl.ds(g * held + i * piece, piece), HD:] * slope[to, :]).astype(BF16)
            dhidden[to, :] = grown
            hidden_sum = hidden_sum + jnp.sum(grown.astype(F32), axis=0, keepdims=True)
    sums[:, : 3 * HD] = joined_sum
    sums[:, 3 * HD :] = hidden_sum


def attention_back(order, dbranch, wout, slope, qkv, probs, tables, piece):
    total, units = slope.shape
    return pl.pallas_call(
        functools.partial(attention_back_kernel, piece),
        out_shape=[
            jax.ShapeDtypeStruct((total, 3 * HD), BF16),
            jax.ShapeDtypeStruct((total, units), BF16),
            jax.ShapeDtypeStruct((1, 3 * HD + units), F32),
        ],
        in_specs=[pl.BlockSpec(memory_space=pltpu.SMEM)] + [vmem()] * 6,
        out_specs=[vmem()] * 3,
        scratch_shapes=[pltpu.VMEM((total, wout.shape[0]), F32)],
        cost_estimate=pl.CostEstimate(flops=0, bytes_accessed=1000, transcendentals=0),
        compiler_params=pltpu.CompilerParams(vmem_limit_bytes=30 << 20),
    )(order, dbranch, wout, slope, qkv, probs, tables)


def fast_shards(
    residual,
    lengths,
    pair_order,
    token_ids,
    desirable,
    ref_match,
    ref_pair,
    attn_gain,
    attn_shift,
    mlp_gain,
    mlp_shift,
    w_joined,
    b_joined,
    w_dense,
    b_dense,
    w_up,
    b_up,
    w_down,
    b_down,
    final_gain,
    final_shift,
    w_vocab,
):
    nz, ny, nx = lax.axis_size("z"), lax.axis_size("y"), lax.axis_size("x")
    n = nz * ny
    chips = n * nx
    iz, iy, ix, ic = (lax.axis_index(a) for a in ALL)
    dp = iz * ny + iy
    held, width = residual.shape
    total = n * held
    blocks = 2 * n
    piece = held // 2
    seqs = lengths.shape[1]
    depth = width // n
    vcols = w_vocab.shape[1] // n
    ffs = w_up.shape[1] // n
    hcols = 3 * HD
    mine = ix * 2 + ic

    info = jnp.stack(
        [
            token_ids.astype(F32),
            ref_match,
            ref_pair,
            jnp.concatenate(
                [lengths[0].astype(F32), desirable.astype(F32), jnp.zeros((held - 2 * seqs,), F32)]
            ),
        ]
    )
    bias_own = jnp.concatenate([b_joined, b_up]).astype(F32)
    natural, info, bias_other, wj, wout, wup, vocab_across = front(
        nz, residual, info, bias_own.reshape(-1, HD), w_joined, w_dense, w_down, w_up, w_vocab
    )
    bias_other = bias_other.reshape(-1)

    send_vocab = vocab_across.reshape(n, vcols, depth)
    vocab_got = exchange(send_vocab)
    bias_first = jnp.where(ic == 0, bias_own, bias_other)
    bias_second = jnp.where(ic == 0, bias_other, bias_own)
    bj_all = jnp.where(iy == 0, bias_first, bias_second)[: nz * hcols].reshape(nz, hcols)
    bj = lax.dynamic_index_in_dim(bj_all, iz, 0, keepdims=False)
    bu_all = jnp.stack([bias_own[nz * hcols :], bias_other[nz * hcols :]]).reshape(2, n, ffs)
    bu = lax.dynamic_index_in_dim(bu_all, dp, 1, keepdims=False).reshape(2 * ffs)

    ids = info[:, 0].astype(jnp.int32)
    refs = jnp.stack([info[:, 1], info[:, 2]])
    lens = info[:, 3, :seqs].astype(jnp.int32)
    wanted = info[:, 3, seqs : 2 * seqs]
    slots = jnp.arange(blocks, dtype=jnp.int32)
    anchor = jnp.sum(
        jnp.where(pair_order[None, :] == slots[:, None], slots[None, :], 0), axis=1
    )
    order = jnp.where(ic == 0, slots, anchor)
    back = jnp.where(ic == 0, slots, pair_order)
    anchor_hot = (anchor[:, None] == slots[None, :])[:, :, None]
    pair_ids = jnp.sum(jnp.where(anchor_hot, ids.reshape(1, blocks, piece), 0), axis=1).reshape(n, held)
    all_ids = jnp.stack([ids, pair_ids])

    ends = jnp.stack([jnp.sum(lens[:, : s + 1], axis=1) for s in range(seqs)], axis=1)
    starts = ends - lens
    places = jnp.arange(held, dtype=jnp.int32)
    segment = jnp.sum((places[None, :, None] >= ends[:, None, :]).astype(jnp.int32), axis=2)
    hot = (segment[:, :, None] == jnp.arange(seqs, dtype=jnp.int32)).astype(F32)
    position = places[None, :] - jnp.sum(hot * starts[:, None, :].astype(F32), axis=2).astype(jnp.int32)
    allowed = (segment[:, :, None] == segment[:, None, :]) & (places[None, :, None] >= places[None, None, :])
    scored = jnp.concatenate(
        [segment[:, 1:] == segment[:, :-1], jnp.zeros((n, 1), jnp.bool_)], axis=1
    ).astype(F32)
    targets = jnp.concatenate([all_ids[:, :, 1:], jnp.zeros((2, n, 1), jnp.int32)], axis=2)

    hat, inverse = normed(natural.astype(F32))
    ga, sa, gm, sm, gf, sf = (
        v.astype(F32) for v in (attn_gain, attn_shift, mlp_gain, mlp_shift, final_gain, final_shift)
    )
    attn_low = (hat * ga + sa).astype(BF16)
    mlp_low = (hat * gm + sm).astype(BF16)
    lane = jnp.arange(HD, dtype=jnp.int32)
    frequency = jnp.exp((lane % (ROT // 2)).astype(F32) * (-2.0 * math.log(10000.0) / ROT))
    angles = position.reshape(total)[:, None].astype(F32) * frequency[None, :]
    cosine = jnp.where(lane < ROT, jnp.cos(angles), 1.0)
    sine = jnp.sin(angles)
    tables = jnp.stack(
        [
            cosine,
            jnp.where(lane < ROT // 2, -sine, 0.0),
            jnp.where((lane >= ROT // 2) & (lane < ROT), sine, 0.0),
        ]
    )
    fused = dot(attn_low, wj, (1, 0)) + bj
    qkv, probs, mixed = attention(order, fused, tables, allowed.astype(F32), piece)
    hidden = dot(mlp_low, wup, (1, 0)) + bu
    bell = 0.5 * (1.0 + lax.erf(hidden * math.sqrt(0.5)))
    active = (hidden * bell).astype(BF16)
    gelu_slope = bell + hidden * jnp.exp(-0.5 * hidden * hidden) * (1.0 / math.sqrt(2.0 * math.pi))
    outs_low = place(order, mixed, active, piece)
    branch_part = dot(outs_low, wout, (1, 0)).astype(BF16)
    share = total // chips
    chip = dp * nx + ix
    first_row = jnp.sum(jnp.where(slots == chip * share // piece, order, 0)) * piece + chip * share % piece
    rows_here = lax.dynamic_slice_in_dim(natural, first_row, share, 0)
    bias_out = (b_dense.astype(F32) + b_down.astype(F32))[None]
    final, resid = reduce_norm_gather(nz, branch_part, rows_here, bias_out, gf[None], sf[None])

    vocab_got, final = lax.optimization_barrier((vocab_got, final))
    vocab_own = vocab_got.transpose(1, 0, 2).reshape(vcols, width)
    vocab_other = swap(vocab_got).transpose(1, 0, 2).reshape(vcols, width)
    my_targets = jnp.where(ic == 0, targets[0], targets[1]).reshape(total)
    logits = [dot(final, w, (1, 1)) for w in (vocab_own, vocab_other)]
    hits = [
        lax.broadcasted_iota(jnp.int32, (total, vcols), 1)
        == (my_targets - ((ix * 2 + core) * n + dp) * vcols)[:, None]
        for core in (ic, 1 - ic)
    ]
    tops = [jnp.max(part, axis=1) for part in logits]
    top = jnp.maximum(tops[0], tops[1])
    sums = sum(jnp.sum(jnp.exp(part - top[:, None]), axis=1) for part in logits)
    picks = sum(jnp.sum(jnp.where(h, part, 0.0), axis=1) for h, part in zip(hits, logits))
    stats = jnp.stack([top, sums, picks]).reshape(3, n, held)
    coef, my_lse, scalars = objective(
        nz, n * seqs, stats, hot.transpose(2, 0, 1), scored, refs, lens.astype(F32), wanted
    )
    coef, my_lse = coef.reshape(total), my_lse.reshape(total)
    kto_loss, kl_estimate = scalars[0, 0, 0], scalars[1, 0, 0]

    dlogits = [
        (coef[:, None] * (jnp.where(h, 1.0, 0.0) - jnp.exp(part - my_lse[:, None]))).astype(BF16)
        for h, part in zip(hits, logits)
    ]
    gv_other = dot(dlogits[1], final, (0, 0)).astype(BF16)
    dfinal_other = dot(dlogits[1], vocab_other, (1, 0)).astype(F32)
    gv_own = dot(dlogits[0], final, (0, 0))
    gv = (gv_own + swap(gv_other).astype(F32)).astype(BF16)
    gv, dlogits_own = lax.optimization_barrier((gv, dlogits[0]))
    dfinal_part = (dot(dlogits_own, vocab_own, (1, 0)) + dfinal_other).astype(BF16)
    gv = gv.reshape(vcols, n, depth).transpose(1, 0, 2)
    early_cols = vcols * 336 // 800
    grad_early = exchange(gv[:, :early_cols])
    dbranch, final_vectors = reduce_back_gather(nz, dfinal_part, resid, gf[None])
    gv_late, dbranch, grad_early = lax.optimization_barrier((gv[:, early_cols:], dbranch, grad_early))
    grad_late = exchange(gv_late)
    grad_vocab = jnp.concatenate([grad_early, grad_late], axis=1).reshape(n * vcols, depth).T
    grad_vocab = with_layout_constraint(lax.optimization_barrier(grad_vocab).astype(F32), Layout((0, 1)))

    dfused, dhidden, bias_sums = attention_back(
        order, dbranch, wout, gelu_slope, qkv, probs, tables, piece
    )
    dhidden, outs_low = lax.optimization_barrier((dhidden, outs_low))
    gout = dot(outs_low, dbranch, (0, 0))
    gu = dot(mlp_low, dhidden, (0, 0))

    def to_send(up, down):
        return jnp.concatenate(
            [up.reshape(n, depth, ffs), down.reshape(ffs, n, depth).transpose(1, 0, 2)], axis=1
        )

    give_grads = to_send(gu[:, ffs:].astype(BF16), gout[HD + ffs :].astype(BF16))
    layer_grads = to_send(gu[:, :ffs], gout[HD : HD + ffs]) + swap(give_grads).astype(F32)
    layer_grads, dfused, dhidden = lax.optimization_barrier((layer_grads.astype(BF16), dfused, dhidden))
    layer_grads = exchange(layer_grads)
    gj = dot(attn_low, dfused, (0, 0)).astype(BF16)
    dattn = dot(dfused, wj, (1, 1))
    dmlp = dot(dhidden, wup, (1, 1))
    g_attn_gain = jnp.sum(dattn * hat, axis=0)
    g_attn_shift = jnp.sum(dattn, axis=0)
    g_mlp_gain = jnp.sum(dmlp * hat, axis=0)
    g_mlp_shift = jnp.sum(dmlp, axis=0)
    t_part = (dattn * ga + dmlp * gm).astype(BF16)
    grad_up = layer_grads[:, :depth].transpose(1, 0, 2).reshape(depth, n * ffs).astype(F32)
    grad_down = layer_grads[:, depth:].reshape(n * ffs, depth).astype(F32)

    share2 = total // (2 * chips)

    def natural_rows(core):
        first = dp * held + (ix * 2 + core) * share2
        place = jnp.sum(jnp.where(slots == first // piece, back, 0)) * piece + first % piece
        return lax.dynamic_slice_in_dim(dbranch, place, share2, 0)

    gbj, gbu = bias_sums[0, :hcols], bias_sums[0, hcols:]
    spare = jnp.zeros((8 * HD - hcols - ffs,), F32)
    keep = jnp.concatenate([gbj, gbu[:ffs], spare]).reshape(8, HD)
    give = jnp.concatenate([gbj, gbu[ffs:], spare]).reshape(8, HD)
    vectors = jnp.concatenate(
        [
            jnp.stack([g_attn_gain, g_attn_shift, g_mlp_gain, g_mlp_shift]),
            final_vectors,
            jnp.zeros((1, width), F32),
        ]
    )
    grad_vocab, t_part = lax.optimization_barrier((grad_vocab, t_part))
    rows_out, vectors, biases, grad_joined, grad_dense = end(
        nz,
        t_part.reshape(nz, 2, 2, 2, share2, width),
        natural_rows(ic),
        natural_rows(1 - ic),
        lax.dynamic_slice_in_dim(residual, mine * share2, share2, 0),
        vectors,
        keep,
        give,
        gj,
        gout[:HD].astype(BF16),
    )
    grad_input = rows_out.reshape(held, width).astype(F32)
    grad_joined, grad_dense = grad_joined.astype(F32), grad_dense.astype(F32)
    g_attn_gain, g_attn_shift, g_mlp_gain, g_mlp_shift, g_final_gain, g_final_shift, g_out = vectors[:7]
    biases = biases.reshape(nz, 2, 8 * HD)
    gb_joined = jnp.where(ic == 0, biases[:, 0, :hcols], biases[:, 1, :hcols]).reshape(nz * hcols)
    gb_up = biases[:, :, hcols : hcols + ffs].reshape(n * ffs)
    return (
        kto_loss,
        kl_estimate,
        grad_input,
        g_attn_gain,
        g_attn_shift,
        g_mlp_gain,
        g_mlp_shift,
        grad_joined,
        gb_joined,
        grad_dense,
        g_out,
        grad_up,
        gb_up,
        grad_down,
        g_out,
        g_final_gain,
        g_final_shift,
        grad_vocab,
    )


def placed(dp, mp):
    ins = (
        P(dp, None),
        P(dp, None),
        P(),
        P(dp),
        P(dp),
        P(dp),
        P(dp),
        P(),
        P(),
        P(),
        P(),
        P(dp, mp),
        P(mp),
        P(mp, dp),
        P(),
        P(dp, mp),
        P(mp),
        P(mp, dp),
        P(),
        P(),
        P(),
        P(dp, mp),
    )
    outs = (
        P(),
        P(),
        P(dp, None),
        P(),
        P(),
        P(),
        P(),
        P(dp, mp),
        P(mp),
        P(mp, dp),
        P(),
        P(dp, mp),
        P(mp),
        P(mp, dp),
        P(),
        P(),
        P(),
        P(dp, mp),
    )
    return ins, outs


def solution(mesh):
    n_dp, n_mp = mesh.shape["dp"], mesh.shape["mp"]
    if n_dp == 8 and n_mp == 4:
        fine = jax.sharding.Mesh(mesh.devices.reshape(n_dp // 2, 2, n_mp // 2, 2), ALL)
        ins, outs = placed(DP, ("x", "c"))
        return jax.shard_map(fast_shards, mesh=fine, in_specs=ins, out_specs=outs, check_vma=False)
    ins, outs = placed("dp", "mp")
    return jax.shard_map(shards, mesh=mesh, in_specs=ins, out_specs=outs, check_vma=False)
```
